128 devices in a mesh: lvl: 4 (over y), gx: 32 (over z, x, core).
Axes of the slice: x: 4, y: 4, z: 4, core: 2. Of those that a mesh axis runs over, the one named last changes fastest.
Arguments:
- populations: float32 [4, 128, 32, 27, 128], P('lvl', 'gx'), as said below
- solid_mask: int32 [4, 128, 32, 128], P('lvl', 'gx'), may hold values 0 or 1
- relax_rates: float32 [4], P('lvl'), may hold values from 0.8 to 1.8
- down_send: int32 [4, 32, 32, 2], P('lvl', 'gx'), may hold values from -1 to 127, as said below
- down_recv: int32 [4, 32, 32, 2], P('lvl', 'gx'), may hold values from -1 to 127, as said below
- up_send: int32 [4, 32, 32, 2], P('lvl', 'gx'), may hold values from -1 to 127, as said below
- up_recv: int32 [4, 32, 32, 2], P('lvl', 'gx'), may hold values from -1 to 127, as said below
Outputs:
- final_populations: float32 [4, 128, 32, 27, 128], P('lvl', 'gx')
The draws below stay inside these ranges and needn't reach their ends.
Inputs may be any that keep to these rules, and one draw needn't show every extreme that they name: down_send[l, p, q, k] is a row of slab p of level l, or -1; it is a row exactly where down_recv[l + 1, q, p, k] is, so level 3 sends nothing down. The rows that are not -1 come first among the 2 slots; in every receiving level and draw some slab receives 2 rows from every slab, and every slab receives 2 rows from the slab at its own position. down_recv[l, q, p, k] is a row of slab q of level l, or -1 (always -1 for level 0); the rows of one slab named in down_recv and up_recv are all different. up_send[l, p, q, k] is a row of slab p of level l, or -1; it is a row exactly where up_recv[l - 1, q, p, k] is, so level 0 sends nothing up. The rows come first among the 2 slots; some slab of each receiving level gets 2 rows from every slab, and every slab gets 2 rows from the slab at its own position. up_recv[l, q, p, k] is a row of slab q of level l, or -1 (always -1 for level 3). Normalized populations of a flow near equilibrium: at every node the weighted sum over the 27 velocities lies between 0.5 and 1.5.
All inputs are finite; a program needn't handle non-finite values. No bound on the sum of `solid_mask` on one device may be relied on, other than what follows from the above.
Results may differ from the reference program's by a relative error of at most 0.0001.
Values sent between devices are 32-bit elements; how exact they have to be, the bound alone decides.
No kernel may reach another device: no remote copies, remote signals or barrier semaphores. Data moves between devices by JAX's collectives and lax.ppermute only.
A program may use at most 192 MiB of HBM per device.

```python
import jax
import jax.numpy as jnp
import numpy as np
from jax import lax

CX = 4
NY = 32
NZ = 128
Q = 27
CAP = 2
LEVELS = 4
SUB = 8
PEERS = 32
NX = 128


def interface_tables(key):
    slab_rows = CX * NY
    keys = jax.random.split(key, 7)
    level_ids = jnp.arange(LEVELS)
    source_ids = jnp.arange(PEERS)[None, :, None]
    target_ids = jnp.arange(PEERS)[None, None, :]

    def counts(count_key, pick_key, allowed):
        base = jax.random.randint(count_key, (LEVELS, PEERS, PEERS), 0, CAP + 1)
        chosen = jax.random.randint(pick_key, (LEVELS, 1, 1), 0, PEERS)
        filled = (source_ids == target_ids) | (target_ids == chosen)
        return jnp.where(allowed[:, None, None], jnp.where(filled, CAP, base), 0).astype(jnp.int32)
    into_down = counts(keys[0], keys[1], level_ids >= 1)
    into_up = counts(keys[2], keys[3], level_ids <= LEVELS - 2)
    order_keys = jax.random.split(keys[4], LEVELS * PEERS)
    orders = jax.vmap(lambda single: jax.random.permutation(single, slab_rows))(order_keys).reshape(LEVELS, PEERS, slab_rows)
    slots = jnp.arange(CAP)[None, None, None, :]
    span = PEERS * CAP
    down_recv = jnp.where(slots < jnp.transpose(into_down, (0, 2, 1))[..., None], orders[:, :, 0:span].reshape(LEVELS, PEERS, PEERS, CAP), -1)
    up_recv = jnp.where(slots < jnp.transpose(into_up, (0, 2, 1))[..., None], orders[:, :, span:2 * span].reshape(LEVELS, PEERS, PEERS, CAP), -1)
    from_down = jnp.concatenate([into_down[1:], jnp.zeros_like(into_down[:1])], axis=0)
    from_up = jnp.concatenate([jnp.zeros_like(into_up[:1]), into_up[:-1]], axis=0)
    down_rows = jax.random.randint(keys[5], (LEVELS, PEERS, PEERS, CAP), 0, slab_rows)
    up_rows = jax.random.randint(keys[6], (LEVELS, PEERS, PEERS, CAP), 0, slab_rows)
    down_send = jnp.where(slots < from_down[..., None], down_rows, -1)
    up_send = jnp.where(slots < from_up[..., None], up_rows, -1)
    return (down_send.astype(jnp.int32), down_recv.astype(jnp.int32), up_send.astype(jnp.int32), up_recv.astype(jnp.int32))


def draw_down_send(key, part):
    return interface_tables(key)[0]


def draw_down_recv(key, part):
    return interface_tables(key)[1]


def draw_up_send(key, part):
    return interface_tables(key)[2]


def draw_up_recv(key, part):
    return interface_tables(key)[3]


def draw_populations(key, part):
    key = jax.random.fold_in(key, 11)
    keys = jax.random.split(key, 5)
    node_shape = (LEVELS, NX, NY, 1, NZ)
    offsets = np.array([[i // 9 - 1, i // 3 % 3 - 1, i % 3 - 1] for i in range(27)])
    first = jnp.asarray(offsets[:, 0], dtype=jnp.float32).reshape(1, 1, 1, Q, 1)
    second = jnp.asarray(offsets[:, 1], dtype=jnp.float32).reshape(1, 1, 1, Q, 1)
    third = jnp.asarray(offsets[:, 2], dtype=jnp.float32).reshape(1, 1, 1, Q, 1)
    density = jax.random.uniform(keys[0], node_shape, jnp.float32, 0.8, 1.2)
    noise = jax.random.uniform(keys[4], (LEVELS, NX, NY, Q, NZ), jnp.float32, -0.3, 0.3)
    along_x = jax.random.uniform(keys[1], node_shape, jnp.float32, -0.1, 0.1)
    along_y = jax.random.uniform(keys[2], node_shape, jnp.float32, -0.1, 0.1)
    along_z = jax.random.uniform(keys[3], node_shape, jnp.float32, -0.1, 0.1)
    projection = along_x * first + along_y * second + along_z * third
    square_speed = along_x * along_x + along_y * along_y + along_z * along_z
    balance = density * (1.0 + 3.0 * projection + 4.5 * projection * projection - 1.5 * square_speed)
    return (balance + noise).astype(jnp.float32)


def with_ends(values, rng, smallest, largest):
    longest = values.shape.index(max(values.shape))
    spots = []
    for shift in (0, 1):
        where = [jax.random.randint(jax.random.fold_in(rng, axis), (), 0, length) for axis, length in enumerate(values.shape)]
        where[longest] = (where[longest] + shift) % values.shape[longest]
        spots.append(tuple(where))
    return values.at[spots[0]].set(smallest).at[spots[1]].set(largest)


def block_levels(rng, extent, shards, low, largest):
    gain = 1.0
    for axis_at, blocks in shards:
        steps = jax.random.uniform(jax.random.fold_in(jax.random.fold_in(rng, 6), axis_at), (blocks,), jnp.float32, low / len(shards), largest / len(shards))
        gain = gain * jnp.repeat(jnp.exp(steps), extent[axis_at] // blocks).reshape((-1,) + (1,) * (len(extent) - 1 - axis_at))
    return gain


def setup_inputs(seed: int = 0) -> dict:
    seeds = jax.random.split(jax.random.key(seed), 8)
    populations = draw_populations(jax.random.fold_in(seeds[7], 71), 0)
    solid_mask = with_ends((jax.random.randint(seeds[1], (LEVELS, NX, NY, NZ), 0, 8) < 1).astype(jnp.int32), jax.random.fold_in(seeds[1], 1), 0, 1)
    relax_rates = jnp.clip(0.8 + 0.99999994 * jax.random.uniform(seeds[2], (LEVELS,), jnp.float32) ** block_levels(seeds[2], (LEVELS,), ((0, 4),), -0.2, 0.2), 0.8, 1.8)
    down_send = draw_down_send(jax.random.fold_in(seeds[7], 71), 0)
    down_recv = draw_down_recv(jax.random.fold_in(seeds[7], 71), 0)
    up_send = draw_up_send(jax.random.fold_in(seeds[7], 71), 0)
    up_recv = draw_up_recv(jax.random.fold_in(seeds[7], 71), 0)
    return dict(populations=populations, solid_mask=solid_mask, relax_rates=relax_rates, down_send=down_send, down_recv=down_recv, up_send=up_send, up_recv=up_recv)


def lattice():
    offsets = np.array([[i // 9 - 1, (i // 3) % 3 - 1, i % 3 - 1] for i in range(27)])
    nonzero = np.sum(np.abs(offsets), axis=1)
    weights = np.array([8.0 / 27.0, 2.0 / 27.0, 1.0 / 54.0, 1.0 / 216.0])[nonzero]
    return offsets, weights


def collide(current, wall_nodes, relax_rate):
    offsets, weights = lattice()
    moment_table = jnp.asarray(np.concatenate([weights[:, None], weights[:, None] * offsets], axis=1), dtype=jnp.float32)
    velocity_table = jnp.asarray(offsets, dtype=jnp.float32)
    moments = jnp.einsum("xyqz,qk->xykz", current, moment_table, precision=lax.Precision.HIGHEST)
    density = moments[:, :, 0:1, :]
    velocity = moments[:, :, 1:4, :] / density
    square_speed = jnp.sum(velocity * velocity, axis=2, keepdims=True)
    projection = jnp.einsum("xykz,qk->xyqz", velocity, velocity_table, precision=lax.Precision.HIGHEST)
    balance = density * (1.0 + 3.0 * projection + 4.5 * projection * projection - 1.5 * square_speed)
    relaxed = current - relax_rate * (current - balance)
    bounced = current[:, :, ::-1, :]
    return jnp.where(wall_nodes[:, :, None, :] == 1, bounced, relaxed)


def spread_lateral(group):
    pieces = []
    for index in range(9):
        lateral = index // 3 - 1
        vertical = index % 3 - 1
        pieces.append(jnp.roll(jnp.roll(group[:, :, index, :], lateral, axis=1), vertical, axis=2))
    return jnp.stack(pieces, axis=2)


def stream_level(collided):
    backward = jnp.roll(collided[:, :, 0:9, :], -1, axis=0)
    middle = collided[:, :, 9:18, :]
    forward = jnp.roll(collided[:, :, 18:27, :], 1, axis=0)
    return jnp.concatenate([spread_lateral(backward), spread_lateral(middle), spread_lateral(forward)], axis=2)


def couple(target, source, send_rows, recv_rows):
    peers = send_rows.shape[0]
    slab_rows = CX * NY
    starts = jnp.arange(peers, dtype=jnp.int32) * slab_rows
    source_index = jnp.transpose(jnp.maximum(send_rows, 0) + starts[:, None, None], (1, 0, 2)).astype(jnp.int32)
    target_index = jnp.where(recv_rows >= 0, recv_rows + starts[:, None, None], peers * slab_rows).astype(jnp.int32)
    flat_source = source.reshape(peers * slab_rows, Q, NZ)
    carried = flat_source[source_index.reshape(-1)]
    flat_target = target.reshape(peers * slab_rows, Q, NZ).at[target_index.reshape(-1)].set(carried, mode="drop")
    return flat_target.reshape(target.shape)


def reference(populations, solid_mask, relax_rates, down_send, down_recv, up_send, up_recv):
    states = [populations[level_index] for level_index in range(LEVELS)]
    for substep in range(SUB):
        for level_index in range(LEVELS):
            if substep % (2 ** (LEVELS - 1 - level_index)) == 0:
                collided = collide(states[level_index], solid_mask[level_index], relax_rates[level_index])
                states[level_index] = stream_level(collided)
        updated = list(states)
        for level_index in range(LEVELS):
            if (substep + 1) % (2 ** (LEVELS - 1 - level_index)) == 0:
                if level_index >= 1:
                    updated[level_index] = couple(updated[level_index], states[level_index - 1], down_send[level_index - 1], down_recv[level_index])
                if level_index <= LEVELS - 2:
                    updated[level_index] = couple(updated[level_index], states[level_index + 1], up_send[level_index + 1], up_recv[level_index])
        states = updated
    return jnp.stack(states)
```

```python
import functools

import jax
import jax.numpy as jnp
from jax import lax
from jax.experimental import pallas as pl
from jax.experimental.pallas import tpu as pltpu
from jax.sharding import PartitionSpec as P

Q = 27
PLANES = 4
WIDTH = 32
ROWS = PLANES * WIDTH
DEPTH = 128
PEERS = 32
LEVELS = 4
HALF = 64
OWN = 32
GHOST = 16
PITCH = 136
QPAD = 32
STATE = QPAD * PITCH
UNIT = 32

VMEM = pl.BlockSpec(memory_space=pltpu.VMEM)
SMEM = pl.BlockSpec(memory_space=pltpu.SMEM)

DOWN_SEND, DOWN_RECV, UP_SEND, UP_RECV = range(4)


def table_at(level, which):
    return (level * 4 + which) * 2 * PEERS


def call(kernel, outs, ins, smem=0, scratch=()):
    return pl.pallas_call(
        kernel,
        out_shape=[jax.ShapeDtypeStruct(shape, jnp.float32) for shape in outs],
        in_specs=[SMEM] * smem + [VMEM] * (len(ins) - smem),
        out_specs=[VMEM] * len(outs),
        scratch_shapes=[pltpu.VMEM(shape, jnp.float32) for shape in scratch],
        compiler_params=pltpu.CompilerParams(vmem_limit_bytes=24 * 1024 * 1024),
    )(*ins)


def lanes_of(shape):
    return lax.broadcasted_iota(jnp.int32, shape, 1)


def in_half(shape, half):
    lanes = lanes_of(shape)
    return lanes < HALF if half == 0 else lanes >= HALF


def turn(value, shift, axis):
    size = value.shape[axis]
    shift = shift % size
    return value if shift == 0 else pltpu.roll(value, shift, axis)


def collide(f, wall, rate):
    t, d = [], []
    for pair in range(9):
        low, mid, high = f[3 * pair : 3 * pair + 3]
        t.append(low + high + 4.0 * mid)
        d.append(high - low)
    total, along_y, along_z = [], [], []
    for a in range(3):
        total.append(t[3 * a] + t[3 * a + 2] + 4.0 * t[3 * a + 1])
        along_y.append(t[3 * a + 2] - t[3 * a])
        along_z.append(d[3 * a] + d[3 * a + 2] + 4.0 * d[3 * a + 1])
    mass = total[0] + total[2] + 4.0 * total[1]
    inverse = 3.0 / mass
    ux = (total[2] - total[0]) * inverse
    uy = (along_y[0] + along_y[2] + 4.0 * along_y[1]) * inverse
    uz = (along_z[0] + along_z[2] + 4.0 * along_z[1]) * inverse
    scaled = rate * mass * (1.0 / 216.0)
    half = 0.5 * scaled
    base = scaled - scaled * ((ux * ux + uy * uy + uz * uz) * (1.0 / 6.0))
    keep = 1.0 - rate
    sums = {
        (0, 0, 1): uz,
        (0, 1, 0): uy,
        (1, 0, 0): ux,
        (0, 1, -1): uy - uz,
        (0, 1, 1): uy + uz,
        (1, 0, -1): ux - uz,
        (1, 0, 1): ux + uz,
        (1, -1, 0): ux - uy,
        (1, 1, 0): ux + uy,
    }
    for b in (-1, 1):
        for e in (-1, 1):
            sums[(1, b, e)] = sums[(1, b, 0)] + uz if e == 1 else sums[(1, b, 0)] - uz
    out = [None] * Q
    out[13] = jnp.where(wall, f[13], keep * f[13] + base)
    for (a, b, e), along in sums.items():
        i = 9 * (a + 1) + 3 * (b + 1) + (e + 1)
        j = 26 - i
        part = half * along
        odd = part + part
        even = base + part * along
        out[i] = jnp.where(wall, f[j], keep * f[i] + (even + odd))
        out[j] = jnp.where(wall, f[i], keep * f[j] + (even - odd))
    return out


def collide_rows(load, wall_ref, rate, c_ref, low_ref, high_ref):
    def tile(i, carry):
        row = pl.multiple_of(i * 8, 8)
        wall = wall_ref[pl.ds(row, 8), :] > 0.5
        out = collide([load(q, row) for q in range(Q)], wall, rate)
        for q in range(Q):
            c_ref[pl.ds(q * ROWS + row, 8), :] = turn(out[q], q % 3 - 1, 1)
        return carry

    lax.fori_loop(0, ROWS // 8, tile, 0)
    for q in range(9):
        low_ref[pl.ds(q * WIDTH, WIDTH), :] = c_ref[pl.ds(q * ROWS, WIDTH), :]
        high_ref[pl.ds(q * WIDTH, WIDTH), :] = c_ref[
            pl.ds((q + 18) * ROWS + ROWS - WIDTH, WIDTH), :
        ]


def streamed(q, plane, c_ref, front_ref, behind_ref):
    source = plane - (q // 9 - 1)
    if source == PLANES:
        value = front_ref[pl.ds((q % 9) * WIDTH, WIDTH), :]
    elif source < 0:
        value = behind_ref[pl.ds((q % 9) * WIDTH, WIDTH), :]
    else:
        value = c_ref[pl.ds(q * ROWS + source * WIDTH, WIDTH), :]
    return turn(value, q // 3 % 3 - 1, 0)


def pick_rows(state_ref, half, tables_ref, at, out_ref, unit, offset):
    group = 4

    def some(g, carry):
        for j in range(group):
            peer = g * group + j
            first = jnp.maximum(tables_ref[at + 2 * peer], 0)
            second = jnp.maximum(tables_ref[at + 2 * peer + 1], 0)
            for c in range(QPAD // 8):
                one = state_ref[pl.ds(first + c * 8 * PITCH, 8, stride=PITCH), :]
                two = state_ref[pl.ds(second + c * 8 * PITCH, 8, stride=PITCH), :]
                if half == 0:
                    two = turn(two, HALF, 1)
                else:
                    one = turn(one, HALF, 1)
                spot = pl.multiple_of(peer * unit + offset + 8 * c, 8)
                out_ref[pl.ds(spot, 8), :] = jnp.where(in_half((8, DEPTH), 0), one, two)
        return carry

    lax.fori_loop(0, PEERS // group, some, 0)


def place_rows(state_ref, half, tables_ref, at, in_ref, unit, offset):
    group = 4

    def some(g, carry):
        stores = []
        for j in range(group):
            peer = g * group + j
            for k in range(2):
                row = tables_ref[at + 2 * peer + k]
                row = jnp.where(row < 0, ROWS, row)
                for c in range(QPAD // 8):
                    spot = pl.multiple_of(peer * unit + offset + 8 * c, 8)
                    value = in_ref[pl.ds(spot, 8), :]
                    if k != half:
                        value = turn(value, HALF, 1)
                    where = pl.ds(row + c * 8 * PITCH, 8, stride=PITCH)
                    stores.append(
                        (where, jnp.where(in_half((8, DEPTH), half), value, state_ref[where, :]))
                    )
        for where, value in stores:
            state_ref[where, :] = value
        return carry

    lax.fori_loop(0, PEERS // group, some, 0)


def copy_state(source_ref, target_ref):
    def one(q, carry):
        at = pl.multiple_of(q * PITCH, 8)
        target_ref[pl.ds(at, ROWS), :] = source_ref[pl.ds(at, ROWS), :]
        return carry

    lax.fori_loop(0, Q, one, 0)


def pair_rate(rates_ref, first, second):
    return jnp.where(in_half((8, DEPTH), 0), rates_ref[first], rates_ref[second])


def first_collide_kernel(rate_ref, x_ref, wall_ref, c_ref, low_ref, high_ref):
    rate = jnp.full((8, DEPTH), rate_ref[0], jnp.float32)

    def load(q, row):
        return x_ref[pl.ds(q * ROWS + row, 8), :]

    collide_rows(load, wall_ref, rate, c_ref, low_ref, high_ref)


def windows_kernel(c_ref, front_ref, behind_ref, wall_ref, out_ref, read_ref):
    for q in range(Q):
        for plane in range(PLANES):
            read_ref[pl.ds(q * ROWS + plane * WIDTH, WIDTH), :] = streamed(
                q, plane, c_ref, front_ref, behind_ref
            )
    read_ref[pl.ds(Q * ROWS, ROWS), :] = wall_ref[...]

    def one(q, carry):
        top = read_ref[pl.ds(pl.multiple_of(q * ROWS, 8), HALF), :]
        bottom = read_ref[pl.ds(pl.multiple_of(q * ROWS + HALF, 8), HALF), :]
        for target in range(LEVELS):
            shift = GHOST - OWN * target
            out_ref[pl.ds(pl.multiple_of((target * (Q + 1) + q) * HALF, 8), HALF), :] = jnp.where(
                in_half((HALF, DEPTH), 0), turn(top, shift, 1), turn(bottom, shift + HALF, 1)
            )
        return carry

    lax.fori_loop(0, Q + 1, one, 0)


def unpack_kernel(tables_ref, in_ref, s_ref, t_ref, wall_s_ref, wall_t_ref, rows_ref):
    def pair(q, first, second):
        one = in_ref[pl.ds(pl.multiple_of((first * (Q + 1) + q) * HALF, 8), HALF), :]
        two = in_ref[pl.ds(pl.multiple_of((second * (Q + 1) + q) * HALF, 8), HALF), :]
        left = in_half((HALF, DEPTH), 0)
        return (
            jnp.where(left, one, turn(two, HALF, 1)),
            jnp.where(left, turn(one, HALF, 1), two),
        )

    def one(q, carry):
        for ref, first, second in ((s_ref, 3, 2), (t_ref, 1, 0)):
            top, bottom = pair(q, first, second)
            at = pl.multiple_of(q * PITCH, 8)
            ref[pl.ds(at, HALF), :] = top
            ref[pl.ds(at + HALF, HALF), :] = bottom
        return carry

    lax.fori_loop(0, Q, one, 0)
    for ref, first, second in ((wall_s_ref, 3, 2), (wall_t_ref, 1, 0)):
        top, bottom = pair(Q, first, second)
        ref[pl.ds(0, HALF), :] = top
        ref[pl.ds(HALF, HALF), :] = bottom
    pick_rows(s_ref, 1, tables_ref, table_at(2, DOWN_SEND), rows_ref, UNIT, 0)


def collide_kernel(levels, couplings, buffers, tables_ref, rates_ref, *refs):
    state_ref, wall_ref = refs[:2]
    in_refs = refs[2 : 2 + buffers]
    c_ref, low_ref, high_ref, work_ref = refs[2 + buffers :]
    copy_state(state_ref, work_ref)
    for half, at, index, unit, offset in couplings:
        place_rows(work_ref, half, tables_ref, at, in_refs[index], unit, offset)

    def load(q, row):
        return work_ref[pl.ds(q * PITCH + row, 8), :]

    collide_rows(
        load, wall_ref, pair_rate(rates_ref, *levels), c_ref, low_ref, high_ref
    )


def stream_kernel(keep, picks, extra, tables_ref, c_ref, front_ref, behind_ref, *refs):
    refs = list(refs)
    old_ref = refs.pop(0) if keep else None
    other_ref = refs.pop(0) if extra else None
    read_ref = refs.pop(0)
    rows_ref = refs.pop(0) if picks else None
    for q in range(Q):
        for plane in range(PLANES):
            value = streamed(q, plane, c_ref, front_ref, behind_ref)
            spot = pl.ds(q * PITCH + plane * WIDTH, WIDTH)
            if keep:
                value = jnp.where(in_half((WIDTH, DEPTH), 0), value, old_ref[spot, :])
            read_ref[spot, :] = value
    for index, (own, half, at) in enumerate(picks):
        source = read_ref if own else other_ref
        pick_rows(source, half, tables_ref, at, rows_ref, UNIT * len(picks), UNIT * index)


def last_kernel(couple_s, couple_t, tables_ref, s_ref, t_ref, b2, b5, b6, b7, out_ref, ws, wt):
    buffers = (b2, b5, b6, b7)
    copy_state(s_ref, ws)
    copy_state(t_ref, wt)
    for work, couplings in ((ws, couple_s), (wt, couple_t)):
        for half, at, index, unit, offset in couplings:
            place_rows(work, half, tables_ref, at, buffers[index], unit, offset)

    def one(q, carry):
        chunk = lanes_of((WIDTH, DEPTH)) // OWN
        for level, (work, half) in enumerate(((wt, 1), (wt, 0), (ws, 1), (ws, 0))):
            packed = None
            for plane in range(PLANES):
                value = work[pl.ds(pl.multiple_of(q * PITCH + plane * WIDTH, 8), WIDTH), :]
                value = turn(value, OWN * plane - HALF * half - GHOST, 1)
                packed = value if packed is None else jnp.where(chunk == plane, value, packed)
            out_ref[pl.ds(pl.multiple_of((level * Q + q) * WIDTH, 8), WIDTH), :] = packed
        return carry

    lax.fori_loop(0, Q, one, 0)


def output_kernel(in_ref, out_ref):
    chunk = lanes_of((WIDTH, DEPTH)) // OWN

    def one(q, carry):
        parts = [
            in_ref[pl.ds(pl.multiple_of((c * Q + q) * WIDTH, 8), WIDTH), :] for c in range(LEVELS)
        ]
        for plane in range(PLANES):
            whole = None
            for c in range(LEVELS):
                value = turn(parts[c], OWN * (c - plane), 1)
                whole = value if whole is None else jnp.where(chunk == c, value, whole)
            out_ref[pl.ds(pl.multiple_of(q * ROWS + plane * WIDTH, 8), WIDTH), :] = whole
        return carry

    lax.fori_loop(0, Q, one, 0)


def trade_planes(low, high):
    count = lax.axis_size("gx")
    forward = [(i, (i + 1) % count) for i in range(count)]
    backward = [(target, source) for source, target in forward]
    return lax.ppermute(low, "gx", backward), lax.ppermute(high, "gx", forward)


def trade_rows(rows, units):
    blocks = rows.reshape(PEERS, UNIT * units, DEPTH)
    return lax.all_to_all(blocks, "gx", split_axis=0, concat_axis=0, tiled=True).reshape(
        rows.shape
    )


def on_device(populations, solid_mask, relax_rates, down_send, down_recv, up_send, up_recv):
    own_tables = jnp.stack(
        [value.reshape(-1) for value in (down_send, down_recv, up_send, up_recv)]
    ).reshape(1, -1)
    tables = lax.all_gather(own_tables, "lvl", axis=0, tiled=True).reshape(-1)
    rates = lax.all_gather(relax_rates, "lvl", axis=0, tiled=True)

    x = jnp.transpose(populations.reshape(ROWS, Q, DEPTH), (1, 0, 2)).reshape(Q * ROWS, DEPTH)
    wall = solid_mask.reshape(ROWS, DEPTH).astype(jnp.float32)
    flow = [(Q * ROWS, DEPTH), (9 * WIDTH, DEPTH), (9 * WIDTH, DEPTH)]
    state = (STATE, DEPTH)

    c, low, high = call(first_collide_kernel, flow, (relax_rates, x, wall), smem=1)
    front, behind = trade_planes(low, high)
    (windows,) = call(
        windows_kernel,
        [(LEVELS * (Q + 1) * HALF, DEPTH)],
        (c, front, behind, wall),
        scratch=[((Q + 1) * ROWS, DEPTH)],
    )
    windows = lax.all_to_all(
        windows.reshape(LEVELS, (Q + 1) * HALF, DEPTH), "lvl", 0, 0, tiled=True
    ).reshape(-1, DEPTH)
    s, t, wall_s, wall_t, rows = call(
        unpack_kernel,
        [state, state, (ROWS, DEPTH), (ROWS, DEPTH), (PEERS * UNIT, DEPTH)],
        (tables, windows),
        smem=1,
    )
    got = {0: (trade_rows(rows, 1), 1)}

    def taken(step, index, half, level, which):
        buffer, units = got[step]
        return buffer, half, table_at(level, which), units * UNIT, index * UNIT

    def collided(value, walls, levels, takes):
        buffers, couplings = [], []
        for buffer, half, at, unit, offset in takes:
            index = next((i for i, b in enumerate(buffers) if b is buffer), len(buffers))
            if index == len(buffers):
                buffers.append(buffer)
            couplings.append((half, at, index, unit, offset))
        return call(
            functools.partial(collide_kernel, levels, couplings, len(buffers)),
            flow,
            (tables, rates, value, walls, *buffers),
            smem=2,
            scratch=[state],
        )

    def stream(c, front, behind, old, picks, other):
        units = len(picks)
        ins = [tables, c, front, behind]
        ins += [old] if old is not None else []
        ins += [other] if other is not None else []
        outs = [state] + ([(PEERS * UNIT * units, DEPTH)] if units else [])
        return call(
            functools.partial(stream_kernel, old is not None, picks, other is not None),
            outs,
            ins,
            smem=1,
        )

    down_23 = (True, 1, table_at(2, DOWN_SEND))
    up_32 = (True, 0, table_at(3, UP_SEND))
    up_21 = (True, 1, table_at(2, UP_SEND))
    down_12 = (False, 0, table_at(1, DOWN_SEND))
    down_01 = (False, 1, table_at(0, DOWN_SEND))
    up_10 = (False, 0, table_at(1, UP_SEND))
    picks = {
        1: [up_32, down_12],
        2: [down_23, down_01],
        3: [up_32, up_21],
        4: [down_23],
        5: [up_32, down_12],
        6: [down_23, up_10],
        7: [up_32, up_21],
    }
    for step in range(1, 8):
        if step % 2:
            takes = [taken(step - 1, 0, 0, 3, DOWN_RECV)]
        else:
            takes = [
                taken(step - 2, 0, 0, 3, DOWN_RECV),
                taken(step - 1, 0, 1, 2, UP_RECV),
                taken(1 if step < 6 else 5, 1, 1, 2, DOWN_RECV),
            ]
        c, low, high = collided(s, wall_s, (3, 2), takes)
        front, behind = trade_planes(low, high)
        if step == 4:
            tc, tlow, thigh = collided(
                t,
                wall_t,
                (1, 0),
                [taken(2, 1, 0, 1, DOWN_RECV), taken(3, 1, 0, 1, UP_RECV)],
            )
            tfront, tbehind = trade_planes(tlow, thigh)
        needs_other = any(not own for own, _, _ in picks[step])
        s, rows = stream(
            c, front, behind, s if step % 2 else None, picks[step], t if needs_other else None
        )
        got[step] = (trade_rows(rows, len(picks[step])), len(picks[step]))
        if step == 4:
            (t,) = stream(tc, tfront, tbehind, t, [], None)

    couple_s = [
        (0, table_at(3, DOWN_RECV), 2, 2 * UNIT, 0),
        (1, table_at(2, UP_RECV), 3, 2 * UNIT, 0),
        (1, table_at(2, DOWN_RECV), 1, 2 * UNIT, UNIT),
    ]
    couple_t = [
        (0, table_at(1, DOWN_RECV), 0, 2 * UNIT, UNIT),
        (0, table_at(1, UP_RECV), 3, 2 * UNIT, UNIT),
        (1, table_at(0, UP_RECV), 2, 2 * UNIT, UNIT),
    ]
    (packed,) = call(
        functools.partial(last_kernel, couple_s, couple_t),
        [(LEVELS * Q * WIDTH, DEPTH)],
        (tables, s, t, *(got[i][0] for i in (2, 5, 6, 7))),
        smem=1,
        scratch=[state, state],
    )
    packed = lax.all_to_all(
        packed.reshape(LEVELS, Q * WIDTH, DEPTH), "lvl", 0, 0, tiled=True
    ).reshape(-1, DEPTH)
    (final,) = call(output_kernel, [(Q * ROWS, DEPTH)], (packed,))
    final = jnp.transpose(final.reshape(Q, ROWS, DEPTH), (1, 0, 2))
    return final.reshape(1, PLANES, WIDTH, Q, DEPTH)


def solution(mesh):
    return jax.shard_map(
        on_device,
        mesh=mesh,
        in_specs=(
            P("lvl", "gx", None, None, None),
            P("lvl", "gx", None, None),
            P("lvl"),
            P("lvl", "gx", None, None),
            P("lvl", "gx", None, None),
            P("lvl", "gx", None, None),
            P("lvl", "gx", None, None),
        ),
        out_specs=P("lvl", "gx", None, None, None),
        check_vma=False,
    )
```

```python
import functools

import jax
import jax.numpy as jnp
from jax import lax
from jax.experimental import pallas as pl
from jax.experimental.pallas import tpu as pltpu
from jax.sharding import PartitionSpec as P

Q = 27
PLANES = 4
WIDTH = 32
ROWS = PLANES * WIDTH
DEPTH = 128
PEERS = 32
LEVELS = 4
HALF = 64
OWN = 32
GHOST = 16
PITCH = 136
QPAD = 32
STATE = QPAD * PITCH
UNIT = 24
GROUPS = 7
META = 8
WINDOW = 3 * GROUPS * HALF + META

VMEM = pl.BlockSpec(memory_space=pltpu.VMEM)
SMEM = pl.BlockSpec(memory_space=pltpu.SMEM)

DOWN_SEND, DOWN_RECV, UP_SEND, UP_RECV = range(4)


def table_at(level, which):
    return (level * 4 + which) * 2 * PEERS


def call(kernel, outs, ins, smem=0, scratch=()):
    return pl.pallas_call(
        kernel,
        out_shape=[jax.ShapeDtypeStruct(shape, jnp.float32) for shape in outs],
        in_specs=[SMEM] * smem + [VMEM] * (len(ins) - smem),
        out_specs=[VMEM] * len(outs),
        scratch_shapes=[pltpu.VMEM(shape, jnp.float32) for shape in scratch],
        compiler_params=pltpu.CompilerParams(vmem_limit_bytes=24 * 1024 * 1024),
    )(*ins)


def lanes_of(shape):
    return lax.broadcasted_iota(jnp.int32, shape, 1)


def in_half(shape, half):
    lanes = lanes_of(shape)
    return lanes < HALF if half == 0 else lanes >= HALF


def turn(value, shift, axis):
    size = value.shape[axis]
    shift = shift % size
    return value if shift == 0 else pltpu.roll(value, shift, axis)


def gaps(shape):
    lanes = lanes_of(shape)
    return (lanes >= 56) & (lanes < 72), (lanes < 8) | (lanes >= 120)


def fold(t0, t1, t2, extra):
    inner, outer = gaps(t0.shape)
    e16, e48, e96 = (turn(extra, shift, 1) for shift in (16, 48, 96))
    return (
        jnp.where(inner, e48, jnp.where(outer, e96, t0)),
        jnp.where(inner, e16, jnp.where(outer, e48, t1)),
        jnp.where(inner, e96, jnp.where(outer, e16, t2)),
    )


def unfold(t0, t1, t2):
    inner, _ = gaps(t0.shape)
    e48 = turn(jnp.where(inner, t0, t1), -48, 1)
    e96 = turn(jnp.where(inner, t2, t0), -96, 1)
    e16 = turn(jnp.where(inner, t1, t2), -16, 1)
    spot = lanes_of(t0.shape) & (HALF - 1)
    return jnp.where(spot < 24, e48, jnp.where(spot < 40, e96, e16))


def collide(f, wall, rate):
    t, d = [], []
    for pair in range(9):
        low, mid, high = f[3 * pair : 3 * pair + 3]
        t.append(low + high + 4.0 * mid)
        d.append(high - low)
    total, along_y, along_z = [], [], []
    for a in range(3):
        total.append(t[3 * a] + t[3 * a + 2] + 4.0 * t[3 * a + 1])
        along_y.append(t[3 * a + 2] - t[3 * a])
        along_z.append(d[3 * a] + d[3 * a + 2] + 4.0 * d[3 * a + 1])
    mass = total[0] + total[2] + 4.0 * total[1]
    inverse = 3.0 / mass
    ux = (total[2] - total[0]) * inverse
    uy = (along_y[0] + along_y[2] + 4.0 * along_y[1]) * inverse
    uz = (along_z[0] + along_z[2] + 4.0 * along_z[1]) * inverse
    scaled = rate * mass * (1.0 / 216.0)
    half = 0.5 * scaled
    base = scaled - scaled * ((ux * ux + uy * uy + uz * uz) * (1.0 / 6.0))
    keep = 1.0 - rate
    sums = {
        (0, 0, 1): uz,
        (0, 1, 0): uy,
        (1, 0, 0): ux,
        (0, 1, -1): uy - uz,
        (0, 1, 1): uy + uz,
        (1, 0, -1): ux - uz,
        (1, 0, 1): ux + uz,
        (1, -1, 0): ux - uy,
        (1, 1, 0): ux + uy,
    }
    for b in (-1, 1):
        for e in (-1, 1):
            sums[(1, b, e)] = sums[(1, b, 0)] + uz if e == 1 else sums[(1, b, 0)] - uz
    out = [None] * Q
    out[13] = jnp.where(wall, f[13], keep * f[13] + base)
    for (a, b, e), along in sums.items():
        i = 9 * (a + 1) + 3 * (b + 1) + (e + 1)
        j = 26 - i
        part = half * along
        odd = part + part
        even = base + part * along
        out[i] = jnp.where(wall, f[j], keep * f[i] + (even + odd))
        out[j] = jnp.where(wall, f[i], keep * f[j] + (even - odd))
    return out


def collide_rows(load, wall_ref, rate, c_ref, low_ref, high_ref):
    def tile(i, carry):
        row = pl.multiple_of(i * 8, 8)
        wall = wall_ref[pl.ds(row, 8), :] > 0.5
        out = collide([load(q, row) for q in range(Q)], wall, rate)
        for q in range(Q):
            c_ref[pl.ds(q * ROWS + row, 8), :] = turn(out[q], q % 3 - 1, 1)
        return carry

    lax.fori_loop(0, ROWS // 8, tile, 0, unroll=2)
    for q in range(9):
        low_ref[pl.ds(q * WIDTH, WIDTH), :] = c_ref[pl.ds(q * ROWS, WIDTH), :]
        high_ref[pl.ds(q * WIDTH, WIDTH), :] = c_ref[
            pl.ds((q + 18) * ROWS + ROWS - WIDTH, WIDTH), :
        ]


def streamed(q, plane, c_ref, front_ref, behind_ref):
    source = plane - (q // 9 - 1)
    if source == PLANES:
        value = front_ref[pl.ds((q % 9) * WIDTH, WIDTH), :]
    elif source < 0:
        value = behind_ref[pl.ds((q % 9) * WIDTH, WIDTH), :]
    else:
        value = c_ref[pl.ds(q * ROWS + source * WIDTH, WIDTH), :]
    return turn(value, q // 3 % 3 - 1, 0)


def pick_rows(state_ref, half, tables_ref, at, out_ref, unit, offset):
    group = 16

    def some(g, carry):
        for j in range(group):
            peer = g * group + j
            first = jnp.maximum(tables_ref[at + 2 * peer], 0)
            second = jnp.maximum(tables_ref[at + 2 * peer + 1], 0)
            merged = []
            for c in range(QPAD // 8):
                one = state_ref[pl.ds(first + c * 8 * PITCH, 8, stride=PITCH), :]
                two = state_ref[pl.ds(second + c * 8 * PITCH, 8, stride=PITCH), :]
                if half == 0:
                    two = turn(two, HALF, 1)
                else:
                    one = turn(one, HALF, 1)
                merged.append(jnp.where(in_half((8, DEPTH), 0), one, two))
            for c, value in enumerate(fold(*merged)):
                spot = pl.multiple_of(peer * unit + offset + 8 * c, 8)
                out_ref[pl.ds(spot, 8), :] = value
        return carry

    lax.fori_loop(0, PEERS // group, some, 0)


def place_rows(state_ref, half, tables_ref, at, in_ref, unit, offset):
    group = 16

    def some(g, carry):
        stores = []
        for j in range(group):
            peer = g * group + j
            parts = [
                in_ref[pl.ds(pl.multiple_of(peer * unit + offset + 8 * c, 8), 8), :]
                for c in range(3)
            ]
            parts.append(unfold(*parts))
            for k in range(2):
                row = tables_ref[at + 2 * peer + k]
                row = jnp.where(row < 0, ROWS, row)
                for c, value in enumerate(parts):
                    if k != half:
                        value = turn(value, HALF, 1)
                    where = pl.ds(row + c * 8 * PITCH, 8, stride=PITCH)
                    stores.append(
                        (where, jnp.where(in_half((8, DEPTH), half), value, state_ref[where, :]))
                    )
        for where, value in stores:
            state_ref[where, :] = value
        return carry

    lax.fori_loop(0, PEERS // group, some, 0)


def copy_state(source_ref, target_ref):
    def one(q, carry):
        at = pl.multiple_of(q * PITCH, 8)
        target_ref[pl.ds(at, ROWS), :] = source_ref[pl.ds(at, ROWS), :]
        return carry

    lax.fori_loop(0, Q, one, 0)


def pair_rate(rates_ref, first, second):
    return jnp.where(in_half((8, DEPTH), 0), rates_ref[first], rates_ref[second])


def first_collide_kernel(rate_ref, x_ref, wall_ref, c_ref, low_ref, high_ref):
    rate = jnp.full((8, DEPTH), rate_ref[0], jnp.float32)

    def load(q, row):
        return x_ref[pl.ds(q * ROWS + row, 8), :]

    collide_rows(load, wall_ref, rate, c_ref, low_ref, high_ref)


def windows_kernel(c_ref, front_ref, behind_ref, wall_ref, meta_ref, out_ref, read_ref):
    for q in range(Q):
        for plane in range(PLANES):
            read_ref[pl.ds(q * ROWS + plane * WIDTH, WIDTH), :] = streamed(
                q, plane, c_ref, front_ref, behind_ref
            )
    read_ref[pl.ds(Q * ROWS, ROWS), :] = wall_ref[...]

    def some(g, carry):
        tops, bottoms = [], []
        for j in range(4):
            at = pl.multiple_of((4 * g + j) * ROWS, 8)
            tops.append(read_ref[pl.ds(at, HALF), :])
            bottoms.append(read_ref[pl.ds(at + HALF, HALF), :])
        for target in range(LEVELS):
            shift = GHOST - OWN * target
            pairs = [
                jnp.where(
                    in_half((HALF, DEPTH), 0), turn(top, shift, 1), turn(bottom, shift + HALF, 1)
                )
                for top, bottom in zip(tops, bottoms)
            ]
            for j, value in enumerate(fold(*pairs)):
                at = pl.multiple_of(target * WINDOW + (3 * g + j) * HALF, 8)
                out_ref[pl.ds(at, HALF), :] = value
        return carry

    lax.fori_loop(0, GROUPS, some, 0)
    for target in range(LEVELS):
        out_ref[pl.ds((target + 1) * WINDOW - META, META), :] = meta_ref[...]


def unpack_kernel(tables_ref, in_ref, s_ref, t_ref, wall_s_ref, wall_t_ref, rows_ref):
    def some(g, carry):
        left = in_half((HALF, DEPTH), 0)
        for ref, first, second in ((s_ref, 3, 2), (t_ref, 1, 0)):
            parts = []
            for level in (first, second):
                at = pl.multiple_of(level * WINDOW + 3 * g * HALF, 8)
                three = [in_ref[pl.ds(at + j * HALF, HALF), :] for j in range(3)]
                parts.append(three + [unfold(*three)])
            for j in range(4):
                one, two = parts[0][j], parts[1][j]
                at = pl.multiple_of((4 * g + j) * PITCH, 8)
                ref[pl.ds(at, HALF), :] = jnp.where(left, one, turn(two, HALF, 1))
                ref[pl.ds(at + HALF, HALF), :] = jnp.where(left, turn(one, HALF, 1), two)
        return carry

    lax.fori_loop(0, GROUPS, some, 0)
    wall_s_ref[...] = s_ref[pl.ds(Q * PITCH, ROWS), :]
    wall_t_ref[...] = t_ref[pl.ds(Q * PITCH, ROWS), :]
    pick_rows(s_ref, 1, tables_ref, table_at(2, DOWN_SEND), rows_ref, UNIT, 0)


def collide_kernel(levels, couplings, buffers, tables_ref, rates_ref, *refs):
    state_ref, wall_ref = refs[:2]
    in_refs = refs[2 : 2 + buffers]
    c_ref, low_ref, high_ref, work_ref = refs[2 + buffers :]
    copy_state(state_ref, work_ref)
    for half, at, index, unit, offset in couplings:
        place_rows(work_ref, half, tables_ref, at, in_refs[index], unit, offset)

    def load(q, row):
        return work_ref[pl.ds(q * PITCH + row, 8), :]

    collide_rows(
        load, wall_ref, pair_rate(rates_ref, *levels), c_ref, low_ref, high_ref
    )


def stream_kernel(keep, picks, extra, tables_ref, c_ref, front_ref, behind_ref, *refs):
    refs = list(refs)
    old_ref = refs.pop(0) if keep else None
    other_ref = refs.pop(0) if extra else None
    read_ref = refs.pop(0)
    rows_ref = refs.pop(0) if picks else None
    for q in range(Q):
        for plane in range(PLANES):
            value = streamed(q, plane, c_ref, front_ref, behind_ref)
            spot = pl.ds(q * PITCH + plane * WIDTH, WIDTH)
            if keep:
                value = jnp.where(in_half((WIDTH, DEPTH), 0), value, old_ref[spot, :])
            read_ref[spot, :] = value
    for index, (own, half, at) in enumerate(picks):
        source = read_ref if own else other_ref
        pick_rows(source, half, tables_ref, at, rows_ref, UNIT * len(picks), UNIT * index)


def last_kernel(couple_s, couple_t, tables_ref, s_ref, t_ref, b2, b5, b6, b7, out_ref, ws, wt):
    buffers = (b2, b5, b6, b7)
    copy_state(s_ref, ws)
    copy_state(t_ref, wt)
    for work, couplings in ((ws, couple_s), (wt, couple_t)):
        for half, at, index, unit, offset in couplings:
            place_rows(work, half, tables_ref, at, buffers[index], unit, offset)

    def one(q, carry):
        chunk = lanes_of((WIDTH, DEPTH)) // OWN
        for level, (work, half) in enumerate(((wt, 1), (wt, 0), (ws, 1), (ws, 0))):
            packed = None
            for plane in range(PLANES):
                value = work[pl.ds(pl.multiple_of(q * PITCH + plane * WIDTH, 8), WIDTH), :]
                value = turn(value, OWN * plane - HALF * half - GHOST, 1)
                packed = value if packed is None else jnp.where(chunk == plane, value, packed)
            out_ref[pl.ds(pl.multiple_of((level * Q + q) * WIDTH, 8), WIDTH), :] = packed
        return carry

    lax.fori_loop(0, Q, one, 0)


def output_kernel(in_ref, out_ref):
    chunk = lanes_of((WIDTH, DEPTH)) // OWN

    def one(q, carry):
        parts = [
            in_ref[pl.ds(pl.multiple_of((c * Q + q) * WIDTH, 8), WIDTH), :] for c in range(LEVELS)
        ]
        for plane in range(PLANES):
            whole = None
            for c in range(LEVELS):
                value = turn(parts[c], OWN * (c - plane), 1)
                whole = value if whole is None else jnp.where(chunk == c, value, whole)
            out_ref[pl.ds(pl.multiple_of(q * ROWS + plane * WIDTH, 8), WIDTH), :] = whole
        return carry

    lax.fori_loop(0, Q, one, 0)


def trade_planes(low, high):
    count = lax.axis_size("gx")
    forward = [(i, (i + 1) % count) for i in range(count)]
    backward = [(target, source) for source, target in forward]
    return lax.ppermute(low, "gx", backward), lax.ppermute(high, "gx", forward)


def trade_rows(rows, units):
    blocks = rows.reshape(PEERS, UNIT * units, DEPTH)
    return lax.all_to_all(blocks, "gx", split_axis=0, concat_axis=0, tiled=True).reshape(
        rows.shape
    )


def on_device(populations, solid_mask, relax_rates, down_send, down_recv, up_send, up_recv):
    meta = jnp.concatenate(
        [value.reshape(-1) for value in (down_send, down_recv, up_send, up_recv)]
    ).astype(jnp.float32)
    meta = jnp.concatenate([meta, jnp.broadcast_to(relax_rates, (META * DEPTH - meta.size,))])
    meta = meta.reshape(META, DEPTH)
    x = jnp.transpose(populations.reshape(ROWS, Q, DEPTH), (1, 0, 2)).reshape(Q * ROWS, DEPTH)
    wall = solid_mask.reshape(ROWS, DEPTH).astype(jnp.float32)
    flow = [(Q * ROWS, DEPTH), (9 * WIDTH, DEPTH), (9 * WIDTH, DEPTH)]
    state = (STATE, DEPTH)

    c, low, high = call(first_collide_kernel, flow, (relax_rates, x, wall), smem=1)
    front, behind = trade_planes(low, high)
    (windows,) = call(
        windows_kernel,
        [(LEVELS * WINDOW, DEPTH)],
        (c, front, behind, wall, meta),
        scratch=[((Q + 1) * ROWS, DEPTH)],
    )
    windows = lax.all_to_all(
        windows.reshape(LEVELS, WINDOW, DEPTH), "lvl", 0, 0, tiled=True
    )
    tables = windows[:, WINDOW - META : WINDOW - META + 2, :].astype(jnp.int32).reshape(-1)
    rates = windows[:, WINDOW - 1, 0]
    windows = windows.reshape(-1, DEPTH)
    s, t, wall_s, wall_t, rows = call(
        unpack_kernel,
        [state, state, (ROWS, DEPTH), (ROWS, DEPTH), (PEERS * UNIT, DEPTH)],
        (tables, windows),
        smem=1,
    )
    got = {0: (trade_rows(rows, 1), 1)}

    def taken(step, index, half, level, which):
        buffer, units = got[step]
        return buffer, half, table_at(level, which), units * UNIT, index * UNIT

    def collided(value, walls, levels, takes):
        buffers, couplings = [], []
        for buffer, half, at, unit, offset in takes:
            index = next((i for i, b in enumerate(buffers) if b is buffer), len(buffers))
            if index == len(buffers):
                buffers.append(buffer)
            couplings.append((half, at, index, unit, offset))
        return call(
            functools.partial(collide_kernel, levels, couplings, len(buffers)),
            flow,
            (tables, rates, value, walls, *buffers),
            smem=2,
            scratch=[state],
        )

    def stream(c, front, behind, old, picks, other):
        units = len(picks)
        ins = [tables, c, front, behind]
        ins += [old] if old is not None else []
        ins += [other] if other is not None else []
        outs = [state] + ([(PEERS * UNIT * units, DEPTH)] if units else [])
        return call(
            functools.partial(stream_kernel, old is not None, picks, other is not None),
            outs,
            ins,
            smem=1,
        )

    down_23 = (True, 1, table_at(2, DOWN_SEND))
    up_32 = (True, 0, table_at(3, UP_SEND))
    up_21 = (True, 1, table_at(2, UP_SEND))
    down_12 = (False, 0, table_at(1, DOWN_SEND))
    down_01 = (False, 1, table_at(0, DOWN_SEND))
    up_10 = (False, 0, table_at(1, UP_SEND))
    picks = {
        1: [up_32, down_12],
        2: [down_23, down_01],
        3: [up_32, up_21],
        4: [down_23],
        5: [up_32, down_12],
        6: [down_23, up_10],
        7: [up_32, up_21],
    }
    for step in range(1, 8):
        if step % 2:
            takes = [taken(step - 1, 0, 0, 3, DOWN_RECV)]
        else:
            takes = [
                taken(step - 2, 0, 0, 3, DOWN_RECV),
                taken(step - 1, 0, 1, 2, UP_RECV),
                taken(1 if step < 6 else 5, 1, 1, 2, DOWN_RECV),
            ]
        c, low, high = collided(s, wall_s, (3, 2), takes)
        front, behind = trade_planes(low, high)
        if step == 4:
            tc, tlow, thigh = collided(
                t,
                wall_t,
                (1, 0),
                [taken(2, 1, 0, 1, DOWN_RECV), taken(3, 1, 0, 1, UP_RECV)],
            )
            tfront, tbehind = trade_planes(tlow, thigh)
        needs_other = any(not own for own, _, _ in picks[step])
        s, rows = stream(
            c, front, behind, s if step % 2 else None, picks[step], t if needs_other else None
        )
        got[step] = (trade_rows(rows, len(picks[step])), len(picks[step]))
        if step == 4:
            (t,) = stream(tc, tfront, tbehind, t, [], None)

    couple_s = [
        (0, table_at(3, DOWN_RECV), 2, 2 * UNIT, 0),
        (1, table_at(2, UP_RECV), 3, 2 * UNIT, 0),
        (1, table_at(2, DOWN_RECV), 1, 2 * UNIT, UNIT),
    ]
    couple_t = [
        (0, table_at(1, DOWN_RECV), 0, 2 * UNIT, UNIT),
        (0, table_at(1, UP_RECV), 3, 2 * UNIT, UNIT),
        (1, table_at(0, UP_RECV), 2, 2 * UNIT, UNIT),
    ]
    (packed,) = call(
        functools.partial(last_kernel, couple_s, couple_t),
        [(LEVELS * Q * WIDTH, DEPTH)],
        (tables, s, t, *(got[i][0] for i in (2, 5, 6, 7))),
        smem=1,
        scratch=[state, state],
    )
    packed = lax.all_to_all(
        packed.reshape(LEVELS, Q * WIDTH, DEPTH), "lvl", 0, 0, tiled=True
    ).reshape(-1, DEPTH)
    (final,) = call(output_kernel, [(Q * ROWS, DEPTH)], (packed,))
    final = jnp.transpose(final.reshape(Q, ROWS, DEPTH), (1, 0, 2))
    return final.reshape(1, PLANES, WIDTH, Q, DEPTH)


def solution(mesh):
    return jax.shard_map(
        on_device,
        mesh=mesh,
        in_specs=(
            P("lvl", "gx", None, None, None),
            P("lvl", "gx", None, None),
            P("lvl"),
            P("lvl", "gx", None, None),
            P("lvl", "gx", None, None),
            P("lvl", "gx", None, None),
            P("lvl", "gx", None, None),
        ),
        out_specs=P("lvl", "gx", None, None, None),
        check_vma=False,
    )
```

```python
import functools

import jax
import jax.numpy as jnp
from jax import lax
from jax.experimental import pallas as pl
from jax.experimental.pallas import tpu as pltpu
from jax.sharding import PartitionSpec as P

Q = 27
PLANES = 4
WIDTH = 32
ROWS = PLANES * WIDTH
DEPTH = 128
PEERS = 32
LEVELS = 4
HALF = 64
OWN = 32
GHOST = 16
PITCH = 136
QPAD = 32
STATE = QPAD * PITCH
UNIT = 24
GROUPS = 7
META = 8
WINDOW = 3 * GROUPS * HALF + META

VMEM = pl.BlockSpec(memory_space=pltpu.VMEM)
SMEM = pl.BlockSpec(memory_space=pltpu.SMEM)

DOWN_SEND, DOWN_RECV, UP_SEND, UP_RECV = range(4)


def table_at(level, which):
    return (level * 4 + which) * 2 * PEERS


def call(kernel, outs, ins, smem=0, scratch=(), aliases=None):
    moved = sum(value.size for value in ins) + sum(rows * depth for rows, depth in outs)
    return pl.pallas_call(
        kernel,
        out_shape=[jax.ShapeDtypeStruct(shape, jnp.float32) for shape in outs],
        in_specs=[SMEM] * smem + [VMEM] * (len(ins) - smem),
        out_specs=[VMEM] * len(outs),
        scratch_shapes=[pltpu.VMEM(shape, jnp.float32) for shape in scratch],
        input_output_aliases=aliases or {},
        cost_estimate=pl.CostEstimate(
            flops=10 * moved, bytes_accessed=4 * moved, transcendentals=0
        ),
        compiler_params=pltpu.CompilerParams(vmem_limit_bytes=24 * 1024 * 1024),
    )(*ins)


def lanes_of(shape):
    return lax.broadcasted_iota(jnp.int32, shape, 1)


def in_half(shape, half):
    lanes = lanes_of(shape)
    return lanes < HALF if half == 0 else lanes >= HALF


def turn(value, shift, axis):
    size = value.shape[axis]
    shift = shift % size
    return value if shift == 0 else pltpu.roll(value, shift, axis)


def gaps(shape):
    lanes = lanes_of(shape)
    return (lanes >= 56) & (lanes < 72), (lanes < 8) | (lanes >= 120)


def fold(t0, t1, t2, extra):
    inner, outer = gaps(t0.shape)
    e16, e48, e96 = (turn(extra, shift, 1) for shift in (16, 48, 96))
    return (
        jnp.where(inner, e48, jnp.where(outer, e96, t0)),
        jnp.where(inner, e16, jnp.where(outer, e48, t1)),
        jnp.where(inner, e96, jnp.where(outer, e16, t2)),
    )


def unfold(t0, t1, t2):
    inner, _ = gaps(t0.shape)
    e48 = turn(jnp.where(inner, t0, t1), -48, 1)
    e96 = turn(jnp.where(inner, t2, t0), -96, 1)
    e16 = turn(jnp.where(inner, t1, t2), -16, 1)
    spot = lanes_of(t0.shape) & (HALF - 1)
    return jnp.where(spot < 24, e48, jnp.where(spot < 40, e96, e16))


def collide(f, wall, rate):
    t, d = [], []
    for pair in range(9):
        low, mid, high = f[3 * pair : 3 * pair + 3]
        t.append(low + high + 4.0 * mid)
        d.append(high - low)
    total, along_y, along_z = [], [], []
    for a in range(3):
        total.append(t[3 * a] + t[3 * a + 2] + 4.0 * t[3 * a + 1])
        along_y.append(t[3 * a + 2] - t[3 * a])
        along_z.append(d[3 * a] + d[3 * a + 2] + 4.0 * d[3 * a + 1])
    mass = total[0] + total[2] + 4.0 * total[1]
    inverse = 3.0 / mass
    ux = (total[2] - total[0]) * inverse
    uy = (along_y[0] + along_y[2] + 4.0 * along_y[1]) * inverse
    uz = (along_z[0] + along_z[2] + 4.0 * along_z[1]) * inverse
    scaled = rate * mass * (1.0 / 216.0)
    half = 0.5 * scaled
    base = scaled - scaled * ((ux * ux + uy * uy + uz * uz) * (1.0 / 6.0))
    keep = 1.0 - rate
    sums = {
        (0, 0, 1): uz,
        (0, 1, 0): uy,
        (1, 0, 0): ux,
        (0, 1, -1): uy - uz,
        (0, 1, 1): uy + uz,
        (1, 0, -1): ux - uz,
        (1, 0, 1): ux + uz,
        (1, -1, 0): ux - uy,
        (1, 1, 0): ux + uy,
    }
    for b in (-1, 1):
        for e in (-1, 1):
            sums[(1, b, e)] = sums[(1, b, 0)] + uz if e == 1 else sums[(1, b, 0)] - uz
    out = [None] * Q
    out[13] = jnp.where(wall, f[13], keep * f[13] + base)
    for (a, b, e), along in sums.items():
        i = 9 * (a + 1) + 3 * (b + 1) + (e + 1)
        j = 26 - i
        part = half * along
        odd = part + part
        even = base + part * along
        out[i] = jnp.where(wall, f[j], keep * f[i] + (even + odd))
        out[j] = jnp.where(wall, f[i], keep * f[j] + (even - odd))
    return out


def collide_rows(load, wall_ref, rate, store, tiles):
    def tile(i, carry):
        row = pl.multiple_of(tiles(i) * 8, 8)
        wall = wall_ref[pl.ds(row, 8), :] > 0.5
        out = collide([load(q, row) for q in range(Q)], wall, rate)
        for q in range(Q):
            store(q, row, turn(out[q], q % 3 - 1, 1))
        return carry

    lax.fori_loop(0, ROWS // 16, tile, 0, unroll=2)


def edge_tiles(i):
    return jnp.where(i < 4, i, i + 8)


def inner_tiles(i):
    return i + 4


def collide_edges(load, wall_ref, rate, edge_ref, low_ref, high_ref):
    def store(q, row, value):
        at = jnp.where(row < WIDTH, row, row - 2 * WIDTH)
        edge_ref[pl.ds(pl.multiple_of(q * HALF + at, 8), 8), :] = value

    collide_rows(load, wall_ref, rate, store, edge_tiles)
    for q in range(9):
        spot = pl.ds(q * WIDTH, WIDTH)
        low_ref[spot, :] = edge_ref[pl.ds(q * HALF, WIDTH), :]
        high_ref[spot, :] = edge_ref[pl.ds((q + 18) * HALF + WIDTH, WIDTH), :]


def collide_inside(load, wall_ref, rate, inside_ref):
    def store(q, row, value):
        inside_ref[pl.ds(pl.multiple_of(q * HALF + row - WIDTH, 8), 8), :] = value

    collide_rows(load, wall_ref, rate, store, inner_tiles)


def stream_known(edge_ref, inside_ref, read_ref, pitch, old_ref):
    for q in range(Q):
        for plane in range(PLANES):
            source = plane - (q // 9 - 1)
            spot = pl.ds(q * pitch + plane * WIDTH, WIDTH)
            if 0 <= source < PLANES:
                if source in (0, PLANES - 1):
                    value = edge_ref[pl.ds(q * HALF + (WIDTH if source else 0), WIDTH), :]
                else:
                    value = inside_ref[pl.ds(q * HALF + (source - 1) * WIDTH, WIDTH), :]
                value = turn(value, q // 3 % 3 - 1, 0)
                if old_ref is not None:
                    value = jnp.where(in_half((WIDTH, DEPTH), 0), value, old_ref[spot, :])
                read_ref[spot, :] = value
            elif old_ref is not None:
                read_ref[spot, :] = old_ref[spot, :]


def stream_rest(front_ref, behind_ref, read_ref, pitch, keep):
    for q in range(9):
        for velocity, plane, ref in ((q, PLANES - 1, front_ref), (q + 18, 0, behind_ref)):
            spot = pl.ds(velocity * pitch + plane * WIDTH, WIDTH)
            value = turn(ref[pl.ds(q * WIDTH, WIDTH), :], q // 3 - 1, 0)
            if keep:
                value = jnp.where(in_half((WIDTH, DEPTH), 0), value, read_ref[spot, :])
            read_ref[spot, :] = value


def pick_rows(state_ref, half, tables_ref, at, out_ref, unit, offset):
    group = 16

    def some(g, carry):
        for j in range(group):
            peer = g * group + j
            first = jnp.maximum(tables_ref[at + 2 * peer], 0)
            second = jnp.maximum(tables_ref[at + 2 * peer + 1], 0)
            merged = []
            for c in range(QPAD // 8):
                one = state_ref[pl.ds(first + c * 8 * PITCH, 8, stride=PITCH), :]
                two = state_ref[pl.ds(second + c * 8 * PITCH, 8, stride=PITCH), :]
                if half == 0:
                    two = turn(two, HALF, 1)
                else:
                    one = turn(one, HALF, 1)
                merged.append(jnp.where(in_half((8, DEPTH), 0), one, two))
            for c, value in enumerate(fold(*merged)):
                spot = pl.multiple_of(peer * unit + offset + 8 * c, 8)
                out_ref[pl.ds(spot, 8), :] = value
        return carry

    lax.fori_loop(0, PEERS // group, some, 0)


def place_rows(state_ref, half, tables_ref, at, in_ref, unit, offset):
    group = 16

    def some(g, carry):
        stores = []
        for j in range(group):
            peer = g * group + j
            parts = [
                in_ref[pl.ds(pl.multiple_of(peer * unit + offset + 8 * c, 8), 8), :]
                for c in range(3)
            ]
            parts.append(unfold(*parts))
            for k in range(2):
                row = tables_ref[at + 2 * peer + k]
                row = jnp.where(row < 0, ROWS, row)
                for c, value in enumerate(parts):
                    if k != half:
                        value = turn(value, HALF, 1)
                    where = pl.ds(row + c * 8 * PITCH, 8, stride=PITCH)
                    stores.append(
                        (where, jnp.where(in_half((8, DEPTH), half), value, state_ref[where, :]))
                    )
        for where, value in stores:
            state_ref[where, :] = value
        return carry

    lax.fori_loop(0, PEERS // group, some, 0)


def copy_state(source_ref, target_ref):
    def one(q, carry):
        at = pl.multiple_of(q * PITCH, 8)
        target_ref[pl.ds(at, ROWS), :] = source_ref[pl.ds(at, ROWS), :]
        return carry

    lax.fori_loop(0, Q, one, 0)


def pair_rate(rates_ref, first, second):
    return jnp.where(in_half((8, DEPTH), 0), rates_ref[first], rates_ref[second])


def first_edges_kernel(rate_ref, x_ref, wall_ref, edge_ref, low_ref, high_ref):
    rate = jnp.full((8, DEPTH), rate_ref[0], jnp.float32)

    def load(q, row):
        return x_ref[pl.ds(q * ROWS + row, 8), :]

    collide_edges(load, wall_ref, rate, edge_ref, low_ref, high_ref)


def first_inside_kernel(rate_ref, x_ref, wall_ref, edge_ref, read_ref, inside_ref):
    rate = jnp.full((8, DEPTH), rate_ref[0], jnp.float32)

    def load(q, row):
        return x_ref[pl.ds(q * ROWS + row, 8), :]

    collide_inside(load, wall_ref, rate, inside_ref)
    stream_known(edge_ref, inside_ref, read_ref, ROWS, None)


def windows_kernel(seen_ref, front_ref, behind_ref, wall_ref, meta_ref, out_ref, read_ref):
    read_ref[pl.ds(0, Q * ROWS), :] = seen_ref[...]
    stream_rest(front_ref, behind_ref, read_ref, ROWS, False)
    read_ref[pl.ds(Q * ROWS, ROWS), :] = wall_ref[...]

    def some(g, carry):
        tops, bottoms = [], []
        for j in range(4):
            at = pl.multiple_of((4 * g + j) * ROWS, 8)
            tops.append(read_ref[pl.ds(at, HALF), :])
            bottoms.append(read_ref[pl.ds(at + HALF, HALF), :])
        for target in range(LEVELS):
            shift = GHOST - OWN * target
            pairs = [
                jnp.where(
                    in_half((HALF, DEPTH), 0), turn(top, shift, 1), turn(bottom, shift + HALF, 1)
                )
                for top, bottom in zip(tops, bottoms)
            ]
            for j, value in enumerate(fold(*pairs)):
                at = pl.multiple_of(target * WINDOW + (3 * g + j) * HALF, 8)
                out_ref[pl.ds(at, HALF), :] = value
        return carry

    lax.fori_loop(0, GROUPS, some, 0)
    for target in range(LEVELS):
        out_ref[pl.ds((target + 1) * WINDOW - META, META), :] = meta_ref[...]


def unpack_kernel(tables_ref, in_ref, s_ref, t_ref, wall_s_ref, wall_t_ref, rows_ref):
    def some(g, carry):
        left = in_half((HALF, DEPTH), 0)
        for ref, first, second in ((s_ref, 3, 2), (t_ref, 1, 0)):
            parts = []
            for level in (first, second):
                at = pl.multiple_of(level * WINDOW + 3 * g * HALF, 8)
                three = [in_ref[pl.ds(at + j * HALF, HALF), :] for j in range(3)]
                parts.append(three + [unfold(*three)])
            for j in range(4):
                one, two = parts[0][j], parts[1][j]
                at = pl.multiple_of((4 * g + j) * PITCH, 8)
                ref[pl.ds(at, HALF), :] = jnp.where(left, one, turn(two, HALF, 1))
                ref[pl.ds(at + HALF, HALF), :] = jnp.where(left, turn(one, HALF, 1), two)
        return carry

    lax.fori_loop(0, GROUPS, some, 0)
    wall_s_ref[...] = s_ref[pl.ds(Q * PITCH, ROWS), :]
    wall_t_ref[...] = t_ref[pl.ds(Q * PITCH, ROWS), :]
    pick_rows(s_ref, 1, tables_ref, table_at(2, DOWN_SEND), rows_ref, UNIT, 0)


def edges_kernel(levels, couplings, buffers, tables_ref, rates_ref, *refs):
    state_ref, wall_ref = refs[:2]
    in_refs = refs[2 : 2 + buffers]
    work_ref, edge_ref, low_ref, high_ref = refs[2 + buffers :]
    copy_state(state_ref, work_ref)
    for half, at, index, unit, offset in couplings:
        place_rows(work_ref, half, tables_ref, at, in_refs[index], unit, offset)

    def load(q, row):
        return work_ref[pl.ds(q * PITCH + row, 8), :]

    rate = pair_rate(rates_ref, *levels)
    collide_edges(load, wall_ref, rate, edge_ref, low_ref, high_ref)


def inside_kernel(levels, keep, extra, tables_ref, rates_ref, *refs):
    refs = list(refs)
    work_ref, wall_ref, edge_ref = refs.pop(0), refs.pop(0), refs.pop(0)
    old_ref = refs.pop(0) if keep else None
    other_ref = refs.pop(0) if extra and not extra[0] else None
    inside_ref = refs.pop()
    read_ref = refs.pop(0)

    def load(q, row):
        return work_ref[pl.ds(q * PITCH + row, 8), :]

    collide_inside(load, wall_ref, pair_rate(rates_ref, *levels), inside_ref)
    stream_known(edge_ref, inside_ref, read_ref, PITCH, old_ref)
    if extra:
        own, half, at = extra
        source = old_ref if own else other_ref
        pick_rows(source, half, tables_ref, at, refs.pop(0), 2 * UNIT, UNIT)


def rest_kernel(keep, pick, extra, tables_ref, front_ref, behind_ref, *refs):
    if pick:
        seen_ref, rows_ref = refs[-2:]
    else:
        seen_ref = refs[-1]
    stream_rest(front_ref, behind_ref, seen_ref, PITCH, keep)
    if pick:
        half, at = pick
        pick_rows(seen_ref, half, tables_ref, at, rows_ref, 2 * UNIT if extra else UNIT, 0)


def last_kernel(couple_s, couple_t, tables_ref, s_ref, t_ref, b2, b5, b6, b7, out_ref, ws, wt):
    buffers = (b2, b5, b6, b7)
    copy_state(s_ref, ws)
    copy_state(t_ref, wt)
    for work, couplings in ((ws, couple_s), (wt, couple_t)):
        for half, at, index, unit, offset in couplings:
            place_rows(work, half, tables_ref, at, buffers[index], unit, offset)

    def one(q, carry):
        chunk = lanes_of((WIDTH, DEPTH)) // OWN
        for level, (work, half) in enumerate(((wt, 1), (wt, 0), (ws, 1), (ws, 0))):
            packed = None
            for plane in range(PLANES):
                value = work[pl.ds(pl.multiple_of(q * PITCH + plane * WIDTH, 8), WIDTH), :]
                value = turn(value, OWN * plane - HALF * half - GHOST, 1)
                packed = value if packed is None else jnp.where(chunk == plane, value, packed)
            out_ref[pl.ds(pl.multiple_of((level * Q + q) * WIDTH, 8), WIDTH), :] = packed
        return carry

    lax.fori_loop(0, Q, one, 0)


def output_kernel(in_ref, out_ref):
    chunk = lanes_of((WIDTH, DEPTH)) // OWN

    def one(q, carry):
        parts = [
            in_ref[pl.ds(pl.multiple_of((c * Q + q) * WIDTH, 8), WIDTH), :] for c in range(LEVELS)
        ]
        for plane in range(PLANES):
            whole = None
            for c in range(LEVELS):
                value = turn(parts[c], OWN * (c - plane), 1)
                whole = value if whole is None else jnp.where(chunk == c, value, whole)
            out_ref[pl.ds(pl.multiple_of(q * ROWS + plane * WIDTH, 8), WIDTH), :] = whole
        return carry

    lax.fori_loop(0, Q, one, 0)


def trade_planes(low, high):
    count = lax.axis_size("gx")
    forward = [(i, (i + 1) % count) for i in range(count)]
    backward = [(target, source) for source, target in forward]
    return lax.ppermute(low, "gx", backward), lax.ppermute(high, "gx", forward)


def trade_rows(rows, units):
    blocks = rows.reshape(PEERS, UNIT * units, DEPTH)
    return lax.all_to_all(blocks, "gx", split_axis=0, concat_axis=0, tiled=True).reshape(
        rows.shape
    )


def on_device(populations, solid_mask, relax_rates, down_send, down_recv, up_send, up_recv):
    meta = jnp.concatenate(
        [value.reshape(-1) for value in (down_send, down_recv, up_send, up_recv)]
    ).astype(jnp.float32)
    meta = jnp.concatenate([meta, jnp.broadcast_to(relax_rates, (META * DEPTH - meta.size,))])
    meta = meta.reshape(META, DEPTH)
    x = jnp.transpose(populations.reshape(ROWS, Q, DEPTH), (1, 0, 2)).reshape(Q * ROWS, DEPTH)
    wall = solid_mask.reshape(ROWS, DEPTH).astype(jnp.float32)
    flow = [(Q * ROWS, DEPTH), (9 * WIDTH, DEPTH), (9 * WIDTH, DEPTH)]
    state = (STATE, DEPTH)

    edge, low, high = call(
        first_edges_kernel, [(Q * HALF, DEPTH), *flow[1:]], (relax_rates, x, wall), smem=1
    )
    front, behind = trade_planes(low, high)
    (seen,) = call(
        first_inside_kernel,
        [flow[0]],
        (relax_rates, x, wall, edge),
        smem=1,
        scratch=[(Q * HALF, DEPTH)],
    )
    (windows,) = call(
        windows_kernel,
        [(LEVELS * WINDOW, DEPTH)],
        (seen, front, behind, wall, meta),
        scratch=[((Q + 1) * ROWS, DEPTH)],
    )
    windows = lax.all_to_all(
        windows.reshape(LEVELS, WINDOW, DEPTH), "lvl", 0, 0, tiled=True
    )
    tables = windows[:, WINDOW - META : WINDOW - META + 2, :].astype(jnp.int32).reshape(-1)
    rates = windows[:, WINDOW - 1, 0]
    windows = windows.reshape(-1, DEPTH)
    s, t, wall_s, wall_t, rows = call(
        unpack_kernel,
        [state, state, (ROWS, DEPTH), (ROWS, DEPTH), (PEERS * UNIT, DEPTH)],
        (tables, windows),
        smem=1,
    )
    got = {0: (trade_rows(rows, 1), 1)}

    def taken(step, index, half, level, which):
        buffer, units = got[step]
        return buffer, half, table_at(level, which), units * UNIT, index * UNIT

    def advance(value, walls, levels, takes, keep, pick=None, extra=None, other=None):
        buffers, couplings = [], []
        for buffer, half, at, unit, offset in takes:
            index = next((i for i, b in enumerate(buffers) if b is buffer), len(buffers))
            if index == len(buffers):
                buffers.append(buffer)
            couplings.append((half, at, index, unit, offset))
        work, edge, low, high = call(
            functools.partial(edges_kernel, levels, couplings, len(buffers)),
            [state, (Q * HALF, DEPTH), *flow[1:]],
            (tables, rates, value, walls, *buffers),
            smem=2,
        )
        front, behind = trade_planes(low, high)
        ins = [tables, rates, work, walls, edge]
        ins += [value] if keep else []
        ins += [other] if extra and not extra[0] else []
        seen, *rows = call(
            functools.partial(inside_kernel, levels, keep, extra),
            [state] + ([(PEERS * 2 * UNIT, DEPTH)] if extra else []),
            ins,
            smem=2,
            scratch=[(Q * HALF, DEPTH)],
        )
        return call(
            functools.partial(rest_kernel, keep, pick, extra),
            [state] + ([(PEERS * (2 if extra else 1) * UNIT, DEPTH)] if pick else []),
            (tables, front, behind, seen, *rows),
            smem=1,
            aliases={3: 0, 4: 1} if extra else {3: 0},
        )

    down_23 = (1, table_at(2, DOWN_SEND))
    up_32 = (0, table_at(3, UP_SEND))
    up_21 = (True, 1, table_at(2, UP_SEND))
    down_12 = (False, 0, table_at(1, DOWN_SEND))
    down_01 = (False, 1, table_at(0, DOWN_SEND))
    up_10 = (False, 0, table_at(1, UP_SEND))
    extras = {1: down_12, 2: down_01, 3: up_21, 5: down_12, 6: up_10, 7: up_21}
    for step in range(1, 8):
        odd = step % 2 == 1
        if odd:
            takes = [taken(step - 1, 0, 0, 3, DOWN_RECV)]
        else:
            takes = [
                taken(step - 2, 0, 0, 3, DOWN_RECV),
                taken(step - 1, 0, 1, 2, UP_RECV),
                taken(1 if step < 6 else 5, 1, 1, 2, DOWN_RECV),
            ]
        extra = extras.get(step)
        s, rows = advance(
            s, wall_s, (3, 2), takes, odd, up_32 if odd else down_23, extra, t
        )
        got[step] = (trade_rows(rows, 2 if extra else 1), 2 if extra else 1)
        if step == 4:
            (t,) = advance(
                t,
                wall_t,
                (1, 0),
                [taken(2, 1, 0, 1, DOWN_RECV), taken(3, 1, 0, 1, UP_RECV)],
                True,
            )

    couple_s = [
        (0, table_at(3, DOWN_RECV), 2, 2 * UNIT, 0),
        (1, table_at(2, UP_RECV), 3, 2 * UNIT, 0),
        (1, table_at(2, DOWN_RECV), 1, 2 * UNIT, UNIT),
    ]
    couple_t = [
        (0, table_at(1, DOWN_RECV), 0, 2 * UNIT, UNIT),
        (0, table_at(1, UP_RECV), 3, 2 * UNIT, UNIT),
        (1, table_at(0, UP_RECV), 2, 2 * UNIT, UNIT),
    ]
    (packed,) = call(
        functools.partial(last_kernel, couple_s, couple_t),
        [(LEVELS * Q * WIDTH, DEPTH)],
        (tables, s, t, *(got[i][0] for i in (2, 5, 6, 7))),
        smem=1,
        scratch=[state, state],
    )
    packed = lax.all_to_all(
        packed.reshape(LEVELS, Q * WIDTH, DEPTH), "lvl", 0, 0, tiled=True
    ).reshape(-1, DEPTH)
    (final,) = call(output_kernel, [(Q * ROWS, DEPTH)], (packed,))
    final = jnp.transpose(final.reshape(Q, ROWS, DEPTH), (1, 0, 2))
    return final.reshape(1, PLANES, WIDTH, Q, DEPTH)


def solution(mesh):
    return jax.shard_map(
        on_device,
        mesh=mesh,
        in_specs=(
            P("lvl", "gx", None, None, None),
            P("lvl", "gx", None, None),
            P("lvl"),
            P("lvl", "gx", None, None),
            P("lvl", "gx", None, None),
            P("lvl", "gx", None, None),
            P("lvl", "gx", None, None),
        ),
        out_specs=P("lvl", "gx", None, None, None),
        check_vma=False,
    )
```

```python
import functools

import jax
import jax.numpy as jnp
from jax import lax
from jax.experimental import pallas as pl
from jax.experimental.pallas import tpu as pltpu
from jax.sharding import PartitionSpec as P

Q = 27
PLANES = 4
WIDTH = 32
ROWS = PLANES * WIDTH
DEPTH = 128
PEERS = 32
LEVELS = 4
HALF = 64
OWN = 32
GHOST = 16
PITCH = 136
QPAD = 32
STATE = QPAD * PITCH
UNIT = 24
NARROW = 16
GROUPS = 7
META = 8
WINDOW = 3 * GROUPS * HALF + META

VMEM = pl.BlockSpec(memory_space=pltpu.VMEM)
SMEM = pl.BlockSpec(memory_space=pltpu.SMEM)

DOWN_SEND, DOWN_RECV, UP_SEND, UP_RECV = range(4)


def table_at(level, which):
    return (level * 4 + which) * 2 * PEERS


def call(kernel, outs, ins, smem=0, scratch=(), aliases=None):
    moved = sum(value.size for value in ins) + sum(rows * depth for rows, depth in outs)
    return pl.pallas_call(
        kernel,
        out_shape=[jax.ShapeDtypeStruct(shape, jnp.float32) for shape in outs],
        in_specs=[SMEM] * smem + [VMEM] * (len(ins) - smem),
        out_specs=[VMEM] * len(outs),
        scratch_shapes=[pltpu.VMEM(shape, jnp.float32) for shape in scratch],
        input_output_aliases=aliases or {},
        cost_estimate=pl.CostEstimate(
            flops=10 * moved, bytes_accessed=4 * moved, transcendentals=0
        ),
        compiler_params=pltpu.CompilerParams(vmem_limit_bytes=24 * 1024 * 1024),
    )(*ins)


def lanes_of(shape):
    return lax.broadcasted_iota(jnp.int32, shape, 1)


def in_half(shape, half):
    lanes = lanes_of(shape)
    return lanes < HALF if half == 0 else lanes >= HALF


def turn(value, shift, axis):
    size = value.shape[axis]
    shift = shift % size
    return value if shift == 0 else pltpu.roll(value, shift, axis)


def gaps(shape):
    lanes = lanes_of(shape)
    return (lanes >= 56) & (lanes < 72), (lanes < 8) | (lanes >= 120)


def fold(t0, t1, t2, extra):
    inner, outer = gaps(t0.shape)
    e16, e48, e96 = (turn(extra, shift, 1) for shift in (16, 48, 96))
    return (
        jnp.where(inner, e48, jnp.where(outer, e96, t0)),
        jnp.where(inner, e16, jnp.where(outer, e48, t1)),
        jnp.where(inner, e96, jnp.where(outer, e16, t2)),
    )


def unfold(t0, t1, t2):
    inner, _ = gaps(t0.shape)
    e48 = turn(jnp.where(inner, t0, t1), -48, 1)
    e96 = turn(jnp.where(inner, t2, t0), -96, 1)
    e16 = turn(jnp.where(inner, t1, t2), -16, 1)
    spot = lanes_of(t0.shape) & (HALF - 1)
    return jnp.where(spot < 24, e48, jnp.where(spot < 40, e96, e16))


def fold_own(m0, m1, m2, m3):
    quarter = lanes_of(m0.shape) // OWN

    def join(a, b):
        return jnp.where(
            quarter < 2,
            jnp.where(quarter == 0, turn(a, -16, 1), turn(a, -48, 1)),
            jnp.where(quarter == 2, turn(b, 48, 1), turn(b, 16, 1)),
        )

    return join(m0, m1), join(m2, m3)


def unfold_own(t0, t1):
    left = in_half(t0.shape, 0)
    out = []
    for value in (t0, t1):
        out.append(jnp.where(left, turn(value, 16, 1), turn(value, 48, 1)))
        out.append(jnp.where(left, turn(value, -48, 1), turn(value, -16, 1)))
    return out


def collide(f, wall, rate):
    t, d = [], []
    for pair in range(9):
        low, mid, high = f[3 * pair : 3 * pair + 3]
        t.append(low + high + 4.0 * mid)
        d.append(high - low)
    total, along_y, along_z = [], [], []
    for a in range(3):
        total.append(t[3 * a] + t[3 * a + 2] + 4.0 * t[3 * a + 1])
        along_y.append(t[3 * a + 2] - t[3 * a])
        along_z.append(d[3 * a] + d[3 * a + 2] + 4.0 * d[3 * a + 1])
    mass = total[0] + total[2] + 4.0 * total[1]
    inverse = 3.0 / mass
    ux = (total[2] - total[0]) * inverse
    uy = (along_y[0] + along_y[2] + 4.0 * along_y[1]) * inverse
    uz = (along_z[0] + along_z[2] + 4.0 * along_z[1]) * inverse
    scaled = rate * mass * (1.0 / 216.0)
    half = 0.5 * scaled
    base = scaled - scaled * ((ux * ux + uy * uy + uz * uz) * (1.0 / 6.0))
    keep = 1.0 - rate
    sums = {
        (0, 0, 1): uz,
        (0, 1, 0): uy,
        (1, 0, 0): ux,
        (0, 1, -1): uy - uz,
        (0, 1, 1): uy + uz,
        (1, 0, -1): ux - uz,
        (1, 0, 1): ux + uz,
        (1, -1, 0): ux - uy,
        (1, 1, 0): ux + uy,
    }
    for b in (-1, 1):
        for e in (-1, 1):
            sums[(1, b, e)] = sums[(1, b, 0)] + uz if e == 1 else sums[(1, b, 0)] - uz
    out = [None] * Q
    out[13] = jnp.where(wall, f[13], keep * f[13] + base)
    for (a, b, e), along in sums.items():
        i = 9 * (a + 1) + 3 * (b + 1) + (e + 1)
        j = 26 - i
        part = half * along
        odd = part + part
        even = base + part * along
        out[i] = jnp.where(wall, f[j], keep * f[i] + (even + odd))
        out[j] = jnp.where(wall, f[i], keep * f[j] + (even - odd))
    return out


def collide_rows(load, wall_ref, rate, store, tiles):
    def tile(i, carry):
        row = pl.multiple_of(tiles(i) * 8, 8)
        wall = wall_ref[pl.ds(row, 8), :] > 0.5
        out = collide([load(q, row) for q in range(Q)], wall, rate)
        for q in range(Q):
            store(q, row, turn(out[q], q % 3 - 1, 1))
        return carry

    lax.fori_loop(0, ROWS // 16, tile, 0, unroll=2)


def edge_tiles(i):
    return jnp.where(i < 4, i, i + 8)


def inner_tiles(i):
    return i + 4


def collide_edges(load, wall_ref, rate, edge_ref, low_ref, high_ref):
    def store(q, row, value):
        at = jnp.where(row < WIDTH, row, row - 2 * WIDTH)
        edge_ref[pl.ds(pl.multiple_of(q * HALF + at, 8), 8), :] = value

    collide_rows(load, wall_ref, rate, store, edge_tiles)
    for q in range(9):
        spot = pl.ds(q * WIDTH, WIDTH)
        low_ref[spot, :] = edge_ref[pl.ds(q * HALF, WIDTH), :]
        high_ref[spot, :] = edge_ref[pl.ds((q + 18) * HALF + WIDTH, WIDTH), :]


def collide_inside(load, wall_ref, rate, inside_ref):
    def store(q, row, value):
        inside_ref[pl.ds(pl.multiple_of(q * HALF + row - WIDTH, 8), 8), :] = value

    collide_rows(load, wall_ref, rate, store, inner_tiles)


def stream_known(edge_ref, inside_ref, read_ref, pitch, old_ref):
    for q in range(Q):
        for plane in range(PLANES):
            source = plane - (q // 9 - 1)
            spot = pl.ds(q * pitch + plane * WIDTH, WIDTH)
            if 0 <= source < PLANES:
                if source in (0, PLANES - 1):
                    value = edge_ref[pl.ds(q * HALF + (WIDTH if source else 0), WIDTH), :]
                else:
                    value = inside_ref[pl.ds(q * HALF + (source - 1) * WIDTH, WIDTH), :]
                value = turn(value, q // 3 % 3 - 1, 0)
                if old_ref is not None:
                    value = jnp.where(in_half((WIDTH, DEPTH), 0), value, old_ref[spot, :])
                read_ref[spot, :] = value
            elif old_ref is not None:
                read_ref[spot, :] = old_ref[spot, :]


def stream_rest(front_ref, behind_ref, read_ref, pitch, keep, start=0):
    for q in range(9):
        for velocity, plane, ref in ((q, PLANES - 1, front_ref), (q + 18, 0, behind_ref)):
            spot = pl.ds(velocity * pitch + plane * WIDTH, WIDTH)
            value = turn(ref[pl.ds(start + q * WIDTH, WIDTH), :], q // 3 - 1, 0)
            if keep:
                value = jnp.where(in_half((WIDTH, DEPTH), 0), value, read_ref[spot, :])
            read_ref[spot, :] = value


def pick_rows(state_ref, half, tables_ref, at, out_ref, unit, offset, narrow=False):
    group = 16

    def some(g, carry):
        for j in range(group):
            peer = g * group + j
            first = jnp.maximum(tables_ref[at + 2 * peer], 0)
            second = jnp.maximum(tables_ref[at + 2 * peer + 1], 0)
            merged = []
            for c in range(QPAD // 8):
                one = state_ref[pl.ds(first + c * 8 * PITCH, 8, stride=PITCH), :]
                two = state_ref[pl.ds(second + c * 8 * PITCH, 8, stride=PITCH), :]
                if half == 0:
                    two = turn(two, HALF, 1)
                else:
                    one = turn(one, HALF, 1)
                merged.append(jnp.where(in_half((8, DEPTH), 0), one, two))
            for c, value in enumerate((fold_own if narrow else fold)(*merged)):
                spot = pl.multiple_of(peer * unit + offset + 8 * c, 8)
                out_ref[pl.ds(spot, 8), :] = value
        return carry

    lax.fori_loop(0, PEERS // group, some, 0)


def place_rows(state_ref, half, tables_ref, at, in_ref, unit, offset, narrow=False):
    group = 16

    def some(g, carry):
        stores = []
        for j in range(group):
            peer = g * group + j
            parts = [
                in_ref[pl.ds(pl.multiple_of(peer * unit + offset + 8 * c, 8), 8), :]
                for c in range(2 if narrow else 3)
            ]
            parts = unfold_own(*parts) if narrow else parts + [unfold(*parts)]
            for k in range(2):
                row = tables_ref[at + 2 * peer + k]
                row = jnp.where(row < 0, ROWS, row)
                for c, value in enumerate(parts):
                    if k != half:
                        value = turn(value, HALF, 1)
                    where = pl.ds(row + c * 8 * PITCH, 8, stride=PITCH)
                    stores.append(
                        (where, jnp.where(in_half((8, DEPTH), half), value, state_ref[where, :]))
                    )
        for where, value in stores:
            state_ref[where, :] = value
        return carry

    lax.fori_loop(0, PEERS // group, some, 0)


def copy_state(source_ref, target_ref):
    def one(q, carry):
        at = pl.multiple_of(q * PITCH, 8)
        target_ref[pl.ds(at, ROWS), :] = source_ref[pl.ds(at, ROWS), :]
        return carry

    lax.fori_loop(0, Q, one, 0)


def pair_rate(rates_ref, first, second):
    return jnp.where(in_half((8, DEPTH), 0), rates_ref[first], rates_ref[second])


def first_edges_kernel(rate_ref, x_ref, wall_ref, edge_ref, low_ref, high_ref):
    rate = jnp.full((8, DEPTH), rate_ref[0], jnp.float32)

    def load(q, row):
        return x_ref[pl.ds(q * ROWS + row, 8), :]

    collide_edges(load, wall_ref, rate, edge_ref, low_ref, high_ref)


def first_inside_kernel(rate_ref, x_ref, wall_ref, edge_ref, read_ref, inside_ref):
    rate = jnp.full((8, DEPTH), rate_ref[0], jnp.float32)

    def load(q, row):
        return x_ref[pl.ds(q * ROWS + row, 8), :]

    collide_inside(load, wall_ref, rate, inside_ref)
    stream_known(edge_ref, inside_ref, read_ref, ROWS, None)


def windows_kernel(seen_ref, front_ref, behind_ref, wall_ref, meta_ref, out_ref, read_ref):
    read_ref[pl.ds(0, Q * ROWS), :] = seen_ref[...]
    stream_rest(front_ref, behind_ref, read_ref, ROWS, False)
    read_ref[pl.ds(Q * ROWS, ROWS), :] = wall_ref[...]

    def some(i, carry):
        g, row = i // 8, pl.multiple_of(i % 8 * 8, 8)
        tops, bottoms = [], []
        for j in range(4):
            at = pl.multiple_of((4 * g + j) * ROWS + row, 8)
            tops.append(read_ref[pl.ds(at, 8), :])
            bottoms.append(read_ref[pl.ds(at + HALF, 8), :])
        for target in range(LEVELS):
            shift = GHOST - OWN * target
            pairs = [
                jnp.where(
                    in_half((8, DEPTH), 0), turn(top, shift, 1), turn(bottom, shift + HALF, 1)
                )
                for top, bottom in zip(tops, bottoms)
            ]
            for j, value in enumerate(fold(*pairs)):
                at = pl.multiple_of(target * WINDOW + (3 * g + j) * HALF + row, 8)
                out_ref[pl.ds(at, 8), :] = value
        return carry

    lax.fori_loop(0, GROUPS * 8, some, 0, unroll=2)
    for target in range(LEVELS):
        out_ref[pl.ds((target + 1) * WINDOW - META, META), :] = meta_ref[...]


def unpack_kernel(
    tables_ref, rates_ref, in_ref, s_ref, t_ref, wall_s_ref, wall_t_ref, rows_ref
):
    def some(i, carry):
        g, row = i // 8, pl.multiple_of(i % 8 * 8, 8)
        left = in_half((8, DEPTH), 0)
        for ref, first, second in ((s_ref, 3, 2), (t_ref, 1, 0)):
            parts = []
            for level in (first, second):
                at = pl.multiple_of(level * WINDOW + 3 * g * HALF + row, 8)
                three = [in_ref[pl.ds(at + j * HALF, 8), :] for j in range(3)]
                parts.append(three + [unfold(*three)])
            for j in range(4):
                one, two = parts[0][j], parts[1][j]
                at = pl.multiple_of((4 * g + j) * PITCH + row, 8)
                ref[pl.ds(at, 8), :] = jnp.where(left, one, turn(two, HALF, 1))
                ref[pl.ds(at + HALF, 8), :] = jnp.where(left, turn(one, HALF, 1), two)
        return carry

    lax.fori_loop(0, GROUPS * 8, some, 0, unroll=2)
    wall_s_ref[...] = s_ref[pl.ds(Q * PITCH, ROWS), :]
    wall_t_ref[...] = t_ref[pl.ds(Q * PITCH, ROWS), :]
    pick_rows(s_ref, 1, tables_ref, table_at(2, DOWN_SEND), rows_ref, UNIT, 0)


def apply(state_ref, couplings, tables_ref, buffers):
    for half, at, index, unit, offset, narrow in couplings:
        place_rows(state_ref, half, tables_ref, at, buffers[index], unit, offset, narrow)


def edges_kernel(levels, couplings, buffers, carried, tables_ref, rates_ref, *refs):
    refs = list(refs)
    state_ref, wall_ref = refs.pop(0), refs.pop(0)
    in_refs = [refs.pop(0) for _ in range(buffers)]
    other_refs = [refs.pop(0) for _ in range(2)] if carried else []
    work_ref, edge_ref, low_ref, high_ref = refs
    copy_state(state_ref, work_ref)
    apply(work_ref, couplings, tables_ref, in_refs)

    def load(q, row):
        return work_ref[pl.ds(q * PITCH + row, 8), :]

    rate = pair_rate(rates_ref, *levels)
    collide_edges(load, wall_ref, rate, edge_ref, low_ref, high_ref)
    for source, target in zip(other_refs, (low_ref, high_ref)):
        target[pl.ds(9 * WIDTH, 9 * WIDTH), :] = source[...]


def inside_kernel(levels, keep, extra, tables_ref, rates_ref, *refs):
    refs = list(refs)
    work_ref, wall_ref, edge_ref = refs.pop(0), refs.pop(0), refs.pop(0)
    old_ref = refs.pop(0) if keep else None
    other_ref = refs.pop(0) if extra and not extra[0] else None
    inside_ref = refs.pop()
    read_ref = refs.pop(0)

    def load(q, row):
        return work_ref[pl.ds(q * PITCH + row, 8), :]

    collide_inside(load, wall_ref, pair_rate(rates_ref, *levels), inside_ref)
    stream_known(edge_ref, inside_ref, read_ref, PITCH, old_ref)
    if extra:
        own, half, at = extra
        source = old_ref if own else other_ref
        pick_rows(source, half, tables_ref, at, refs.pop(0), 2 * UNIT, UNIT)


def rest_kernel(keep, picks, unit, carried, ready, tables_ref, front_ref, behind_ref, *refs):
    refs = list(refs)[1 + carried + ready :]
    seen_ref, rows_ref = refs[:2]
    stream_rest(front_ref, behind_ref, seen_ref, PITCH, keep)
    if carried:
        stream_rest(front_ref, behind_ref, refs[2], PITCH, True, 9 * WIDTH)
    for other, half, at, offset, narrow in picks:
        source = refs[2] if other else seen_ref
        pick_rows(source, half, tables_ref, at, rows_ref, unit, offset, narrow)


def pack_level(work_ref, half, level, out_ref):
    def one(q, carry):
        chunk = lanes_of((8, DEPTH)) // OWN
        for row in range(0, WIDTH, 8):
            packed = None
            for plane in range(PLANES):
                at = pl.multiple_of(q * PITCH + plane * WIDTH + row, 8)
                value = turn(work_ref[pl.ds(at, 8), :], OWN * plane - HALF * half - GHOST, 1)
                packed = value if packed is None else jnp.where(chunk == plane, value, packed)
            out_ref[pl.ds(pl.multiple_of((level * Q + q) * WIDTH + row, 8), 8), :] = packed
        return carry

    lax.fori_loop(0, Q, one, 0, unroll=3)


def other_last_kernel(couplings, tables_ref, state_ref, b2, b5, b6, out_ref, work_ref):
    copy_state(state_ref, work_ref)
    apply(work_ref, couplings, tables_ref, (b2, b5, b6))
    pack_level(work_ref, 1, 0, out_ref)
    pack_level(work_ref, 0, 1, out_ref)


def last_kernel(couplings, tables_ref, state_ref, b5, b6, b7, half_ref, out_ref, work_ref):
    copy_state(state_ref, work_ref)
    apply(work_ref, couplings, tables_ref, (b5, b6, b7))
    pack_level(work_ref, 1, 2, out_ref)
    pack_level(work_ref, 0, 3, out_ref)


def output_kernel(in_ref, out_ref):
    chunk = lanes_of((WIDTH, DEPTH)) // OWN

    def one(q, carry):
        parts = [
            in_ref[pl.ds(pl.multiple_of((c * Q + q) * WIDTH, 8), WIDTH), :] for c in range(LEVELS)
        ]
        for plane in range(PLANES):
            whole = None
            for c in range(LEVELS):
                value = turn(parts[c], OWN * (c - plane), 1)
                whole = value if whole is None else jnp.where(chunk == c, value, whole)
            out_ref[pl.ds(pl.multiple_of(q * ROWS + plane * WIDTH, 8), WIDTH), :] = whole
        return carry

    lax.fori_loop(0, Q, one, 0)


def trade_planes(low, high):
    count = lax.axis_size("gx")
    forward = [(i, (i + 1) % count) for i in range(count)]
    backward = [(target, source) for source, target in forward]
    return lax.ppermute(low, "gx", backward), lax.ppermute(high, "gx", forward)


def trade_rows(rows):
    blocks = rows.reshape(PEERS, -1, DEPTH)
    return lax.all_to_all(blocks, "gx", split_axis=0, concat_axis=0, tiled=True).reshape(
        rows.shape
    )


def on_device(populations, solid_mask, relax_rates, down_send, down_recv, up_send, up_recv):
    meta = jnp.concatenate(
        [value.reshape(-1) for value in (down_send, down_recv, up_send, up_recv)]
    ).astype(jnp.float32)
    meta = jnp.concatenate([meta, jnp.broadcast_to(relax_rates, (META * DEPTH - meta.size,))])
    meta = meta.reshape(META, DEPTH)
    x = jnp.transpose(populations.reshape(ROWS, Q, DEPTH), (1, 0, 2)).reshape(Q * ROWS, DEPTH)
    wall = solid_mask.reshape(ROWS, DEPTH).astype(jnp.float32)
    flow = [(Q * ROWS, DEPTH), (9 * WIDTH, DEPTH), (9 * WIDTH, DEPTH)]
    state = (STATE, DEPTH)

    edge, low, high = call(
        first_edges_kernel, [(Q * HALF, DEPTH), *flow[1:]], (relax_rates, x, wall), smem=1
    )
    front, behind = trade_planes(low, high)
    (seen,) = call(
        first_inside_kernel,
        [flow[0]],
        (relax_rates, x, wall, edge),
        smem=1,
        scratch=[(Q * HALF, DEPTH)],
    )
    (windows,) = call(
        windows_kernel,
        [(LEVELS * WINDOW, DEPTH)],
        (seen, front, behind, wall, meta),
        scratch=[((Q + 1) * ROWS, DEPTH)],
    )
    windows = lax.all_to_all(
        windows.reshape(LEVELS, WINDOW, DEPTH), "lvl", 0, 0, tiled=True
    )
    tables = windows[:, WINDOW - META : WINDOW - META + 2, :].astype(jnp.int32).reshape(-1)
    rates = windows[:, WINDOW - 1, 0]
    windows = windows.reshape(-1, DEPTH)
    s, t, wall_s, wall_t, rows = call(
        unpack_kernel,
        [state, state, (ROWS, DEPTH), (ROWS, DEPTH), (PEERS * UNIT, DEPTH)],
        (tables, rates, windows),
        smem=2,
    )
    got = {0: trade_rows(rows)}

    def taken(step, offset, half, level, which, narrow=False):
        buffer = got[step]
        return buffer, half, table_at(level, which), buffer.shape[0] // PEERS, offset, narrow

    def edges(value, walls, levels, takes, carried=()):
        buffers, couplings = [], []
        for buffer, half, at, unit, offset, narrow in takes:
            index = next((i for i, b in enumerate(buffers) if b is buffer), len(buffers))
            if index == len(buffers):
                buffers.append(buffer)
            couplings.append((half, at, index, unit, offset, narrow))
        planes = (9 * WIDTH * (2 if carried else 1), DEPTH)
        return call(
            functools.partial(edges_kernel, levels, couplings, len(buffers), bool(carried)),
            [state, (Q * HALF, DEPTH), planes, planes],
            (tables, rates, value, walls, *buffers, *carried),
            smem=2,
        )

    def inside(work, walls, edge, levels, old=None, extra=None, other=None):
        ins = [tables, rates, work, walls, edge]
        ins += [old] if old is not None else []
        ins += [other] if extra and not extra[0] else []
        return call(
            functools.partial(inside_kernel, levels, old is not None, extra),
            [state] + ([(PEERS * 2 * UNIT, DEPTH)] if extra else []),
            ins,
            smem=2,
            scratch=[(Q * HALF, DEPTH)],
        )

    down_23 = (False, 1, table_at(2, DOWN_SEND), 0, False)
    up_32 = (False, 0, table_at(3, UP_SEND), 0, False)
    extras = {
        1: (False, 0, table_at(1, DOWN_SEND)),
        2: (False, 1, table_at(0, DOWN_SEND)),
        3: (True, 1, table_at(2, UP_SEND)),
    }
    picks = {
        1: [up_32],
        2: [down_23],
        3: [up_32],
        4: [down_23],
        5: [
            up_32,
            (True, 0, table_at(1, DOWN_SEND), UNIT, False),
            (True, 0, table_at(1, UP_SEND), 2 * UNIT, True),
        ],
        6: [down_23, (False, 1, table_at(2, UP_SEND), UNIT, True)],
        7: [(False, 0, table_at(3, UP_SEND), 0, True)],
    }
    units = {1: 48, 2: 48, 3: 48, 4: 24, 5: 64, 6: 40, 7: 16}
    for step in range(1, 8):
        odd = step % 2 == 1
        if odd:
            takes = [taken(step - 1, 0, 0, 3, DOWN_RECV)]
        else:
            takes = [
                taken(step - 2, 0, 0, 3, DOWN_RECV),
                taken(step - 1, 0, 1, 2, UP_RECV),
                taken(1 if step < 6 else 5, UNIT, 1, 2, DOWN_RECV),
            ]
        carried = step == 5
        work, edge, low, high = edges(
            s, wall_s, (3, 2), takes, (t_low, t_high) if carried else ()
        )
        front, behind = trade_planes(low, high)
        extra = extras.get(step)
        seen, *rows = inside(work, wall_s, edge, (3, 2), s if odd else None, extra, t)
        if step == 4:
            takes = [taken(2, UNIT, 0, 1, DOWN_RECV), taken(3, UNIT, 0, 1, UP_RECV)]
            t_work, t_edge, t_low, t_high = edges(t, wall_t, (1, 0), takes)
            seen, t_work, t_edge, t_low, t_high = lax.optimization_barrier(
                (seen, t_work, t_edge, t_low, t_high)
            )
        if step == 5:
            (t,) = inside(t_work, wall_t, t_edge, (1, 0), t)
        if step == 7:
            couplings = [
                (0, table_at(1, DOWN_RECV), 0, units[2], UNIT, False),
                (1, table_at(0, UP_RECV), 1, units[5], 2 * UNIT, True),
                (0, table_at(1, UP_RECV), 2, units[6], UNIT, True),
            ]
            (packed,) = call(
                functools.partial(other_last_kernel, couplings),
                [(LEVELS * Q * WIDTH, DEPTH)],
                (tables, t, got[2], got[5], got[6]),
                smem=1,
                scratch=[state],
            )
            seen, packed = lax.optimization_barrier((seen, packed))
        unit = units[step]
        aliases = {3: 0}
        if extra:
            aliases[4] = 1
        if carried:
            aliases[4] = 2
        s, got[step], *rest = call(
            functools.partial(rest_kernel, odd, picks[step], unit, carried, bool(extra)),
            [state, (PEERS * unit, DEPTH)] + ([state] if carried else []),
            (tables, front, behind, seen, *rows, *([t] if carried else [])),
            smem=1,
            aliases=aliases,
        )
        if carried:
            (t,) = rest
        got[step] = trade_rows(got[step])

    couplings = [
        (0, table_at(3, DOWN_RECV), 1, units[6], 0, False),
        (1, table_at(2, UP_RECV), 2, units[7], 0, True),
        (1, table_at(2, DOWN_RECV), 0, units[5], UNIT, False),
    ]
    (packed,) = call(
        functools.partial(last_kernel, couplings),
        [(LEVELS * Q * WIDTH, DEPTH)],
        (tables, s, got[5], got[6], got[7], packed),
        smem=1,
        scratch=[state],
        aliases={5: 0},
    )
    packed = lax.all_to_all(
        packed.reshape(LEVELS, Q * WIDTH, DEPTH), "lvl", 0, 0, tiled=True
    ).reshape(-1, DEPTH)
    (final,) = call(output_kernel, [(Q * ROWS, DEPTH)], (packed,))
    final = jnp.transpose(final.reshape(Q, ROWS, DEPTH), (1, 0, 2))
    return final.reshape(1, PLANES, WIDTH, Q, DEPTH)


def solution(mesh):
    return jax.shard_map(
        on_device,
        mesh=mesh,
        in_specs=(
            P("lvl", "gx", None, None, None),
            P("lvl", "gx", None, None),
            P("lvl"),
            P("lvl", "gx", None, None),
            P("lvl", "gx", None, None),
            P("lvl", "gx", None, None),
            P("lvl", "gx", None, None),
        ),
        out_specs=P("lvl", "gx", None, None, None),
        check_vma=False,
    )
```

```python
import functools

import jax
import jax.numpy as jnp
from jax import lax
from jax.experimental import pallas as pl
from jax.experimental.pallas import tpu as pltpu
from jax.sharding import PartitionSpec as P

Q = 27
PLANES = 4
WIDTH = 32
ROWS = PLANES * WIDTH
DEPTH = 128
PEERS = 32
LEVELS = 4
HALF = 64
OWN = 32
GHOST = 16
PITCH = 136
QPAD = 32
STATE = QPAD * PITCH
UNIT = 24
NARROW = 16
GROUPS = 7
META = 8
WINDOW = 3 * GROUPS * HALF + META

VMEM = pl.BlockSpec(memory_space=pltpu.VMEM)
SMEM = pl.BlockSpec(memory_space=pltpu.SMEM)

DOWN_SEND, DOWN_RECV, UP_SEND, UP_RECV = range(4)
ME = LEVELS * 4 * 2 * PEERS


def table_at(level, which):
    return (level * 4 + which) * 2 * PEERS


def call(kernel, outs, ins, smem=0, scratch=(), aliases=None):
    moved = sum(value.size for value in ins) + sum(rows * depth for rows, depth in outs)
    return pl.pallas_call(
        kernel,
        out_shape=[jax.ShapeDtypeStruct(shape, jnp.float32) for shape in outs],
        in_specs=[SMEM] * smem + [VMEM] * (len(ins) - smem),
        out_specs=[VMEM] * len(outs),
        scratch_shapes=[pltpu.VMEM(shape, jnp.float32) for shape in scratch],
        input_output_aliases=aliases or {},
        cost_estimate=pl.CostEstimate(
            flops=10 * moved, bytes_accessed=4 * moved, transcendentals=0
        ),
        compiler_params=pltpu.CompilerParams(vmem_limit_bytes=14 * 1024 * 1024),
    )(*ins)


def lanes_of(shape):
    return lax.broadcasted_iota(jnp.int32, shape, 1)


def in_half(shape, half):
    lanes = lanes_of(shape)
    return lanes < HALF if half == 0 else lanes >= HALF


def turn(value, shift, axis):
    size = value.shape[axis]
    shift = shift % size
    return value if shift == 0 else pltpu.roll(value, shift, axis)


def gaps(shape):
    lanes = lanes_of(shape)
    return (lanes >= 56) & (lanes < 72), (lanes < 8) | (lanes >= 120)


def fold(t0, t1, t2, extra):
    return fold_turned(t0, t1, t2, *(turn(extra, shift, 1) for shift in (16, 48, 96)))


def fold_turned(t0, t1, t2, e16, e48, e96):
    inner, outer = gaps(t0.shape)
    return (
        jnp.where(inner, e48, jnp.where(outer, e96, t0)),
        jnp.where(inner, e16, jnp.where(outer, e48, t1)),
        jnp.where(inner, e96, jnp.where(outer, e16, t2)),
    )


def unfold(t0, t1, t2):
    inner, _ = gaps(t0.shape)
    e48 = turn(jnp.where(inner, t0, t1), -48, 1)
    e96 = turn(jnp.where(inner, t2, t0), -96, 1)
    e16 = turn(jnp.where(inner, t1, t2), -16, 1)
    spot = lanes_of(t0.shape) & (HALF - 1)
    return jnp.where(spot < 24, e48, jnp.where(spot < 40, e96, e16))


def fold_own(m0, m1, m2, m3):
    quarter = lanes_of(m0.shape) // OWN

    def join(a, b):
        return jnp.where(
            quarter < 2,
            jnp.where(quarter == 0, turn(a, -16, 1), turn(a, -48, 1)),
            jnp.where(quarter == 2, turn(b, 48, 1), turn(b, 16, 1)),
        )

    return join(m0, m1), join(m2, m3)


def unfold_own(t0, t1):
    left = in_half(t0.shape, 0)
    out = []
    for value in (t0, t1):
        out.append(jnp.where(left, turn(value, 16, 1), turn(value, 48, 1)))
        out.append(jnp.where(left, turn(value, -48, 1), turn(value, -16, 1)))
    return out


def collide(f, wall, rate):
    t, d = [], []
    for pair in range(9):
        low, mid, high = f[3 * pair : 3 * pair + 3]
        t.append(low + high + 4.0 * mid)
        d.append(high - low)
    total, along_y, along_z = [], [], []
    for a in range(3):
        total.append(t[3 * a] + t[3 * a + 2] + 4.0 * t[3 * a + 1])
        along_y.append(t[3 * a + 2] - t[3 * a])
        along_z.append(d[3 * a] + d[3 * a + 2] + 4.0 * d[3 * a + 1])
    mass = total[0] + total[2] + 4.0 * total[1]
    inverse = 3.0 / mass
    ux = (total[2] - total[0]) * inverse
    uy = (along_y[0] + along_y[2] + 4.0 * along_y[1]) * inverse
    uz = (along_z[0] + along_z[2] + 4.0 * along_z[1]) * inverse
    scaled = rate * mass * (1.0 / 216.0)
    half = 0.5 * scaled
    base = scaled - scaled * ((ux * ux + uy * uy + uz * uz) * (1.0 / 6.0))
    keep = 1.0 - rate
    sums = {
        (0, 0, 1): uz,
        (0, 1, 0): uy,
        (1, 0, 0): ux,
        (0, 1, -1): uy - uz,
        (0, 1, 1): uy + uz,
        (1, 0, -1): ux - uz,
        (1, 0, 1): ux + uz,
        (1, -1, 0): ux - uy,
        (1, 1, 0): ux + uy,
    }
    for b in (-1, 1):
        for e in (-1, 1):
            sums[(1, b, e)] = sums[(1, b, 0)] + uz if e == 1 else sums[(1, b, 0)] - uz
    out = [None] * Q
    out[13] = jnp.where(wall, f[13], keep * f[13] + base)
    for (a, b, e), along in sums.items():
        i = 9 * (a + 1) + 3 * (b + 1) + (e + 1)
        j = 26 - i
        part = half * along
        odd = part + part
        even = base + part * along
        out[i] = jnp.where(wall, f[j], keep * f[i] + (even + odd))
        out[j] = jnp.where(wall, f[i], keep * f[j] + (even - odd))
    return out


def collide_rows(load, wall_ref, rate, store, tiles):
    def tile(i, carry):
        row = pl.multiple_of(tiles(i) * 8, 8)
        wall = wall_ref[pl.ds(row, 8), :] > 0.5
        out = collide([load(q, row) for q in range(Q)], wall, rate)
        for q in range(Q):
            store(q, row, turn(out[q], q % 3 - 1, 1))
        return carry

    lax.fori_loop(0, ROWS // 16, tile, 0, unroll=4)


def edge_tiles(i):
    return jnp.where(i < 4, i, i + 8)


def inner_tiles(i):
    return i + 4


def collide_edges(load, wall_ref, rate, edge_ref, low_ref, high_ref):
    def store(q, row, value):
        at = jnp.where(row < WIDTH, row, row - 2 * WIDTH)
        edge_ref[pl.ds(pl.multiple_of(q * HALF + at, 8), 8), :] = value

    collide_rows(load, wall_ref, rate, store, edge_tiles)
    for q in range(9):
        spot = pl.ds(q * WIDTH, WIDTH)
        low_ref[spot, :] = edge_ref[pl.ds(q * HALF, WIDTH), :]
        high_ref[spot, :] = edge_ref[pl.ds((q + 18) * HALF + WIDTH, WIDTH), :]


def collide_inside(load, wall_ref, rate, inside_ref):
    def store(q, row, value):
        inside_ref[pl.ds(pl.multiple_of(q * HALF + row - WIDTH, 8), 8), :] = value

    collide_rows(load, wall_ref, rate, store, inner_tiles)


def stream_known(edge_ref, inside_ref, read_ref, pitch, old_ref, next_ref=None):
    for q in range(Q):
        for plane in range(PLANES):
            source = plane - (q // 9 - 1)
            spot = pl.ds(q * pitch + plane * WIDTH, WIDTH)
            if 0 <= source < PLANES:
                if source in (0, PLANES - 1):
                    value = edge_ref[pl.ds(q * HALF + (WIDTH if source else 0), WIDTH), :]
                else:
                    value = inside_ref[pl.ds(q * HALF + (source - 1) * WIDTH, WIDTH), :]
                value = turn(value, q // 3 % 3 - 1, 0)
                if old_ref is not None:
                    value = jnp.where(in_half((WIDTH, DEPTH), 0), value, old_ref[spot, :])
            elif old_ref is not None:
                value = old_ref[spot, :]
            else:
                continue
            read_ref[spot, :] = value
            if next_ref is not None:
                next_ref[spot, :] = value


def stream_rest(
    front_ref, behind_ref, read_ref, pitch, keep, start=0, next_ref=None, taken_ref=None
):
    for q in range(9):
        for velocity, plane, ref in ((q, PLANES - 1, front_ref), (q + 18, 0, behind_ref)):
            spot = pl.ds(velocity * pitch + plane * WIDTH, WIDTH)
            value = turn(ref[pl.ds(start + q * WIDTH, WIDTH), :], q // 3 - 1, 0)
            if keep:
                value = jnp.where(in_half((WIDTH, DEPTH), 0), value, read_ref[spot, :])
            read_ref[spot, :] = value
            if next_ref is not None:
                placed = taken_ref[pl.ds(plane * WIDTH, WIDTH), :] > 0.5
                free = in_half((WIDTH, DEPTH), 0) & jnp.logical_not(placed)
                next_ref[spot, :] = jnp.where(free, value, next_ref[spot, :])


def pick_rows(state_ref, half, tables_ref, at, out_ref, unit, offset, narrow=False):
    group = 16

    def some(g, carry):
        for j in range(group):
            peer = g * group + j
            first = jnp.maximum(tables_ref[at + 2 * peer], 0)
            second = jnp.maximum(tables_ref[at + 2 * peer + 1], 0)
            merged = []
            for c in range(QPAD // 8):
                one = state_ref[pl.ds(first + c * 8 * PITCH, 8, stride=PITCH), :]
                two = state_ref[pl.ds(second + c * 8 * PITCH, 8, stride=PITCH), :]
                if half == 0:
                    two = turn(two, HALF, 1)
                else:
                    one = turn(one, HALF, 1)
                merged.append(jnp.where(in_half((8, DEPTH), 0), one, two))
            for c, value in enumerate((fold_own if narrow else fold)(*merged)):
                spot = pl.multiple_of(peer * unit + offset + 8 * c, 8)
                out_ref[pl.ds(spot, 8), :] = value
        return carry

    lax.fori_loop(0, PEERS // group, some, 0)


def place_rows(state_ref, half, tables_ref, at, in_ref, unit, offset, narrow=False):
    group = 16

    def some(g, carry):
        stores = []
        for j in range(group):
            peer = g * group + j
            parts = [
                in_ref[pl.ds(pl.multiple_of(peer * unit + offset + 8 * c, 8), 8), :]
                for c in range(2 if narrow else 3)
            ]
            parts = unfold_own(*parts) if narrow else parts + [unfold(*parts)]
            for k in range(2):
                row = tables_ref[at + 2 * peer + k]
                row = jnp.where(row < 0, ROWS, row)
                for c, value in enumerate(parts):
                    if k != half:
                        value = turn(value, HALF, 1)
                    where = pl.ds(row + c * 8 * PITCH, 8, stride=PITCH)
                    stores.append(
                        (where, jnp.where(in_half((8, DEPTH), half), value, state_ref[where, :]))
                    )
        for where, value in stores:
            state_ref[where, :] = value
        return carry

    lax.fori_loop(0, PEERS // group, some, 0)


def copy_state(source_ref, target_ref):
    def one(q, carry):
        at = pl.multiple_of(q * PITCH, 8)
        target_ref[pl.ds(at, ROWS), :] = source_ref[pl.ds(at, ROWS), :]
        return carry

    lax.fori_loop(0, Q, one, 0)


def pair_rate(rates_ref, first, second):
    return jnp.where(in_half((8, DEPTH), 0), rates_ref[first], rates_ref[second])


def first_edges_kernel(rate_ref, x_ref, wall_ref, edge_ref, low_ref, high_ref):
    rate = jnp.full((8, DEPTH), rate_ref[0], jnp.float32)

    def load(q, row):
        return x_ref[pl.ds(q * ROWS + row, 8), :]

    collide_edges(load, wall_ref, rate, edge_ref, low_ref, high_ref)


def first_inside_kernel(rate_ref, x_ref, wall_ref, edge_ref, read_ref, inside_ref):
    rate = jnp.full((8, DEPTH), rate_ref[0], jnp.float32)

    def load(q, row):
        return x_ref[pl.ds(q * ROWS + row, 8), :]

    collide_inside(load, wall_ref, rate, inside_ref)
    stream_known(edge_ref, inside_ref, read_ref, ROWS, None)


def windows_kernel(seen_ref, front_ref, behind_ref, wall_ref, meta_ref, out_ref, read_ref):
    read_ref[pl.ds(0, Q * ROWS), :] = seen_ref[...]
    stream_rest(front_ref, behind_ref, read_ref, ROWS, False)
    read_ref[pl.ds(Q * ROWS, ROWS), :] = wall_ref[...]

    def some(g, carry):
        lanes = lanes_of((8, DEPTH))
        for row in range(0, HALF, 8):
            mixed = []
            for j in range(4):
                at = pl.multiple_of((4 * g + j) * ROWS + row, 8)
                top = read_ref[pl.ds(at, 8), :]
                bottom = turn(read_ref[pl.ds(at + HALF, 8), :], HALF, 1)
                mixed.append(
                    [
                        jnp.where(((lanes + GHOST - OWN * k) & (DEPTH - 1)) < HALF, top, bottom)
                        for k in range(LEVELS)
                    ]
                )
            for target in range(LEVELS):
                shift = GHOST - OWN * target
                main = [turn(mixed[j][target], shift, 1) for j in range(3)]
                extra = [turn(mixed[3][target], shift + by, 1) for by in (16, 48, 96)]
                for j, value in enumerate(fold_turned(*main, *extra)):
                    at = pl.multiple_of(target * WINDOW + (3 * g + j) * HALF + row, 8)
                    out_ref[pl.ds(at, 8), :] = value
        return carry

    lax.fori_loop(0, GROUPS, some, 0)
    for target in range(LEVELS):
        out_ref[pl.ds((target + 1) * WINDOW - META, META), :] = meta_ref[...]


def unpack_kernel(
    tables_ref, rates_ref, in_ref, s_ref, t_ref, wall_s_ref, wall_t_ref, rows_ref, taken_ref
):
    def some(g, carry):
        left = in_half((8, DEPTH), 0)
        for row in range(0, HALF, 8):
            for ref, first, second in ((s_ref, 3, 2), (t_ref, 1, 0)):
                parts = []
                for level in (first, second):
                    at = pl.multiple_of(level * WINDOW + 3 * g * HALF + row, 8)
                    three = [in_ref[pl.ds(at + j * HALF, 8), :] for j in range(3)]
                    parts.append(three + [unfold(*three)])
                for j in range(4):
                    one, two = parts[0][j], parts[1][j]
                    crossed = turn(jnp.where(left, two, one), HALF, 1)
                    at = pl.multiple_of((4 * g + j) * PITCH + row, 8)
                    ref[pl.ds(at, 8), :] = jnp.where(left, one, crossed)
                    ref[pl.ds(at + HALF, 8), :] = jnp.where(left, crossed, two)
        return carry

    lax.fori_loop(0, GROUPS, some, 0)
    wall_s_ref[...] = s_ref[pl.ds(Q * PITCH, ROWS), :]
    wall_t_ref[...] = t_ref[pl.ds(Q * PITCH, ROWS), :]
    pick_rows(s_ref, 1, tables_ref, table_at(2, DOWN_SEND), rows_ref, UNIT, 0)
    taken_ref[...] = jnp.zeros((PITCH, DEPTH), jnp.float32)

    def mark(j, carry):
        row = tables_ref[table_at(3, DOWN_RECV) + j]
        spot = pl.ds(jnp.where(row < 0, ROWS, row), 1)
        taken_ref[spot, :] = jnp.where(in_half((1, DEPTH), 0), 1.0, 0.0)
        return carry

    lax.fori_loop(0, 2 * PEERS, mark, 0, unroll=8)


def apply(state_ref, couplings, tables_ref, buffers):
    for half, at, index, unit, offset, narrow in couplings:
        place_rows(state_ref, half, tables_ref, at, buffers[index], unit, offset, narrow)


def edges_kernel(levels, couplings, buffers, carried, tables_ref, rates_ref, *refs):
    refs = list(refs)
    state_ref, wall_ref = refs.pop(0), refs.pop(0)
    in_refs = [refs.pop(0) for _ in range(buffers)]
    other_refs = [refs.pop(0) for _ in range(2)] if carried else []
    work_ref, edge_ref, low_ref, high_ref = refs
    copy_state(state_ref, work_ref)
    apply(work_ref, couplings, tables_ref, in_refs)

    def load(q, row):
        return work_ref[pl.ds(q * PITCH + row, 8), :]

    rate = pair_rate(rates_ref, *levels)
    collide_edges(load, wall_ref, rate, edge_ref, low_ref, high_ref)
    for source, target in zip(other_refs, (low_ref, high_ref)):
        target[pl.ds(9 * WIDTH, 9 * WIDTH), :] = source[...]


def inside_kernel(levels, keep, extra, couplings, buffers, tables_ref, rates_ref, *refs):
    refs = list(refs)
    work_ref, wall_ref, edge_ref = refs.pop(0), refs.pop(0), refs.pop(0)
    old_ref = refs.pop(0) if keep else None
    other_ref = refs.pop(0) if extra and not extra[0] else None
    in_refs = [refs.pop(0) for _ in range(buffers)]
    inside_ref = refs.pop()
    read_ref = refs.pop(0)
    next_ref = refs.pop(0) if couplings else None

    def load(q, row):
        return work_ref[pl.ds(q * PITCH + row, 8), :]

    collide_inside(load, wall_ref, pair_rate(rates_ref, *levels), inside_ref)
    stream_known(edge_ref, inside_ref, read_ref, PITCH, old_ref, next_ref)
    apply(next_ref, couplings, tables_ref, in_refs)
    if extra:
        own, half, at = extra
        source = old_ref if own else other_ref
        pick_rows(source, half, tables_ref, at, refs.pop(0), 2 * UNIT, UNIT)


def joined_kernel(first, second, ins, outs, *refs):
    refs = list(refs)
    scalars = [[refs.pop(0), refs.pop(0)] for _ in range(2)]
    inputs = [[refs.pop(0) for _ in range(count)] for count in ins]
    outputs = [[refs.pop(0) for _ in range(count)] for count in outs]
    for i, kernel in enumerate((first, second)):
        kernel(*scalars[i], *inputs[i], *outputs[i], refs[i])


def rest_kernel(keep, picks, unit, carried, ahead, inputs, tables_ref, front_ref, behind_ref, *refs):
    taken_ref = refs[0] if ahead else None
    refs = list(refs)[inputs:]
    seen_ref, rows_ref = refs.pop(0), refs.pop(0)
    next_ref = refs.pop(0) if ahead else None
    other_ref = refs.pop(0) if carried else None
    stream_rest(front_ref, behind_ref, seen_ref, PITCH, keep, 0, next_ref, taken_ref)
    if carried:
        stream_rest(front_ref, behind_ref, other_ref, PITCH, True, 9 * WIDTH)
    for other, half, at, offset, narrow in picks:
        source = other_ref if other else seen_ref
        pick_rows(source, half, tables_ref, at, rows_ref, unit, offset, narrow)


def pack_level(work_ref, half, out_ref):
    def one(q, carry):
        chunk = lanes_of((8, DEPTH)) // OWN
        for row in range(0, WIDTH, 8):
            packed = None
            for plane in range(PLANES):
                at = pl.multiple_of(q * PITCH + plane * WIDTH + row, 8)
                value = turn(work_ref[pl.ds(at, 8), :], OWN * plane - HALF * half - GHOST, 1)
                packed = value if packed is None else jnp.where(chunk == plane, value, packed)
            out_ref[pl.ds(pl.multiple_of(q * WIDTH + row, 8), 8), :] = packed
        return carry

    lax.fori_loop(0, Q, one, 0, unroll=9)


def pack_levels(tables_ref, work_ref, levels, out_refs):
    for me in range(LEVELS):

        @pl.when(tables_ref[ME] == me)
        def _():
            for half, level in levels:
                pack_level(work_ref, half, out_refs[(level - me) % LEVELS])


def other_last_kernel(couplings, tables_ref, rates_ref, state_ref, b2, b5, b6, *refs):
    out_refs, work_ref = refs[:-1], refs[-1]
    copy_state(state_ref, work_ref)
    apply(work_ref, couplings, tables_ref, (b2, b5, b6))
    pack_levels(tables_ref, work_ref, ((1, 0), (0, 1)), out_refs)


def last_kernel(couplings, tables_ref, rates_ref, state_ref, b7, *refs):
    out_refs, work_ref = refs[LEVELS:-1], refs[-1]
    copy_state(state_ref, work_ref)
    apply(work_ref, couplings, tables_ref, (b7,))
    pack_levels(tables_ref, work_ref, ((1, 2), (0, 3)), out_refs)


def output_kernel(tables_ref, *refs):
    in_refs, out_ref = refs[:-1], refs[-1]
    chunk = lanes_of((WIDTH, DEPTH)) // OWN
    for me in range(LEVELS):

        @pl.when(tables_ref[ME] == me)
        def _():
            def one(q, carry):
                parts = [
                    in_refs[(me - c) % LEVELS][pl.ds(pl.multiple_of(q * WIDTH, 8), WIDTH), :]
                    for c in range(LEVELS)
                ]
                for plane in range(PLANES):
                    whole = None
                    for c in range(LEVELS):
                        value = turn(parts[c], OWN * (c - plane), 1)
                        whole = value if whole is None else jnp.where(chunk == c, value, whole)
                    out_ref[pl.ds(pl.multiple_of(q * ROWS + plane * WIDTH, 8), WIDTH), :] = whole
                return carry

            lax.fori_loop(0, Q, one, 0, unroll=3)


def trade_planes(low, high):
    count = lax.axis_size("gx")
    forward = [(i, (i + 1) % count) for i in range(count)]
    backward = [(target, source) for source, target in forward]
    return lax.ppermute(low, "gx", backward), lax.ppermute(high, "gx", forward)


def trade_rows(rows):
    blocks = rows.reshape(PEERS, -1, DEPTH)
    return lax.all_to_all(blocks, "gx", split_axis=0, concat_axis=0, tiled=True).reshape(
        rows.shape
    )


def on_device(populations, solid_mask, relax_rates, down_send, down_recv, up_send, up_recv):
    meta = jnp.concatenate(
        [value.reshape(-1) for value in (down_send, down_recv, up_send, up_recv)]
    ).astype(jnp.float32)
    meta = jnp.concatenate([meta, jnp.broadcast_to(relax_rates, (META * DEPTH - meta.size,))])
    meta = meta.reshape(META, DEPTH)
    x = jnp.transpose(populations.reshape(ROWS, Q, DEPTH), (1, 0, 2)).reshape(Q * ROWS, DEPTH)
    wall = solid_mask.reshape(ROWS, DEPTH).astype(jnp.float32)
    flow = [(Q * ROWS, DEPTH), (9 * WIDTH, DEPTH), (9 * WIDTH, DEPTH)]
    state = (STATE, DEPTH)

    edge, low, high = call(
        first_edges_kernel, [(Q * HALF, DEPTH), *flow[1:]], (relax_rates, x, wall), smem=1
    )
    front, behind = trade_planes(low, high)
    (seen,) = call(
        first_inside_kernel,
        [flow[0]],
        (relax_rates, x, wall, edge),
        smem=1,
        scratch=[(Q * HALF, DEPTH)],
    )
    (windows,) = call(
        windows_kernel,
        [(LEVELS * WINDOW, DEPTH)],
        (seen, front, behind, wall, meta),
        scratch=[((Q + 1) * ROWS, DEPTH)],
    )
    windows = lax.all_to_all(
        windows.reshape(LEVELS, WINDOW, DEPTH), "lvl", 0, 0, tiled=True
    )
    tables = windows[:, WINDOW - META : WINDOW - META + 2, :].astype(jnp.int32).reshape(-1)
    me = lax.axis_index("lvl").astype(jnp.int32)
    tables = jnp.concatenate([tables, jnp.full((DEPTH,), me, jnp.int32)])
    rates = windows[:, WINDOW - 1, 0]
    windows = windows.reshape(-1, DEPTH)
    s, t, wall_s, wall_t, rows, coupled = call(
        unpack_kernel,
        [state, state, (ROWS, DEPTH), (ROWS, DEPTH), (PEERS * UNIT, DEPTH), (PITCH, DEPTH)],
        (tables, rates, windows),
        smem=2,
    )
    got = {0: trade_rows(rows)}

    def taken(step, offset, half, level, which, narrow=False):
        buffer = got[step]
        return buffer, half, table_at(level, which), buffer.shape[0] // PEERS, offset, narrow

    def gather_takes(takes):
        buffers, couplings = [], []
        for buffer, half, at, unit, offset, narrow in takes:
            index = next((i for i, b in enumerate(buffers) if b is buffer), len(buffers))
            if index == len(buffers):
                buffers.append(buffer)
            couplings.append((half, at, index, unit, offset, narrow))
        return buffers, couplings

    def edges(value, walls, levels, takes, carried=()):
        buffers, couplings = gather_takes(takes)
        planes = (9 * WIDTH * (2 if carried else 1), DEPTH)
        return call(
            functools.partial(edges_kernel, levels, couplings, len(buffers), bool(carried)),
            [state, (Q * HALF, DEPTH), planes, planes],
            (tables, rates, value, walls, *buffers, *carried),
            smem=2,
        )

    def inside(work, walls, edge, levels, old=None, extra=None, other=None, takes=(), join=None):
        buffers, couplings = gather_takes(takes)
        ins = [work, walls, edge]
        ins += [old] if old is not None else []
        ins += [other] if extra and not extra[0] else []
        ins += buffers
        kernel = functools.partial(
            inside_kernel, levels, old is not None, extra, couplings, len(buffers)
        )
        outs = [state] * (2 if takes else 1) + ([(PEERS * 2 * UNIT, DEPTH)] if extra else [])
        scratch = [(Q * HALF, DEPTH)]
        if join is None:
            return call(kernel, outs, (tables, rates, *ins), smem=2, scratch=scratch)
        second, more_ins, more_outs = join
        return call(
            functools.partial(
                joined_kernel, kernel, second, (len(ins), len(more_ins)), (len(outs), len(more_outs))
            ),
            outs + more_outs,
            (tables, rates, tables, rates, *ins, *more_ins),
            smem=4,
            scratch=scratch + [state],
        )

    down_23 = (False, 1, table_at(2, DOWN_SEND), 0, False)
    up_32 = (False, 0, table_at(3, UP_SEND), 0, False)
    extras = {
        1: (False, 0, table_at(1, DOWN_SEND)),
        2: (False, 1, table_at(0, DOWN_SEND)),
        3: (True, 1, table_at(2, UP_SEND)),
    }
    picks = {
        1: [up_32],
        2: [down_23],
        3: [up_32],
        4: [down_23],
        5: [
            up_32,
            (True, 0, table_at(1, DOWN_SEND), UNIT, False),
            (True, 0, table_at(1, UP_SEND), 2 * UNIT, True),
        ],
        6: [down_23, (False, 1, table_at(2, UP_SEND), UNIT, True)],
        7: [(False, 0, table_at(3, UP_SEND), 0, True)],
    }
    units = {1: 48, 2: 48, 3: 48, 4: 24, 5: 64, 6: 40, 7: 16}
    for step in range(1, 8):
        odd = step % 2 == 1
        if odd:
            takes = [taken(step - 1, 0, 0, 3, DOWN_RECV)]
        else:
            takes = [taken(step - 1, 0, 1, 2, UP_RECV)]
            if step == 6:
                takes.append(taken(5, UNIT, 1, 2, DOWN_RECV))
            elif step == 2:
                takes.append(taken(1, UNIT, 1, 2, DOWN_RECV))
        carried = step == 5
        work, edge, low, high = edges(
            s, wall_s, (3, 2), takes, (t_low, t_high) if carried else ()
        )
        front, behind = trade_planes(low, high)
        extra = extras.get(step)
        ahead = []
        if odd:
            ahead.append(taken(step - 1, 0, 0, 3, DOWN_RECV))
            if step in (3, 7):
                ahead.append(taken(1 if step == 3 else 5, UNIT, 1, 2, DOWN_RECV))
        join = None
        if step == 7:
            couplings = [
                (0, table_at(1, DOWN_RECV), 0, units[2], UNIT, False),
                (1, table_at(0, UP_RECV), 1, units[5], 2 * UNIT, True),
                (0, table_at(1, UP_RECV), 2, units[6], UNIT, True),
            ]
            join = (
                functools.partial(other_last_kernel, couplings),
                (t, got[2], got[5], got[6]),
                [(Q * WIDTH, DEPTH)] * LEVELS,
            )
        seen, *rows = inside(work, wall_s, edge, (3, 2), s if odd else None, extra, t, ahead, join)
        following = [rows.pop(0)] if ahead else []
        if join:
            packed, rows = rows, []
        if step == 4:
            takes = [taken(2, UNIT, 0, 1, DOWN_RECV), taken(3, UNIT, 0, 1, UP_RECV)]
            t_work, t_edge, t_low, t_high = edges(t, wall_t, (1, 0), takes)
            seen, t_work, t_edge, t_low, t_high = lax.optimization_barrier(
                (seen, t_work, t_edge, t_low, t_high)
            )
        if step == 5:
            (t,) = inside(t_work, wall_t, t_edge, (1, 0), t)
        unit = units[step]
        ins = [tables, front, behind] + ([coupled] if ahead else [])
        outs, aliases = [], {}
        for value in (seen, *rows, *following, *([t] if carried else [])):
            if value is seen or rows:
                slot = len(outs)
            else:
                slot = len(outs) + 1 if len(outs) == 1 else len(outs)
            if slot == 2 and len(outs) == 1:
                outs.append((PEERS * unit, DEPTH))
            aliases[len(ins)] = slot
            outs.append(value.shape)
            ins.append(value)
        if len(outs) == 1:
            outs.append((PEERS * unit, DEPTH))
        s, got[step], *others = call(
            functools.partial(
                rest_kernel, odd, picks[step], unit, carried, bool(ahead), len(ins) - 3
            ),
            outs,
            ins,
            smem=1,
            aliases=aliases,
        )
        if ahead:
            s = others.pop(0)
        if carried:
            (t,) = others
        got[step] = trade_rows(got[step])

    couplings = [(1, table_at(2, UP_RECV), 0, units[7], 0, True)]
    packed = call(
        functools.partial(last_kernel, couplings),
        [(Q * WIDTH, DEPTH)] * LEVELS,
        (tables, rates, s, got[7], *packed),
        smem=2,
        scratch=[state],
        aliases={4 + i: i for i in range(LEVELS)},
    )
    parts = [packed[0]] + [
        lax.ppermute(packed[by], "lvl", [(i, (i + by) % LEVELS) for i in range(LEVELS)])
        for by in range(1, LEVELS)
    ]
    (final,) = call(output_kernel, [(Q * ROWS, DEPTH)], (tables, *parts), smem=1)
    final = jnp.transpose(final.reshape(Q, ROWS, DEPTH), (1, 0, 2))
    return final.reshape(1, PLANES, WIDTH, Q, DEPTH)


def solution(mesh):
    return jax.shard_map(
        on_device,
        mesh=mesh,
        in_specs=(
            P("lvl", "gx", None, None, None),
            P("lvl", "gx", None, None),
            P("lvl"),
            P("lvl", "gx", None, None),
            P("lvl", "gx", None, None),
            P("lvl", "gx", None, None),
            P("lvl", "gx", None, None),
        ),
        out_specs=P("lvl", "gx", None, None, None),
        check_vma=False,
    )
```

```python
import functools

import jax
import jax.numpy as jnp
from jax import lax
from jax.experimental import pallas as pl
from jax.experimental.pallas import tpu as pltpu
from jax.sharding import PartitionSpec as P

Q = 27
PLANES = 4
WIDTH = 32
ROWS = PLANES * WIDTH
DEPTH = 128
PEERS = 32
LEVELS = 4
HALF = 64
OWN = 32
GHOST = 16
PITCH = 136
QPAD = 32
STATE = QPAD * PITCH
UNIT = 24
NARROW = 16
BLOCKS = 9 * WIDTH // 8
GROUPS = 7
META = 8
WINDOW = 3 * GROUPS * HALF + META

VMEM = pl.BlockSpec(memory_space=pltpu.VMEM)
SMEM = pl.BlockSpec(memory_space=pltpu.SMEM)

DOWN_SEND, DOWN_RECV, UP_SEND, UP_RECV = range(4)
ME = 4 * 2 * PEERS
LEVEL_TABLES = ME + DEPTH


def table_at(level, which):
    return level * LEVEL_TABLES + which * 2 * PEERS


def call(kernel, outs, ins, smem=0, scratch=(), aliases=None):
    moved = sum(value.size for value in ins) + sum(rows * depth for rows, depth in outs)
    return pl.pallas_call(
        kernel,
        out_shape=[jax.ShapeDtypeStruct(shape, jnp.float32) for shape in outs],
        in_specs=[SMEM] * smem + [VMEM] * (len(ins) - smem),
        out_specs=[VMEM] * len(outs),
        scratch_shapes=[pltpu.VMEM(shape, jnp.float32) for shape in scratch],
        input_output_aliases=aliases or {},
        cost_estimate=pl.CostEstimate(
            flops=10 * moved, bytes_accessed=4 * moved, transcendentals=0
        ),
        compiler_params=pltpu.CompilerParams(vmem_limit_bytes=14 * 1024 * 1024),
    )(*ins)


def lanes_of(shape):
    return lax.broadcasted_iota(jnp.int32, shape, 1)


def in_half(shape, half):
    lanes = lanes_of(shape)
    return lanes < HALF if half == 0 else lanes >= HALF


def turn(value, shift, axis):
    size = value.shape[axis]
    shift = shift % size
    return value if shift == 0 else pltpu.roll(value, shift, axis)


def gaps(shape):
    lanes = lanes_of(shape)
    return (lanes >= 56) & (lanes < 72), (lanes < 8) | (lanes >= 120)


def fold(t0, t1, t2, extra):
    return fold_turned(t0, t1, t2, *(turn(extra, shift, 1) for shift in (16, 48, 96)))


def fold_turned(t0, t1, t2, e16, e48, e96):
    inner, outer = gaps(t0.shape)
    return (
        jnp.where(inner, e48, jnp.where(outer, e96, t0)),
        jnp.where(inner, e16, jnp.where(outer, e48, t1)),
        jnp.where(inner, e96, jnp.where(outer, e16, t2)),
    )


def unfold(t0, t1, t2):
    inner, _ = gaps(t0.shape)
    e48 = turn(jnp.where(inner, t0, t1), -48, 1)
    e96 = turn(jnp.where(inner, t2, t0), -96, 1)
    e16 = turn(jnp.where(inner, t1, t2), -16, 1)
    spot = lanes_of(t0.shape) & (HALF - 1)
    return jnp.where(spot < 24, e48, jnp.where(spot < 40, e96, e16))


def fold_own(m0, m1, m2, m3):
    quarter = lanes_of(m0.shape) // OWN

    def join(a, b):
        return jnp.where(
            quarter < 2,
            jnp.where(quarter == 0, turn(a, -16, 1), turn(a, -48, 1)),
            jnp.where(quarter == 2, turn(b, 48, 1), turn(b, 16, 1)),
        )

    return join(m0, m1), join(m2, m3)


def unfold_own(t0, t1):
    left = in_half(t0.shape, 0)
    out = []
    for value in (t0, t1):
        out.append(jnp.where(left, turn(value, 16, 1), turn(value, 48, 1)))
        out.append(jnp.where(left, turn(value, -48, 1), turn(value, -16, 1)))
    return out


def collide(f, wall, rate):
    t, d = [], []
    for pair in range(9):
        low, mid, high = f[3 * pair : 3 * pair + 3]
        t.append(low + high + 4.0 * mid)
        d.append(high - low)
    total, along_y, along_z = [], [], []
    for a in range(3):
        total.append(t[3 * a] + t[3 * a + 2] + 4.0 * t[3 * a + 1])
        along_y.append(t[3 * a + 2] - t[3 * a])
        along_z.append(d[3 * a] + d[3 * a + 2] + 4.0 * d[3 * a + 1])
    mass = total[0] + total[2] + 4.0 * total[1]
    inverse = 3.0 / mass
    ux = (total[2] - total[0]) * inverse
    uy = (along_y[0] + along_y[2] + 4.0 * along_y[1]) * inverse
    uz = (along_z[0] + along_z[2] + 4.0 * along_z[1]) * inverse
    scaled = rate * mass * (1.0 / 216.0)
    half = 0.5 * scaled
    base = scaled - scaled * ((ux * ux + uy * uy + uz * uz) * (1.0 / 6.0))
    keep = 1.0 - rate
    sums = {
        (0, 0, 1): uz,
        (0, 1, 0): uy,
        (1, 0, 0): ux,
        (0, 1, -1): uy - uz,
        (0, 1, 1): uy + uz,
        (1, 0, -1): ux - uz,
        (1, 0, 1): ux + uz,
        (1, -1, 0): ux - uy,
        (1, 1, 0): ux + uy,
    }
    for b in (-1, 1):
        for e in (-1, 1):
            sums[(1, b, e)] = sums[(1, b, 0)] + uz if e == 1 else sums[(1, b, 0)] - uz
    out = [None] * Q
    out[13] = jnp.where(wall, f[13], keep * f[13] + base)
    for (a, b, e), along in sums.items():
        i = 9 * (a + 1) + 3 * (b + 1) + (e + 1)
        j = 26 - i
        part = half * along
        odd = part + part
        even = base + part * along
        out[i] = jnp.where(wall, f[j], keep * f[i] + (even + odd))
        out[j] = jnp.where(wall, f[i], keep * f[j] + (even - odd))
    return out


def collide_rows(load, wall_ref, rate, store, tiles):
    def tile(i, carry):
        row = pl.multiple_of(tiles(i) * 8, 8)
        wall = wall_ref[pl.ds(row, 8), :] > 0.5
        out = collide([load(q, row) for q in range(Q)], wall, rate)
        for q in range(Q):
            store(q, row, turn(out[q], q % 3 - 1, 1))
        return carry

    lax.fori_loop(0, ROWS // 16, tile, 0, unroll=4)


def edge_tiles(i):
    return jnp.where(i < 4, i, i + 8)


def inner_tiles(i):
    return i + 4


def collide_edges(load, wall_ref, rate, edge_ref, low_ref, high_ref, halved=False):
    def store(q, row, value):
        at = jnp.where(row < WIDTH, row, row - 2 * WIDTH)
        edge_ref[pl.ds(pl.multiple_of(q * HALF + at, 8), 8), :] = value

    collide_rows(load, wall_ref, rate, store, edge_tiles)

    def block(first, i):
        return edge_ref[pl.ds(first + i // 4 * HALF + i % 4 * 8, 8), :]

    for ref, first in ((low_ref, 0), (high_ref, 18 * HALF + WIDTH)):
        if halved:
            for i in range(BLOCKS // 2):
                ref[pl.ds(8 * i, 8), :] = jnp.where(
                    in_half((8, DEPTH), 0),
                    block(first, i),
                    turn(block(first, i + BLOCKS // 2), HALF, 1),
                )
        else:
            for i in range(BLOCKS):
                ref[pl.ds(8 * i, 8), :] = block(first, i)


def collide_inside(load, wall_ref, rate, inside_ref):
    def store(q, row, value):
        inside_ref[pl.ds(pl.multiple_of(q * HALF + row - WIDTH, 8), 8), :] = value

    collide_rows(load, wall_ref, rate, store, inner_tiles)


def stream_known(edge_ref, inside_ref, read_ref, pitch, old_ref, next_ref=None):
    for q in range(Q):
        for plane in range(PLANES):
            source = plane - (q // 9 - 1)
            spot = pl.ds(q * pitch + plane * WIDTH, WIDTH)
            if 0 <= source < PLANES:
                if source in (0, PLANES - 1):
                    value = edge_ref[pl.ds(q * HALF + (WIDTH if source else 0), WIDTH), :]
                else:
                    value = inside_ref[pl.ds(q * HALF + (source - 1) * WIDTH, WIDTH), :]
                value = turn(value, q // 3 % 3 - 1, 0)
                if old_ref is not None:
                    value = jnp.where(in_half((WIDTH, DEPTH), 0), value, old_ref[spot, :])
            elif old_ref is not None:
                value = old_ref[spot, :]
            else:
                continue
            read_ref[spot, :] = value
            if next_ref is not None:
                next_ref[spot, :] = value


def stream_rest(
    front_ref, behind_ref, read_ref, pitch, keep, start=0, next_ref=None, taken_ref=None, halved=False
):
    def block(ref, i):
        if halved and i >= BLOCKS // 2:
            return turn(ref[pl.ds(start + 8 * i - 4 * BLOCKS, 8), :], HALF, 1)
        return ref[pl.ds(start + 8 * i, 8), :]

    for q in range(9):
        for velocity, plane, ref in ((q, PLANES - 1, front_ref), (q + 18, 0, behind_ref)):
            spot = pl.ds(velocity * pitch + plane * WIDTH, WIDTH)
            value = jnp.concatenate([block(ref, 4 * q + i) for i in range(4)], axis=0)
            value = turn(value, q // 3 - 1, 0)
            if keep:
                value = jnp.where(in_half((WIDTH, DEPTH), 0), value, read_ref[spot, :])
            read_ref[spot, :] = value
            if next_ref is not None:
                placed = taken_ref[pl.ds(plane * WIDTH, WIDTH), :] > 0.5
                free = in_half((WIDTH, DEPTH), 0) & jnp.logical_not(placed)
                next_ref[spot, :] = jnp.where(free, value, next_ref[spot, :])


def pick_rows(state_ref, half, tables_ref, at, out_ref, unit, offset, narrow=False):
    group = 16

    def some(g, carry):
        for j in range(group):
            peer = g * group + j
            first = jnp.maximum(tables_ref[at + 2 * peer], 0)
            second = jnp.maximum(tables_ref[at + 2 * peer + 1], 0)
            merged = []
            for c in range(QPAD // 8):
                one = state_ref[pl.ds(first + c * 8 * PITCH, 8, stride=PITCH), :]
                two = state_ref[pl.ds(second + c * 8 * PITCH, 8, stride=PITCH), :]
                if half == 0:
                    two = turn(two, HALF, 1)
                else:
                    one = turn(one, HALF, 1)
                merged.append(jnp.where(in_half((8, DEPTH), 0), one, two))
            for c, value in enumerate((fold_own if narrow else fold)(*merged)):
                spot = pl.multiple_of(peer * unit + offset + 8 * c, 8)
                out_ref[pl.ds(spot, 8), :] = value
        return carry

    lax.fori_loop(0, PEERS // group, some, 0)


def place_rows(state_ref, half, tables_ref, at, in_ref, unit, offset, narrow=False):
    group = 16

    def some(g, carry):
        stores = []
        for j in range(group):
            peer = g * group + j
            parts = [
                in_ref[pl.ds(pl.multiple_of(peer * unit + offset + 8 * c, 8), 8), :]
                for c in range(2 if narrow else 3)
            ]
            parts = unfold_own(*parts) if narrow else parts + [unfold(*parts)]
            for k in range(2):
                row = tables_ref[at + 2 * peer + k]
                row = jnp.where(row < 0, ROWS, row)
                for c, value in enumerate(parts):
                    if k != half:
                        value = turn(value, HALF, 1)
                    where = pl.ds(row + c * 8 * PITCH, 8, stride=PITCH)
                    stores.append(
                        (where, jnp.where(in_half((8, DEPTH), half), value, state_ref[where, :]))
                    )
        for where, value in stores:
            state_ref[where, :] = value
        return carry

    lax.fori_loop(0, PEERS // group, some, 0)


def copy_state(source_ref, target_ref):
    def one(q, carry):
        at = pl.multiple_of(q * PITCH, 8)
        target_ref[pl.ds(at, ROWS), :] = source_ref[pl.ds(at, ROWS), :]
        return carry

    lax.fori_loop(0, Q, one, 0)


def pair_rate(rates_ref, first, second):
    return jnp.where(in_half((8, DEPTH), 0), rates_ref[first], rates_ref[second])


def first_edges_kernel(rate_ref, x_ref, wall_ref, edge_ref, low_ref, high_ref):
    rate = jnp.full((8, DEPTH), rate_ref[0], jnp.float32)

    def load(q, row):
        return x_ref[pl.ds(q * ROWS + row, 8), :]

    collide_edges(load, wall_ref, rate, edge_ref, low_ref, high_ref)


def first_inside_kernel(rate_ref, x_ref, wall_ref, edge_ref, read_ref, inside_ref):
    rate = jnp.full((8, DEPTH), rate_ref[0], jnp.float32)

    def load(q, row):
        return x_ref[pl.ds(q * ROWS + row, 8), :]

    collide_inside(load, wall_ref, rate, inside_ref)
    stream_known(edge_ref, inside_ref, read_ref, ROWS, None)


def windows_kernel(seen_ref, front_ref, behind_ref, wall_ref, meta_ref, out_ref, read_ref):
    read_ref[pl.ds(0, Q * ROWS), :] = seen_ref[...]
    stream_rest(front_ref, behind_ref, read_ref, ROWS, False)
    read_ref[pl.ds(Q * ROWS, ROWS), :] = wall_ref[...].astype(jnp.float32)

    def some(g, carry):
        lanes = lanes_of((8, DEPTH))
        for row in range(0, HALF, 8):
            mixed = []
            for j in range(4):
                at = pl.multiple_of((4 * g + j) * ROWS + row, 8)
                top = read_ref[pl.ds(at, 8), :]
                bottom = turn(read_ref[pl.ds(at + HALF, 8), :], HALF, 1)
                mixed.append(
                    [
                        jnp.where(((lanes + GHOST - OWN * k) & (DEPTH - 1)) < HALF, top, bottom)
                        for k in range(LEVELS)
                    ]
                )
            for target in range(LEVELS):
                shift = GHOST - OWN * target
                main = [turn(mixed[j][target], shift, 1) for j in range(3)]
                extra = [turn(mixed[3][target], shift + by, 1) for by in (16, 48, 96)]
                for j, value in enumerate(fold_turned(*main, *extra)):
                    at = pl.multiple_of(target * WINDOW + (3 * g + j) * HALF + row, 8)
                    out_ref[pl.ds(at, 8), :] = value
        return carry

    lax.fori_loop(0, GROUPS, some, 0)
    for target in range(LEVELS):
        at = (target + 1) * WINDOW - META
        out_ref[pl.ds(at, META), :] = meta_ref[...]
        out_ref[pl.ds(at + 2, 1), :] = jnp.full((1, DEPTH), target, jnp.float32)


def unpack_kernel(
    tables_ref, rates_ref, in_ref, s_ref, t_ref, wall_s_ref, wall_t_ref, rows_ref, taken_ref
):
    def some(g, carry):
        left = in_half((8, DEPTH), 0)
        for row in range(0, HALF, 8):
            for ref, first, second in ((s_ref, 3, 2), (t_ref, 1, 0)):
                parts = []
                for level in (first, second):
                    at = pl.multiple_of(level * WINDOW + 3 * g * HALF + row, 8)
                    three = [in_ref[pl.ds(at + j * HALF, 8), :] for j in range(3)]
                    parts.append(three + [unfold(*three)])
                for j in range(4):
                    one, two = parts[0][j], parts[1][j]
                    crossed = turn(jnp.where(left, two, one), HALF, 1)
                    at = pl.multiple_of((4 * g + j) * PITCH + row, 8)
                    ref[pl.ds(at, 8), :] = jnp.where(left, one, crossed)
                    ref[pl.ds(at + HALF, 8), :] = jnp.where(left, crossed, two)
        return carry

    lax.fori_loop(0, GROUPS, some, 0)
    wall_s_ref[...] = s_ref[pl.ds(Q * PITCH, ROWS), :]
    wall_t_ref[...] = t_ref[pl.ds(Q * PITCH, ROWS), :]
    pick_rows(s_ref, 1, tables_ref, table_at(2, DOWN_SEND), rows_ref, UNIT, 0)
    taken_ref[...] = jnp.zeros((PITCH, DEPTH), jnp.float32)

    def mark(j, carry):
        row = tables_ref[table_at(3, DOWN_RECV) + j]
        spot = pl.ds(jnp.where(row < 0, ROWS, row), 1)
        taken_ref[spot, :] = jnp.where(in_half((1, DEPTH), 0), 1.0, 0.0)
        return carry

    lax.fori_loop(0, 2 * PEERS, mark, 0, unroll=8)


def apply(state_ref, couplings, tables_ref, buffers):
    for half, at, index, unit, offset, narrow in couplings:
        place_rows(state_ref, half, tables_ref, at, buffers[index], unit, offset, narrow)


def edges_kernel(levels, couplings, buffers, carried, halved, tables_ref, rates_ref, *refs):
    refs = list(refs)
    state_ref, wall_ref = refs.pop(0), refs.pop(0)
    in_refs = [refs.pop(0) for _ in range(buffers)]
    other_refs = [refs.pop(0) for _ in range(2)] if carried else []
    work_ref, edge_ref, low_ref, high_ref = refs
    copy_state(state_ref, work_ref)
    apply(work_ref, couplings, tables_ref, in_refs)

    def load(q, row):
        return work_ref[pl.ds(q * PITCH + row, 8), :]

    rate = pair_rate(rates_ref, *levels)
    collide_edges(load, wall_ref, rate, edge_ref, low_ref, high_ref, halved)
    for source, target in zip(other_refs, (low_ref, high_ref)):
        target[pl.ds(4 * BLOCKS, 4 * BLOCKS), :] = source[...]


def inside_kernel(levels, keep, extra, couplings, buffers, tables_ref, rates_ref, *refs):
    refs = list(refs)
    work_ref, wall_ref, edge_ref = refs.pop(0), refs.pop(0), refs.pop(0)
    old_ref = refs.pop(0) if keep else None
    other_ref = refs.pop(0) if extra and not extra[0] else None
    in_refs = [refs.pop(0) for _ in range(buffers)]
    inside_ref = refs.pop()
    read_ref = refs.pop(0)
    next_ref = refs.pop(0) if couplings else None

    def load(q, row):
        return work_ref[pl.ds(q * PITCH + row, 8), :]

    collide_inside(load, wall_ref, pair_rate(rates_ref, *levels), inside_ref)
    stream_known(edge_ref, inside_ref, read_ref, PITCH, old_ref, next_ref)
    apply(next_ref, couplings, tables_ref, in_refs)
    if extra:
        own, half, at = extra
        source = old_ref if own else other_ref
        pick_rows(source, half, tables_ref, at, refs.pop(0), 2 * UNIT, UNIT)


def joined_kernel(first, second, ins, outs, *refs):
    refs = list(refs)
    scalars = [[refs.pop(0), refs.pop(0)] for _ in range(2)]
    inputs = [[refs.pop(0) for _ in range(count)] for count in ins]
    outputs = [[refs.pop(0) for _ in range(count)] for count in outs]
    for i, kernel in enumerate((first, second)):
        kernel(*scalars[i], *inputs[i], *outputs[i], refs[i])


def rest_kernel(keep, picks, unit, carried, ahead, inputs, tables_ref, front_ref, behind_ref, *refs):
    taken_ref = refs[0] if ahead else None
    refs = list(refs)[inputs:]
    seen_ref, rows_ref = refs.pop(0), refs.pop(0)
    next_ref = refs.pop(0) if ahead else None
    other_ref = refs.pop(0) if carried else None
    stream_rest(
        front_ref, behind_ref, seen_ref, PITCH, keep, 0, next_ref, taken_ref, halved=keep
    )
    if carried:
        stream_rest(front_ref, behind_ref, other_ref, PITCH, True, 4 * BLOCKS, halved=True)
    for other, half, at, offset, narrow in picks:
        source = other_ref if other else seen_ref
        pick_rows(source, half, tables_ref, at, rows_ref, unit, offset, narrow)


def pack_level(work_ref, half, out_ref):
    def one(q, carry):
        chunk = lanes_of((8, DEPTH)) // OWN
        for row in range(0, WIDTH, 8):
            packed = None
            for plane in range(PLANES):
                at = pl.multiple_of(q * PITCH + plane * WIDTH + row, 8)
                value = turn(work_ref[pl.ds(at, 8), :], OWN * plane - HALF * half - GHOST, 1)
                packed = value if packed is None else jnp.where(chunk == plane, value, packed)
            out_ref[pl.ds(pl.multiple_of(q * WIDTH + row, 8), 8), :] = packed
        return carry

    lax.fori_loop(0, Q, one, 0, unroll=9)


def pack_levels(tables_ref, work_ref, levels, out_refs):
    for me in range(LEVELS):

        @pl.when(tables_ref[ME] == me)
        def _():
            for half, level in levels:
                pack_level(work_ref, half, out_refs[(level - me) % LEVELS])


def other_last_kernel(couplings, tables_ref, rates_ref, state_ref, b2, b5, b6, *refs):
    out_refs, work_ref = refs[:-1], refs[-1]
    copy_state(state_ref, work_ref)
    apply(work_ref, couplings, tables_ref, (b2, b5, b6))
    pack_levels(tables_ref, work_ref, ((1, 0), (0, 1)), out_refs)


def last_kernel(couplings, tables_ref, rates_ref, state_ref, b7, *refs):
    out_refs, work_ref = refs[LEVELS:-1], refs[-1]
    copy_state(state_ref, work_ref)
    apply(work_ref, couplings, tables_ref, (b7,))
    pack_levels(tables_ref, work_ref, ((1, 2), (0, 3)), out_refs)


def output_kernel(tables_ref, *refs):
    in_refs, out_ref = refs[:-1], refs[-1]
    chunk = lanes_of((WIDTH, DEPTH)) // OWN
    for me in range(LEVELS):

        @pl.when(tables_ref[ME] == me)
        def _():
            def one(q, carry):
                parts = [
                    in_refs[(me - c) % LEVELS][pl.ds(pl.multiple_of(q * WIDTH, 8), WIDTH), :]
                    for c in range(LEVELS)
                ]
                for plane in range(PLANES):
                    whole = None
                    for c in range(LEVELS):
                        value = turn(parts[c], OWN * (c - plane), 1)
                        whole = value if whole is None else jnp.where(chunk == c, value, whole)
                    out_ref[pl.ds(pl.multiple_of(q * ROWS + plane * WIDTH, 8), WIDTH), :] = whole
                return carry

            lax.fori_loop(0, Q, one, 0, unroll=3)


def trade_planes(low, high):
    count = lax.axis_size("gx")
    forward = [(i, (i + 1) % count) for i in range(count)]
    backward = [(target, source) for source, target in forward]
    return lax.ppermute(low, "gx", backward), lax.ppermute(high, "gx", forward)


def trade_rows(rows):
    blocks = rows.reshape(PEERS, -1, DEPTH)
    return lax.all_to_all(blocks, "gx", split_axis=0, concat_axis=0, tiled=True).reshape(
        rows.shape
    )


def on_device(populations, solid_mask, relax_rates, down_send, down_recv, up_send, up_recv):
    meta = jnp.concatenate(
        [value.reshape(-1) for value in (down_send, down_recv, up_send, up_recv)]
    ).astype(jnp.float32)
    meta = jnp.concatenate([meta, jnp.broadcast_to(relax_rates, (META * DEPTH - meta.size,))])
    meta = meta.reshape(META, DEPTH)
    x = jnp.transpose(populations.reshape(ROWS, Q, DEPTH), (1, 0, 2)).reshape(Q * ROWS, DEPTH)
    wall = solid_mask.reshape(ROWS, DEPTH)
    flow = [(Q * ROWS, DEPTH), (9 * WIDTH, DEPTH), (9 * WIDTH, DEPTH)]
    state = (STATE, DEPTH)

    edge, low, high = call(
        first_edges_kernel, [(Q * HALF, DEPTH), *flow[1:]], (relax_rates, x, wall), smem=1
    )
    front, behind = trade_planes(low, high)
    (seen,) = call(
        first_inside_kernel,
        [flow[0]],
        (relax_rates, x, wall, edge),
        smem=1,
        scratch=[(Q * HALF, DEPTH)],
    )
    (windows,) = call(
        windows_kernel,
        [(LEVELS * WINDOW, DEPTH)],
        (seen, front, behind, wall, meta),
        scratch=[((Q + 1) * ROWS, DEPTH)],
    )
    windows = lax.all_to_all(
        windows.reshape(LEVELS, WINDOW, DEPTH), "lvl", 0, 0, tiled=True
    )
    tables = windows[:, WINDOW - META : WINDOW - META + 3, :].astype(jnp.int32).reshape(-1)
    rates = windows[:, WINDOW - 1, 0]
    windows = windows.reshape(-1, DEPTH)
    s, t, wall_s, wall_t, rows, coupled = call(
        unpack_kernel,
        [state, state, (ROWS, DEPTH), (ROWS, DEPTH), (PEERS * UNIT, DEPTH), (PITCH, DEPTH)],
        (tables, rates, windows),
        smem=2,
    )
    got = {0: trade_rows(rows)}

    def taken(step, offset, half, level, which, narrow=False):
        buffer = got[step]
        return buffer, half, table_at(level, which), buffer.shape[0] // PEERS, offset, narrow

    def gather_takes(takes):
        buffers, couplings = [], []
        for buffer, half, at, unit, offset, narrow in takes:
            index = next((i for i, b in enumerate(buffers) if b is buffer), len(buffers))
            if index == len(buffers):
                buffers.append(buffer)
            couplings.append((half, at, index, unit, offset, narrow))
        return buffers, couplings

    def edges(value, walls, levels, takes, halved, carried=()):
        buffers, couplings = gather_takes(takes)
        planes = (8 * BLOCKS // (1 if carried or not halved else 2), DEPTH)
        return call(
            functools.partial(
                edges_kernel, levels, couplings, len(buffers), bool(carried), halved
            ),
            [state, (Q * HALF, DEPTH), planes, planes],
            (tables, rates, value, walls, *buffers, *carried),
            smem=2,
        )

    def inside(work, walls, edge, levels, old=None, extra=None, other=None, takes=(), join=None):
        buffers, couplings = gather_takes(takes)
        ins = [work, walls, edge]
        ins += [old] if old is not None else []
        ins += [other] if extra and not extra[0] else []
        ins += buffers
        kernel = functools.partial(
            inside_kernel, levels, old is not None, extra, couplings, len(buffers)
        )
        outs = [state] * (2 if takes else 1) + ([(PEERS * 2 * UNIT, DEPTH)] if extra else [])
        scratch = [(Q * HALF, DEPTH)]
        if join is None:
            return call(kernel, outs, (tables, rates, *ins), smem=2, scratch=scratch)
        second, more_ins, more_outs = join
        return call(
            functools.partial(
                joined_kernel, kernel, second, (len(ins), len(more_ins)), (len(outs), len(more_outs))
            ),
            outs + more_outs,
            (tables, rates, tables, rates, *ins, *more_ins),
            smem=4,
            scratch=scratch + [state],
        )

    down_23 = (False, 1, table_at(2, DOWN_SEND), 0, False)
    up_32 = (False, 0, table_at(3, UP_SEND), 0, False)
    extras = {
        1: (False, 0, table_at(1, DOWN_SEND)),
        2: (False, 1, table_at(0, DOWN_SEND)),
        3: (True, 1, table_at(2, UP_SEND)),
    }
    picks = {
        1: [up_32],
        2: [down_23],
        3: [up_32],
        4: [down_23],
        5: [
            up_32,
            (True, 0, table_at(1, DOWN_SEND), UNIT, False),
            (True, 0, table_at(1, UP_SEND), 2 * UNIT, True),
        ],
        6: [down_23, (False, 1, table_at(2, UP_SEND), UNIT, True)],
        7: [(False, 0, table_at(3, UP_SEND), 0, True)],
    }
    units = {1: 48, 2: 48, 3: 48, 4: 24, 5: 64, 6: 40, 7: 16}
    for step in range(1, 8):
        odd = step % 2 == 1
        if odd:
            takes = [taken(step - 1, 0, 0, 3, DOWN_RECV)]
        else:
            takes = [taken(step - 1, 0, 1, 2, UP_RECV)]
            if step == 6:
                takes.append(taken(5, UNIT, 1, 2, DOWN_RECV))
            elif step == 2:
                takes.append(taken(1, UNIT, 1, 2, DOWN_RECV))
        carried = step == 5
        work, edge, low, high = edges(
            s, wall_s, (3, 2), takes, odd, (t_low, t_high) if carried else ()
        )
        front, behind = trade_planes(low, high)
        extra = extras.get(step)
        ahead = []
        if odd:
            ahead.append(taken(step - 1, 0, 0, 3, DOWN_RECV))
            if step in (3, 7):
                ahead.append(taken(1 if step == 3 else 5, UNIT, 1, 2, DOWN_RECV))
        join = None
        if step == 7:
            couplings = [
                (0, table_at(1, DOWN_RECV), 0, units[2], UNIT, False),
                (1, table_at(0, UP_RECV), 1, units[5], 2 * UNIT, True),
                (0, table_at(1, UP_RECV), 2, units[6], UNIT, True),
            ]
            join = (
                functools.partial(other_last_kernel, couplings),
                (t, got[2], got[5], got[6]),
                [(Q * WIDTH, DEPTH)] * LEVELS,
            )
        seen, *rows = inside(work, wall_s, edge, (3, 2), s if odd else None, extra, t, ahead, join)
        following = [rows.pop(0)] if ahead else []
        if join:
            packed, rows = rows, []
        if step == 4:
            takes = [taken(2, UNIT, 0, 1, DOWN_RECV), taken(3, UNIT, 0, 1, UP_RECV)]
            t_work, t_edge, t_low, t_high = edges(t, wall_t, (1, 0), takes, True)
            seen, t_work, t_edge, t_low, t_high = lax.optimization_barrier(
                (seen, t_work, t_edge, t_low, t_high)
            )
        if step == 5:
            (t,) = inside(t_work, wall_t, t_edge, (1, 0), t)
        unit = units[step]
        ins = [tables, front, behind] + ([coupled] if ahead else [])
        outs, aliases = [], {}
        for value in (seen, *rows, *following, *([t] if carried else [])):
            if value is seen or rows:
                slot = len(outs)
            else:
                slot = len(outs) + 1 if len(outs) == 1 else len(outs)
            if slot == 2 and len(outs) == 1:
                outs.append((PEERS * unit, DEPTH))
            aliases[len(ins)] = slot
            outs.append(value.shape)
            ins.append(value)
        if len(outs) == 1:
            outs.append((PEERS * unit, DEPTH))
        s, got[step], *others = call(
            functools.partial(
                rest_kernel, odd, picks[step], unit, carried, bool(ahead), len(ins) - 3
            ),
            outs,
            ins,
            smem=1,
            aliases=aliases,
        )
        if ahead:
            s = others.pop(0)
        if carried:
            (t,) = others
        got[step] = trade_rows(got[step])

    couplings = [(1, table_at(2, UP_RECV), 0, units[7], 0, True)]
    packed = call(
        functools.partial(last_kernel, couplings),
        [(Q * WIDTH, DEPTH)] * LEVELS,
        (tables, rates, s, got[7], *packed),
        smem=2,
        scratch=[state],
        aliases={4 + i: i for i in range(LEVELS)},
    )
    parts = [packed[0]] + [
        lax.ppermute(packed[by], "lvl", [(i, (i + by) % LEVELS) for i in range(LEVELS)])
        for by in range(1, LEVELS)
    ]
    (final,) = call(output_kernel, [(Q * ROWS, DEPTH)], (tables, *parts), smem=1)
    final = jnp.transpose(final.reshape(Q, ROWS, DEPTH), (1, 0, 2))
    return final.reshape(1, PLANES, WIDTH, Q, DEPTH)


def solution(mesh):
    return jax.shard_map(
        on_device,
        mesh=mesh,
        in_specs=(
            P("lvl", "gx", None, None, None),
            P("lvl", "gx", None, None),
            P("lvl"),
            P("lvl", "gx", None, None),
            P("lvl", "gx", None, None),
            P("lvl", "gx", None, None),
            P("lvl", "gx", None, None),
        ),
        out_specs=P("lvl", "gx", None, None, None),
        check_vma=False,
    )
```

```python
import functools

import jax
import jax.numpy as jnp
from jax import lax
from jax.experimental import pallas as pl
from jax.experimental.pallas import tpu as pltpu
from jax.sharding import PartitionSpec as P

Q = 27
PLANES = 4
WIDTH = 32
ROWS = PLANES * WIDTH
DEPTH = 128
PEERS = 32
LEVELS = 4
HALF = 64
OWN = 32
GHOST = 16
PITCH = 136
QPAD = 32
STATE = QPAD * PITCH
UNIT = 24
NARROW = 16
BLOCKS = 9 * WIDTH // 8
GROUPS = 7
META = 8
WINDOW = 3 * GROUPS * HALF + META

VMEM = pl.BlockSpec(memory_space=pltpu.VMEM)
SMEM = pl.BlockSpec(memory_space=pltpu.SMEM)

DOWN_SEND, DOWN_RECV, UP_SEND, UP_RECV = range(4)
ME = 4 * 2 * PEERS
LEVEL_TABLES = ME + DEPTH


def table_at(level, which):
    return level * LEVEL_TABLES + which * 2 * PEERS


def call(kernel, outs, ins, smem=0, scratch=(), aliases=None):
    moved = sum(value.size for value in ins) + sum(rows * depth for rows, depth in outs)
    return pl.pallas_call(
        kernel,
        out_shape=[jax.ShapeDtypeStruct(shape, jnp.float32) for shape in outs],
        in_specs=[SMEM] * smem + [VMEM] * (len(ins) - smem),
        out_specs=[VMEM] * len(outs),
        scratch_shapes=[pltpu.VMEM(shape, jnp.float32) for shape in scratch],
        input_output_aliases=aliases or {},
        cost_estimate=pl.CostEstimate(
            flops=10 * moved, bytes_accessed=4 * moved, transcendentals=0
        ),
        compiler_params=pltpu.CompilerParams(vmem_limit_bytes=14 * 1024 * 1024),
    )(*ins)


def lanes_of(shape):
    return lax.broadcasted_iota(jnp.int32, shape, 1)


def in_half(shape, half):
    lanes = lanes_of(shape)
    return lanes < HALF if half == 0 else lanes >= HALF


def turn(value, shift, axis):
    size = value.shape[axis]
    shift = shift % size
    return value if shift == 0 else pltpu.roll(value, shift, axis)


def gaps(shape):
    lanes = lanes_of(shape)
    return (lanes >= 56) & (lanes < 72), (lanes < 8) | (lanes >= 120)


def fold(t0, t1, t2, extra):
    return fold_turned(t0, t1, t2, *(turn(extra, shift, 1) for shift in (16, 48, 96)))


def fold_turned(t0, t1, t2, e16, e48, e96):
    inner, outer = gaps(t0.shape)
    return (
        jnp.where(inner, e48, jnp.where(outer, e96, t0)),
        jnp.where(inner, e16, jnp.where(outer, e48, t1)),
        jnp.where(inner, e96, jnp.where(outer, e16, t2)),
    )


def unfold(t0, t1, t2):
    inner, _ = gaps(t0.shape)
    e48 = turn(jnp.where(inner, t0, t1), -48, 1)
    e96 = turn(jnp.where(inner, t2, t0), -96, 1)
    e16 = turn(jnp.where(inner, t1, t2), -16, 1)
    spot = lanes_of(t0.shape) & (HALF - 1)
    return jnp.where(spot < 24, e48, jnp.where(spot < 40, e96, e16))


def fold_own(m0, m1, m2, m3):
    quarter = lanes_of(m0.shape) // OWN

    def join(a, b):
        return jnp.where(
            quarter < 2,
            jnp.where(quarter == 0, turn(a, -16, 1), turn(a, -48, 1)),
            jnp.where(quarter == 2, turn(b, 48, 1), turn(b, 16, 1)),
        )

    return join(m0, m1), join(m2, m3)


def unfold_own(t0, t1):
    left = in_half(t0.shape, 0)
    out = []
    for value in (t0, t1):
        out.append(jnp.where(left, turn(value, 16, 1), turn(value, 48, 1)))
        out.append(jnp.where(left, turn(value, -48, 1), turn(value, -16, 1)))
    return out


def collide(f, wall, rate):
    t, d = [], []
    for pair in range(9):
        low, mid, high = f[3 * pair : 3 * pair + 3]
        t.append(low + high + 4.0 * mid)
        d.append(high - low)
    total, along_y, along_z = [], [], []
    for a in range(3):
        total.append(t[3 * a] + t[3 * a + 2] + 4.0 * t[3 * a + 1])
        along_y.append(t[3 * a + 2] - t[3 * a])
        along_z.append(d[3 * a] + d[3 * a + 2] + 4.0 * d[3 * a + 1])
    mass = total[0] + total[2] + 4.0 * total[1]
    inverse = 3.0 / mass
    ux = (total[2] - total[0]) * inverse
    uy = (along_y[0] + along_y[2] + 4.0 * along_y[1]) * inverse
    uz = (along_z[0] + along_z[2] + 4.0 * along_z[1]) * inverse
    scaled = rate * mass * (1.0 / 216.0)
    half = 0.5 * scaled
    base = scaled - scaled * ((ux * ux + uy * uy + uz * uz) * (1.0 / 6.0))
    keep = 1.0 - rate
    sums = {
        (0, 0, 1): uz,
        (0, 1, 0): uy,
        (1, 0, 0): ux,
        (0, 1, -1): uy - uz,
        (0, 1, 1): uy + uz,
        (1, 0, -1): ux - uz,
        (1, 0, 1): ux + uz,
        (1, -1, 0): ux - uy,
        (1, 1, 0): ux + uy,
    }
    for b in (-1, 1):
        for e in (-1, 1):
            sums[(1, b, e)] = sums[(1, b, 0)] + uz if e == 1 else sums[(1, b, 0)] - uz
    out = [None] * Q
    out[13] = jnp.where(wall, f[13], keep * f[13] + base)
    for (a, b, e), along in sums.items():
        i = 9 * (a + 1) + 3 * (b + 1) + (e + 1)
        j = 26 - i
        part = half * along
        odd = part + part
        even = base + part * along
        out[i] = jnp.where(wall, f[j], keep * f[i] + (even + odd))
        out[j] = jnp.where(wall, f[i], keep * f[j] + (even - odd))
    return out


def collide_rows(load, wall_ref, rate, store, tiles):
    def tile(i, carry):
        row = pl.multiple_of(tiles(i) * 8, 8)
        wall = wall_ref[pl.ds(row, 8), :] > 0.5
        out = collide([load(q, row) for q in range(Q)], wall, rate)
        for q in range(Q):
            store(q, row, turn(out[q], q % 3 - 1, 1))
        return carry

    lax.fori_loop(0, ROWS // 16, tile, 0, unroll=4)


def edge_tiles(i):
    return jnp.where(i < 4, i, i + 8)


def inner_tiles(i):
    return i + 4


def collide_edges(load, wall_ref, rate, edge_ref, low_ref, high_ref, halved=False):
    def store(q, row, value):
        at = jnp.where(row < WIDTH, row, row - 2 * WIDTH)
        edge_ref[pl.ds(pl.multiple_of(q * HALF + at, 8), 8), :] = value

    collide_rows(load, wall_ref, rate, store, edge_tiles)

    def block(first, i):
        return edge_ref[pl.ds(first + i // 4 * HALF + i % 4 * 8, 8), :]

    for ref, first in ((low_ref, 0), (high_ref, 18 * HALF + WIDTH)):
        if halved:
            for i in range(BLOCKS // 2):
                ref[pl.ds(8 * i, 8), :] = jnp.where(
                    in_half((8, DEPTH), 0),
                    block(first, i),
                    turn(block(first, i + BLOCKS // 2), HALF, 1),
                )
        else:
            for i in range(BLOCKS):
                ref[pl.ds(8 * i, 8), :] = block(first, i)


def collide_inside(load, wall_ref, rate, inside_ref):
    def store(q, row, value):
        inside_ref[pl.ds(pl.multiple_of(q * HALF + row - WIDTH, 8), 8), :] = value

    collide_rows(load, wall_ref, rate, store, inner_tiles)


def stream_known(edge_ref, inside_ref, read_ref, pitch, old_ref, next_ref=None):
    for q in range(Q):
        for plane in range(PLANES):
            source = plane - (q // 9 - 1)
            spot = pl.ds(q * pitch + plane * WIDTH, WIDTH)
            if 0 <= source < PLANES:
                if source in (0, PLANES - 1):
                    value = edge_ref[pl.ds(q * HALF + (WIDTH if source else 0), WIDTH), :]
                else:
                    value = inside_ref[pl.ds(q * HALF + (source - 1) * WIDTH, WIDTH), :]
                value = turn(value, q // 3 % 3 - 1, 0)
                if old_ref is not None:
                    value = jnp.where(in_half((WIDTH, DEPTH), 0), value, old_ref[spot, :])
            elif old_ref is not None:
                value = old_ref[spot, :]
            else:
                continue
            read_ref[spot, :] = value
            if next_ref is not None:
                next_ref[spot, :] = value


def stream_rest(
    front_ref, behind_ref, read_ref, pitch, keep, start=0, next_ref=None, taken_ref=None, halved=False
):
    def block(ref, i):
        if halved and i >= BLOCKS // 2:
            return turn(ref[pl.ds(start + 8 * i - 4 * BLOCKS, 8), :], HALF, 1)
        return ref[pl.ds(start + 8 * i, 8), :]

    for q in range(9):
        for velocity, plane, ref in ((q, PLANES - 1, front_ref), (q + 18, 0, behind_ref)):
            spot = pl.ds(velocity * pitch + plane * WIDTH, WIDTH)
            value = jnp.concatenate([block(ref, 4 * q + i) for i in range(4)], axis=0)
            value = turn(value, q // 3 - 1, 0)
            if keep:
                value = jnp.where(in_half((WIDTH, DEPTH), 0), value, read_ref[spot, :])
            read_ref[spot, :] = value
            if next_ref is not None:
                placed = taken_ref[pl.ds(plane * WIDTH, WIDTH), :] > 0.5
                free = in_half((WIDTH, DEPTH), 0) & jnp.logical_not(placed)
                next_ref[spot, :] = jnp.where(free, value, next_ref[spot, :])


def pick_rows(state_ref, half, tables_ref, at, out_ref, unit, offset, narrow=False):
    group = 16

    def some(g, carry):
        for j in range(group):
            peer = g * group + j
            first = jnp.maximum(tables_ref[at + 2 * peer], 0)
            second = jnp.maximum(tables_ref[at + 2 * peer + 1], 0)
            merged = []
            for c in range(QPAD // 8):
                one = state_ref[pl.ds(first + c * 8 * PITCH, 8, stride=PITCH), :]
                two = state_ref[pl.ds(second + c * 8 * PITCH, 8, stride=PITCH), :]
                if half == 0:
                    two = turn(two, HALF, 1)
                else:
                    one = turn(one, HALF, 1)
                merged.append(jnp.where(in_half((8, DEPTH), 0), one, two))
            for c, value in enumerate((fold_own if narrow else fold)(*merged)):
                spot = pl.multiple_of(peer * unit + offset + 8 * c, 8)
                out_ref[pl.ds(spot, 8), :] = value
        return carry

    lax.fori_loop(0, PEERS // group, some, 0)


def place_rows(state_ref, half, tables_ref, at, in_ref, unit, offset, narrow=False):
    group = 16

    def some(g, carry):
        stores = []
        for j in range(group):
            peer = g * group + j
            parts = [
                in_ref[pl.ds(pl.multiple_of(peer * unit + offset + 8 * c, 8), 8), :]
                for c in range(2 if narrow else 3)
            ]
            parts = unfold_own(*parts) if narrow else parts + [unfold(*parts)]
            for k in range(2):
                row = tables_ref[at + 2 * peer + k]
                row = jnp.where(row < 0, ROWS, row)
                for c, value in enumerate(parts):
                    if k != half:
                        value = turn(value, HALF, 1)
                    where = pl.ds(row + c * 8 * PITCH, 8, stride=PITCH)
                    stores.append(
                        (where, jnp.where(in_half((8, DEPTH), half), value, state_ref[where, :]))
                    )
        for where, value in stores:
            state_ref[where, :] = value
        return carry

    lax.fori_loop(0, PEERS // group, some, 0)


def copy_state(source_ref, target_ref):
    def one(q, carry):
        at = pl.multiple_of(q * PITCH, 8)
        target_ref[pl.ds(at, ROWS), :] = source_ref[pl.ds(at, ROWS), :]
        return carry

    lax.fori_loop(0, Q, one, 0)


def pair_rate(rates_ref, first, second):
    return jnp.where(in_half((8, DEPTH), 0), rates_ref[first], rates_ref[second])


def first_edges_kernel(rate_ref, x_ref, wall_ref, edge_ref, low_ref, high_ref):
    rate = jnp.full((8, DEPTH), rate_ref[0], jnp.float32)

    def load(q, row):
        return x_ref[pl.ds(q * ROWS + row, 8), :]

    collide_edges(load, wall_ref, rate, edge_ref, low_ref, high_ref)


def first_inside_kernel(rate_ref, x_ref, wall_ref, edge_ref, read_ref, inside_ref):
    rate = jnp.full((8, DEPTH), rate_ref[0], jnp.float32)

    def load(q, row):
        return x_ref[pl.ds(q * ROWS + row, 8), :]

    collide_inside(load, wall_ref, rate, inside_ref)
    stream_known(edge_ref, inside_ref, read_ref, ROWS, None)
    read_ref[pl.ds(Q * ROWS, ROWS), :] = wall_ref[...].astype(jnp.float32)


def windows_kernel(seen_ref, front_ref, behind_ref, meta_ref, out_ref, read_ref):
    stream_rest(front_ref, behind_ref, read_ref, ROWS, False)

    def some(g, carry):
        lanes = lanes_of((8, DEPTH))
        for row in range(0, HALF, 8):
            mixed = []
            for j in range(4):
                at = pl.multiple_of((4 * g + j) * ROWS + row, 8)
                top = read_ref[pl.ds(at, 8), :]
                bottom = turn(read_ref[pl.ds(at + HALF, 8), :], HALF, 1)
                mixed.append(
                    [
                        jnp.where(((lanes + GHOST - OWN * k) & (DEPTH - 1)) < HALF, top, bottom)
                        for k in range(LEVELS)
                    ]
                )
            for target in range(LEVELS):
                shift = GHOST - OWN * target
                main = [turn(mixed[j][target], shift, 1) for j in range(3)]
                extra = [turn(mixed[3][target], shift + by, 1) for by in (16, 48, 96)]
                for j, value in enumerate(fold_turned(*main, *extra)):
                    at = pl.multiple_of(target * WINDOW + (3 * g + j) * HALF + row, 8)
                    out_ref[pl.ds(at, 8), :] = value
        return carry

    lax.fori_loop(0, GROUPS, some, 0)
    for target in range(LEVELS):
        at = (target + 1) * WINDOW - META
        out_ref[pl.ds(at, META), :] = meta_ref[...]
        out_ref[pl.ds(at + 2, 1), :] = jnp.full((1, DEPTH), target, jnp.float32)


def unpack_pair(in_ref, state_ref, wall_ref, first, second):
    def some(g, carry):
        left = in_half((8, DEPTH), 0)
        for row in range(0, HALF, 8):
            parts = []
            for level in (first, second):
                at = pl.multiple_of(level * WINDOW + 3 * g * HALF + row, 8)
                three = [in_ref[pl.ds(at + j * HALF, 8), :] for j in range(3)]
                parts.append(three + [unfold(*three)])
            for j in range(4):
                one, two = parts[0][j], parts[1][j]
                crossed = turn(jnp.where(left, two, one), HALF, 1)
                at = pl.multiple_of((4 * g + j) * PITCH + row, 8)
                state_ref[pl.ds(at, 8), :] = jnp.where(left, one, crossed)
                state_ref[pl.ds(at + HALF, 8), :] = jnp.where(left, crossed, two)
        return carry

    lax.fori_loop(0, GROUPS, some, 0)
    wall_ref[...] = state_ref[pl.ds(Q * PITCH, ROWS), :]


def unpack_kernel(tables_ref, rates_ref, in_ref, s_ref, wall_ref, rows_ref):
    unpack_pair(in_ref, s_ref, wall_ref, 3, 2)
    pick_rows(s_ref, 1, tables_ref, table_at(2, DOWN_SEND), rows_ref, UNIT, 0)


def unpack_other_kernel(tables_ref, rates_ref, in_ref, low_ref, t_ref, wall_ref, taken_ref):
    unpack_pair(in_ref, t_ref, wall_ref, 1, 0)
    taken_ref[...] = jnp.zeros((PITCH, DEPTH), jnp.float32)

    def mark(j, carry):
        row = tables_ref[table_at(3, DOWN_RECV) + j]
        spot = pl.ds(jnp.where(row < 0, ROWS, row), 1)
        taken_ref[spot, :] = jnp.where(in_half((1, DEPTH), 0), 1.0, 0.0)
        return carry

    lax.fori_loop(0, 2 * PEERS, mark, 0, unroll=8)


def apply(state_ref, couplings, tables_ref, buffers):
    for half, at, index, unit, offset, narrow in couplings:
        place_rows(state_ref, half, tables_ref, at, buffers[index], unit, offset, narrow)


def edges_kernel(levels, couplings, buffers, carried, halved, tables_ref, rates_ref, *refs):
    refs = list(refs)[1:]
    wall_ref = refs.pop(0)
    in_refs = [refs.pop(0) for _ in range(buffers)]
    other_refs = [refs.pop(0) for _ in range(2)] if carried else []
    work_ref, edge_ref, low_ref, high_ref = refs
    apply(work_ref, couplings, tables_ref, in_refs)

    def load(q, row):
        return work_ref[pl.ds(q * PITCH + row, 8), :]

    rate = pair_rate(rates_ref, *levels)
    collide_edges(load, wall_ref, rate, edge_ref, low_ref, high_ref, halved)
    for source, target in zip(other_refs, (low_ref, high_ref)):
        target[pl.ds(4 * BLOCKS, 4 * BLOCKS), :] = source[...]


def inside_kernel(levels, keep, extra, couplings, buffers, tables_ref, rates_ref, *refs):
    refs = list(refs)
    work_ref, wall_ref, edge_ref = refs.pop(0), refs.pop(0), refs.pop(0)
    old_ref = work_ref if keep else None
    other_ref = refs.pop(0) if extra and not extra[0] else None
    in_refs = [refs.pop(0) for _ in range(buffers)]
    inside_ref = refs.pop()
    read_ref = refs.pop(0)
    next_ref = refs.pop(0) if couplings else None

    def load(q, row):
        return work_ref[pl.ds(q * PITCH + row, 8), :]

    collide_inside(load, wall_ref, pair_rate(rates_ref, *levels), inside_ref)
    stream_known(edge_ref, inside_ref, read_ref, PITCH, old_ref, next_ref)
    apply(next_ref, couplings, tables_ref, in_refs)
    if extra:
        own, half, at = extra
        source = old_ref if own else other_ref
        pick_rows(source, half, tables_ref, at, refs.pop(0), 2 * UNIT, UNIT)


def joined_kernel(first, second, ins, outs, *refs):
    refs = list(refs)
    scalars = [[refs.pop(0), refs.pop(0)] for _ in range(2)]
    inputs = [[refs.pop(0) for _ in range(count)] for count in ins]
    outputs = [[refs.pop(0) for _ in range(count)] for count in outs]
    for i, kernel in enumerate((first, second)):
        kernel(*scalars[i], *inputs[i], *outputs[i], refs[i])


def rest_kernel(keep, picks, unit, carried, ahead, inputs, tables_ref, front_ref, behind_ref, *refs):
    taken_ref = refs[0] if ahead else None
    refs = list(refs)[inputs:]
    seen_ref, rows_ref = refs.pop(0), refs.pop(0)
    next_ref = refs.pop(0) if ahead else None
    other_ref = refs.pop(0) if carried else None
    stream_rest(
        front_ref, behind_ref, seen_ref, PITCH, keep, 0, next_ref, taken_ref, halved=keep
    )
    if carried:
        stream_rest(front_ref, behind_ref, other_ref, PITCH, True, 4 * BLOCKS, halved=True)
    for other, half, at, offset, narrow in picks:
        source = other_ref if other else seen_ref
        pick_rows(source, half, tables_ref, at, rows_ref, unit, offset, narrow)


def pack_level(work_ref, half, out_ref):
    def one(q, carry):
        chunk = lanes_of((8, DEPTH)) // OWN
        for row in range(0, WIDTH, 8):
            packed = None
            for plane in range(PLANES):
                at = pl.multiple_of(q * PITCH + plane * WIDTH + row, 8)
                value = turn(work_ref[pl.ds(at, 8), :], OWN * plane - HALF * half - GHOST, 1)
                packed = value if packed is None else jnp.where(chunk == plane, value, packed)
            out_ref[pl.ds(pl.multiple_of(q * WIDTH + row, 8), 8), :] = packed
        return carry

    lax.fori_loop(0, Q, one, 0, unroll=9)


def pack_levels(tables_ref, work_ref, levels, out_refs):
    for me in range(LEVELS):

        @pl.when(tables_ref[ME] == me)
        def _():
            for half, level in levels:
                pack_level(work_ref, half, out_refs[(level - me) % LEVELS])


def other_last_kernel(couplings, tables_ref, rates_ref, state_ref, b2, b5, b6, *refs):
    out_refs, work_ref = refs[:-1], refs[-1]
    copy_state(state_ref, work_ref)
    apply(work_ref, couplings, tables_ref, (b2, b5, b6))
    pack_levels(tables_ref, work_ref, ((1, 0), (0, 1)), out_refs)


def last_kernel(couplings, tables_ref, rates_ref, state_ref, b7, *refs):
    out_refs, work_ref = refs[LEVELS:-1], refs[-1]
    copy_state(state_ref, work_ref)
    apply(work_ref, couplings, tables_ref, (b7,))
    pack_levels(tables_ref, work_ref, ((1, 2), (0, 3)), out_refs)


def output_kernel(tables_ref, *refs):
    in_refs, out_ref = refs[:-1], refs[-1]
    chunk = lanes_of((WIDTH, DEPTH)) // OWN
    for me in range(LEVELS):

        @pl.when(tables_ref[ME] == me)
        def _():
            def one(q, carry):
                parts = [
                    in_refs[(me - c) % LEVELS][pl.ds(pl.multiple_of(q * WIDTH, 8), WIDTH), :]
                    for c in range(LEVELS)
                ]
                for plane in range(PLANES):
                    whole = None
                    for c in range(LEVELS):
                        value = turn(parts[c], OWN * (c - plane), 1)
                        whole = value if whole is None else jnp.where(chunk == c, value, whole)
                    out_ref[pl.ds(pl.multiple_of(q * ROWS + plane * WIDTH, 8), WIDTH), :] = whole
                return carry

            lax.fori_loop(0, Q, one, 0, unroll=3)


def trade_planes(low, high):
    count = lax.axis_size("gx")
    forward = [(i, (i + 1) % count) for i in range(count)]
    backward = [(target, source) for source, target in forward]
    return lax.ppermute(low, "gx", backward), lax.ppermute(high, "gx", forward)


def trade_rows(rows):
    blocks = rows.reshape(PEERS, -1, DEPTH)
    return lax.all_to_all(blocks, "gx", split_axis=0, concat_axis=0, tiled=True).reshape(
        rows.shape
    )


def on_device(populations, solid_mask, relax_rates, down_send, down_recv, up_send, up_recv):
    meta = jnp.concatenate(
        [value.reshape(-1) for value in (down_send, down_recv, up_send, up_recv)]
    ).astype(jnp.float32)
    meta = jnp.concatenate([meta, jnp.broadcast_to(relax_rates, (META * DEPTH - meta.size,))])
    meta = meta.reshape(META, DEPTH)
    x = jnp.transpose(populations.reshape(ROWS, Q, DEPTH), (1, 0, 2)).reshape(Q * ROWS, DEPTH)
    wall = solid_mask.reshape(ROWS, DEPTH)
    flow = [(Q * ROWS, DEPTH), (9 * WIDTH, DEPTH), (9 * WIDTH, DEPTH)]
    state = (STATE, DEPTH)

    edge, low, high = call(
        first_edges_kernel, [(Q * HALF, DEPTH), *flow[1:]], (relax_rates, x, wall), smem=1
    )
    front, behind = trade_planes(low, high)
    (seen,) = call(
        first_inside_kernel,
        [((Q + 1) * ROWS, DEPTH)],
        (relax_rates, x, wall, edge),
        smem=1,
        scratch=[(Q * HALF, DEPTH)],
    )
    windows, _ = call(
        windows_kernel,
        [(LEVELS * WINDOW, DEPTH), ((Q + 1) * ROWS, DEPTH)],
        (seen, front, behind, meta),
        aliases={0: 1},
    )
    windows = lax.all_to_all(
        windows.reshape(LEVELS, WINDOW, DEPTH), "lvl", 0, 0, tiled=True
    )
    tables = windows[:, WINDOW - META : WINDOW - META + 3, :].astype(jnp.int32).reshape(-1)
    rates = windows[:, WINDOW - 1, 0]
    windows = windows.reshape(-1, DEPTH)
    s, wall_s, rows = call(
        unpack_kernel,
        [state, (ROWS, DEPTH), (PEERS * UNIT, DEPTH)],
        (tables, rates, windows),
        smem=2,
    )
    got = {0: trade_rows(rows)}

    def taken(step, offset, half, level, which, narrow=False):
        buffer = got[step]
        return buffer, half, table_at(level, which), buffer.shape[0] // PEERS, offset, narrow

    def gather_takes(takes):
        buffers, couplings = [], []
        for buffer, half, at, unit, offset, narrow in takes:
            index = next((i for i, b in enumerate(buffers) if b is buffer), len(buffers))
            if index == len(buffers):
                buffers.append(buffer)
            couplings.append((half, at, index, unit, offset, narrow))
        return buffers, couplings

    def edges(value, walls, levels, takes, halved, carried=()):
        buffers, couplings = gather_takes(takes)
        planes = (8 * BLOCKS // (1 if carried or not halved else 2), DEPTH)
        return call(
            functools.partial(
                edges_kernel, levels, couplings, len(buffers), bool(carried), halved
            ),
            [state, (Q * HALF, DEPTH), planes, planes],
            (tables, rates, value, walls, *buffers, *carried),
            smem=2,
            aliases={2: 0},
        )

    def inside(work, walls, edge, levels, keep, extra=None, other=None, takes=(), join=None):
        buffers, couplings = gather_takes(takes)
        ins = [work, walls, edge]
        ins += [other] if extra and not extra[0] else []
        ins += buffers
        kernel = functools.partial(
            inside_kernel, levels, keep, extra, couplings, len(buffers)
        )
        outs = [state] * (2 if takes else 1) + ([(PEERS * 2 * UNIT, DEPTH)] if extra else [])
        scratch = [(Q * HALF, DEPTH)]
        if join is None:
            return call(kernel, outs, (tables, rates, *ins), smem=2, scratch=scratch)
        second, more_ins, more_outs = join
        return call(
            functools.partial(
                joined_kernel, kernel, second, (len(ins), len(more_ins)), (len(outs), len(more_outs))
            ),
            outs + more_outs,
            (tables, rates, tables, rates, *ins, *more_ins),
            smem=4,
            scratch=scratch + [state],
        )

    down_23 = (False, 1, table_at(2, DOWN_SEND), 0, False)
    up_32 = (False, 0, table_at(3, UP_SEND), 0, False)
    extras = {
        1: (False, 0, table_at(1, DOWN_SEND)),
        2: (False, 1, table_at(0, DOWN_SEND)),
        3: (True, 1, table_at(2, UP_SEND)),
    }
    picks = {
        1: [up_32],
        2: [down_23],
        3: [up_32],
        4: [down_23],
        5: [
            up_32,
            (True, 0, table_at(1, DOWN_SEND), UNIT, False),
            (True, 0, table_at(1, UP_SEND), 2 * UNIT, True),
        ],
        6: [down_23, (False, 1, table_at(2, UP_SEND), UNIT, True)],
        7: [(False, 0, table_at(3, UP_SEND), 0, True)],
    }
    units = {1: 48, 2: 48, 3: 48, 4: 24, 5: 64, 6: 40, 7: 16}
    for step in range(1, 8):
        odd = step % 2 == 1
        if odd:
            takes = [taken(step - 1, 0, 0, 3, DOWN_RECV)]
        else:
            takes = [taken(step - 1, 0, 1, 2, UP_RECV)]
            if step == 6:
                takes.append(taken(5, UNIT, 1, 2, DOWN_RECV))
            elif step == 2:
                takes.append(taken(1, UNIT, 1, 2, DOWN_RECV))
        carried = step == 5
        work, edge, low, high = edges(
            s, wall_s, (3, 2), takes, odd, (t_low, t_high) if carried else ()
        )
        front, behind = trade_planes(low, high)
        if step == 1:
            t, wall_t, coupled = call(
                unpack_other_kernel,
                [state, (ROWS, DEPTH), (PITCH, DEPTH)],
                (tables, rates, windows, low),
                smem=2,
            )
        extra = extras.get(step)
        ahead = []
        if odd:
            ahead.append(taken(step - 1, 0, 0, 3, DOWN_RECV))
            if step in (3, 7):
                ahead.append(taken(1 if step == 3 else 5, UNIT, 1, 2, DOWN_RECV))
        join = None
        if step == 7:
            couplings = [
                (0, table_at(1, DOWN_RECV), 0, units[2], UNIT, False),
                (1, table_at(0, UP_RECV), 1, units[5], 2 * UNIT, True),
                (0, table_at(1, UP_RECV), 2, units[6], UNIT, True),
            ]
            join = (
                functools.partial(other_last_kernel, couplings),
                (t, got[2], got[5], got[6]),
                [(Q * WIDTH, DEPTH)] * LEVELS,
            )
        seen, *rows = inside(work, wall_s, edge, (3, 2), odd, extra, t, ahead, join)
        following = [rows.pop(0)] if ahead else []
        if join:
            packed, rows = rows, []
        if step == 4:
            takes = [taken(2, UNIT, 0, 1, DOWN_RECV), taken(3, UNIT, 0, 1, UP_RECV)]
            t_work, t_edge, t_low, t_high = edges(t, wall_t, (1, 0), takes, True)
            seen, t_work, t_edge, t_low, t_high = lax.optimization_barrier(
                (seen, t_work, t_edge, t_low, t_high)
            )
        if step == 5:
            (t,) = inside(t_work, wall_t, t_edge, (1, 0), True)
        unit = units[step]
        ins = [tables, front, behind] + ([coupled] if ahead else [])
        outs, aliases = [], {}
        for value in (seen, *rows, *following, *([t] if carried else [])):
            if value is seen or rows:
                slot = len(outs)
            else:
                slot = len(outs) + 1 if len(outs) == 1 else len(outs)
            if slot == 2 and len(outs) == 1:
                outs.append((PEERS * unit, DEPTH))
            aliases[len(ins)] = slot
            outs.append(value.shape)
            ins.append(value)
        if len(outs) == 1:
            outs.append((PEERS * unit, DEPTH))
        s, got[step], *others = call(
            functools.partial(
                rest_kernel, odd, picks[step], unit, carried, bool(ahead), len(ins) - 3
            ),
            outs,
            ins,
            smem=1,
            aliases=aliases,
        )
        if ahead:
            s = others.pop(0)
        if carried:
            (t,) = others
        got[step] = trade_rows(got[step])

    couplings = [(1, table_at(2, UP_RECV), 0, units[7], 0, True)]
    packed = call(
        functools.partial(last_kernel, couplings),
        [(Q * WIDTH, DEPTH)] * LEVELS,
        (tables, rates, s, got[7], *packed),
        smem=2,
        scratch=[state],
        aliases={4 + i: i for i in range(LEVELS)},
    )
    parts = [packed[0]] + [
        lax.ppermute(packed[by], "lvl", [(i, (i + by) % LEVELS) for i in range(LEVELS)])
        for by in range(1, LEVELS)
    ]
    (final,) = call(output_kernel, [(Q * ROWS, DEPTH)], (tables, *parts), smem=1)
    final = jnp.transpose(final.reshape(Q, ROWS, DEPTH), (1, 0, 2))
    return final.reshape(1, PLANES, WIDTH, Q, DEPTH)


def solution(mesh):
    return jax.shard_map(
        on_device,
        mesh=mesh,
        in_specs=(
            P("lvl", "gx", None, None, None),
            P("lvl", "gx", None, None),
            P("lvl"),
            P("lvl", "gx", None, None),
            P("lvl", "gx", None, None),
            P("lvl", "gx", None, None),
            P("lvl", "gx", None, None),
        ),
        out_specs=P("lvl", "gx", None, None, None),
        check_vma=False,
    )
```

```python
import functools

import jax
import jax.numpy as jnp
from jax import lax
from jax.experimental import pallas as pl
from jax.experimental.pallas import tpu as pltpu
from jax.sharding import PartitionSpec as P

Q = 27
PLANES = 4
WIDTH = 32
ROWS = PLANES * WIDTH
DEPTH = 128
PEERS = 32
LEVELS = 4
HALF = 64
OWN = 32
GHOST = 16
PITCH = 136
QPAD = 32
STATE = QPAD * PITCH
UNIT = 24
NARROW = 16
BLOCKS = 9 * WIDTH // 8
GROUPS = 7
META = 8
WINDOW = 3 * GROUPS * HALF + META

VMEM = pl.BlockSpec(memory_space=pltpu.VMEM)
SMEM = pl.BlockSpec(memory_space=pltpu.SMEM)

DOWN_SEND, DOWN_RECV, UP_SEND, UP_RECV = range(4)
ME = 4 * 2 * PEERS
LEVEL_TABLES = ME + DEPTH


def table_at(level, which):
    return level * LEVEL_TABLES + which * 2 * PEERS


def call(kernel, outs, ins, smem=0, scratch=(), aliases=None):
    moved = sum(value.size for value in ins) + sum(rows * depth for rows, depth in outs)
    return pl.pallas_call(
        kernel,
        out_shape=[jax.ShapeDtypeStruct(shape, jnp.float32) for shape in outs],
        in_specs=[SMEM] * smem + [VMEM] * (len(ins) - smem),
        out_specs=[VMEM] * len(outs),
        scratch_shapes=[pltpu.VMEM(shape, jnp.float32) for shape in scratch],
        input_output_aliases=aliases or {},
        cost_estimate=pl.CostEstimate(
            flops=10 * moved, bytes_accessed=4 * moved, transcendentals=0
        ),
        compiler_params=pltpu.CompilerParams(vmem_limit_bytes=14 * 1024 * 1024),
    )(*ins)


def lanes_of(shape):
    return lax.broadcasted_iota(jnp.int32, shape, 1)


def in_half(shape, half):
    lanes = lanes_of(shape)
    return lanes < HALF if half == 0 else lanes >= HALF


def turn(value, shift, axis):
    size = value.shape[axis]
    shift = shift % size
    return value if shift == 0 else pltpu.roll(value, shift, axis)


def gaps(shape):
    lanes = lanes_of(shape)
    return (lanes >= 56) & (lanes < 72), (lanes < 8) | (lanes >= 120)


def fold(t0, t1, t2, extra):
    return fold_turned(t0, t1, t2, *(turn(extra, shift, 1) for shift in (16, 48, 96)))


def fold_turned(t0, t1, t2, e16, e48, e96):
    inner, outer = gaps(t0.shape)
    return (
        jnp.where(inner, e48, jnp.where(outer, e96, t0)),
        jnp.where(inner, e16, jnp.where(outer, e48, t1)),
        jnp.where(inner, e96, jnp.where(outer, e16, t2)),
    )


def unfold(t0, t1, t2):
    inner, _ = gaps(t0.shape)
    e48 = turn(jnp.where(inner, t0, t1), -48, 1)
    e96 = turn(jnp.where(inner, t2, t0), -96, 1)
    e16 = turn(jnp.where(inner, t1, t2), -16, 1)
    spot = lanes_of(t0.shape) & (HALF - 1)
    return jnp.where(spot < 24, e48, jnp.where(spot < 40, e96, e16))


def fold_own(m0, m1, m2, m3):
    quarter = lanes_of(m0.shape) // OWN

    def join(a, b):
        return jnp.where(
            quarter < 2,
            jnp.where(quarter == 0, turn(a, -16, 1), turn(a, -48, 1)),
            jnp.where(quarter == 2, turn(b, 48, 1), turn(b, 16, 1)),
        )

    return join(m0, m1), join(m2, m3)


def unfold_own(t0, t1):
    left = in_half(t0.shape, 0)
    out = []
    for value in (t0, t1):
        out.append(jnp.where(left, turn(value, 16, 1), turn(value, 48, 1)))
        out.append(jnp.where(left, turn(value, -48, 1), turn(value, -16, 1)))
    return out


def collide(f, wall, rate):
    t, d = [], []
    for pair in range(9):
        low, mid, high = f[3 * pair : 3 * pair + 3]
        t.append(low + high + 4.0 * mid)
        d.append(high - low)
    total, along_y, along_z = [], [], []
    for a in range(3):
        total.append(t[3 * a] + t[3 * a + 2] + 4.0 * t[3 * a + 1])
        along_y.append(t[3 * a + 2] - t[3 * a])
        along_z.append(d[3 * a] + d[3 * a + 2] + 4.0 * d[3 * a + 1])
    mass = total[0] + total[2] + 4.0 * total[1]
    inverse = 3.0 / mass
    ux = (total[2] - total[0]) * inverse
    uy = (along_y[0] + along_y[2] + 4.0 * along_y[1]) * inverse
    uz = (along_z[0] + along_z[2] + 4.0 * along_z[1]) * inverse
    scaled = rate * mass * (1.0 / 216.0)
    half = 0.5 * scaled
    base = scaled - scaled * ((ux * ux + uy * uy + uz * uz) * (1.0 / 6.0))
    keep = 1.0 - rate
    sums = {
        (0, 0, 1): uz,
        (0, 1, 0): uy,
        (1, 0, 0): ux,
        (0, 1, -1): uy - uz,
        (0, 1, 1): uy + uz,
        (1, 0, -1): ux - uz,
        (1, 0, 1): ux + uz,
        (1, -1, 0): ux - uy,
        (1, 1, 0): ux + uy,
    }
    for b in (-1, 1):
        for e in (-1, 1):
            sums[(1, b, e)] = sums[(1, b, 0)] + uz if e == 1 else sums[(1, b, 0)] - uz
    out = [None] * Q
    out[13] = jnp.where(wall, f[13], keep * f[13] + base)
    for (a, b, e), along in sums.items():
        i = 9 * (a + 1) + 3 * (b + 1) + (e + 1)
        j = 26 - i
        part = half * along
        odd = part + part
        even = base + part * along
        out[i] = jnp.where(wall, f[j], keep * f[i] + (even + odd))
        out[j] = jnp.where(wall, f[i], keep * f[j] + (even - odd))
    return out


def collide_rows(load, wall_ref, rate, store, tiles):
    def tile(i, carry):
        row = pl.multiple_of(tiles(i) * 8, 8)
        wall = wall_ref[pl.ds(row, 8), :] > 0.5
        out = collide([load(q, row) for q in range(Q)], wall, rate)
        for q in range(Q):
            store(q, row, turn(out[q], q % 3 - 1, 1))
        return carry

    lax.fori_loop(0, ROWS // 16, tile, 0, unroll=4)


def edge_tiles(i):
    return jnp.where(i < 4, i, i + 8)


def inner_tiles(i):
    return i + 4


def collide_edges(load, wall_ref, rate, edge_ref, low_ref, high_ref, halved=False):
    def store(q, row, value):
        at = jnp.where(row < WIDTH, row, row - 2 * WIDTH)
        edge_ref[pl.ds(pl.multiple_of(q * HALF + at, 8), 8), :] = value

    collide_rows(load, wall_ref, rate, store, edge_tiles)

    def block(first, i):
        return edge_ref[pl.ds(first + i // 4 * HALF + i % 4 * 8, 8), :]

    for ref, first in ((low_ref, 0), (high_ref, 18 * HALF + WIDTH)):
        if halved:
            for i in range(BLOCKS // 2):
                ref[pl.ds(8 * i, 8), :] = jnp.where(
                    in_half((8, DEPTH), 0),
                    block(first, i),
                    turn(block(first, i + BLOCKS // 2), HALF, 1),
                )
        else:
            for i in range(BLOCKS):
                ref[pl.ds(8 * i, 8), :] = block(first, i)


def collide_inside(load, wall_ref, rate, inside_ref):
    def store(q, row, value):
        inside_ref[pl.ds(pl.multiple_of(q * HALF + row - WIDTH, 8), 8), :] = value

    collide_rows(load, wall_ref, rate, store, inner_tiles)


def stream_known(edge_ref, inside_ref, read_ref, pitch, old_ref, next_ref=None):
    for q in range(Q):
        for plane in range(PLANES):
            source = plane - (q // 9 - 1)
            spot = pl.ds(q * pitch + plane * WIDTH, WIDTH)
            if 0 <= source < PLANES:
                if source in (0, PLANES - 1):
                    value = edge_ref[pl.ds(q * HALF + (WIDTH if source else 0), WIDTH), :]
                else:
                    value = inside_ref[pl.ds(q * HALF + (source - 1) * WIDTH, WIDTH), :]
                value = turn(value, q // 3 % 3 - 1, 0)
                if old_ref is not None:
                    value = jnp.where(in_half((WIDTH, DEPTH), 0), value, old_ref[spot, :])
            elif old_ref is not None:
                value = old_ref[spot, :]
            else:
                continue
            read_ref[spot, :] = value
            if next_ref is not None:
                next_ref[spot, :] = value


def stream_rest(
    front_ref, behind_ref, read_ref, pitch, keep, start=0, next_ref=None, taken_ref=None, halved=False
):
    def block(ref, i):
        if halved and i >= BLOCKS // 2:
            return turn(ref[pl.ds(start + 8 * i - 4 * BLOCKS, 8), :], HALF, 1)
        return ref[pl.ds(start + 8 * i, 8), :]

    for q in range(9):
        for velocity, plane, ref in ((q, PLANES - 1, front_ref), (q + 18, 0, behind_ref)):
            spot = pl.ds(velocity * pitch + plane * WIDTH, WIDTH)
            value = jnp.concatenate([block(ref, 4 * q + i) for i in range(4)], axis=0)
            value = turn(value, q // 3 - 1, 0)
            if keep:
                value = jnp.where(in_half((WIDTH, DEPTH), 0), value, read_ref[spot, :])
            read_ref[spot, :] = value
            if next_ref is not None:
                placed = taken_ref[pl.ds(plane * WIDTH, WIDTH), :] > 0.5
                free = in_half((WIDTH, DEPTH), 0) & jnp.logical_not(placed)
                next_ref[spot, :] = jnp.where(free, value, next_ref[spot, :])


def pick_rows(state_ref, half, tables_ref, at, out_ref, unit, offset, narrow=False):
    group = 16

    def some(g, carry):
        for j in range(group):
            peer = g * group + j
            first = jnp.maximum(tables_ref[at + 2 * peer], 0)
            second = jnp.maximum(tables_ref[at + 2 * peer + 1], 0)
            merged = []
            for c in range(QPAD // 8):
                one = state_ref[pl.ds(first + c * 8 * PITCH, 8, stride=PITCH), :]
                two = state_ref[pl.ds(second + c * 8 * PITCH, 8, stride=PITCH), :]
                if half == 0:
                    two = turn(two, HALF, 1)
                else:
                    one = turn(one, HALF, 1)
                merged.append(jnp.where(in_half((8, DEPTH), 0), one, two))
            for c, value in enumerate((fold_own if narrow else fold)(*merged)):
                spot = pl.multiple_of(peer * unit + offset + 8 * c, 8)
                out_ref[pl.ds(spot, 8), :] = value
        return carry

    lax.fori_loop(0, PEERS // group, some, 0)


def place_rows(state_ref, half, tables_ref, at, in_ref, unit, offset, narrow=False):
    group = 16

    def some(g, carry):
        stores = []
        for j in range(group):
            peer = g * group + j
            parts = [
                in_ref[pl.ds(pl.multiple_of(peer * unit + offset + 8 * c, 8), 8), :]
                for c in range(2 if narrow else 3)
            ]
            parts = unfold_own(*parts) if narrow else parts + [unfold(*parts)]
            for k in range(2):
                row = tables_ref[at + 2 * peer + k]
                row = jnp.where(row < 0, ROWS, row)
                for c, value in enumerate(parts):
                    if k != half:
                        value = turn(value, HALF, 1)
                    where = pl.ds(row + c * 8 * PITCH, 8, stride=PITCH)
                    stores.append(
                        (where, jnp.where(in_half((8, DEPTH), half), value, state_ref[where, :]))
                    )
        for where, value in stores:
            state_ref[where, :] = value
        return carry

    lax.fori_loop(0, PEERS // group, some, 0)


def copy_state(source_ref, target_ref):
    def one(q, carry):
        at = pl.multiple_of(q * PITCH, 8)
        target_ref[pl.ds(at, ROWS), :] = source_ref[pl.ds(at, ROWS), :]
        return carry

    lax.fori_loop(0, Q, one, 0)


def pair_rate(rates_ref, first, second):
    return jnp.where(in_half((8, DEPTH), 0), rates_ref[first], rates_ref[second])


def first_edges_kernel(rate_ref, x_ref, wall_ref, edge_ref, low_ref, high_ref):
    rate = jnp.full((8, DEPTH), rate_ref[0], jnp.float32)

    def load(q, row):
        return x_ref[pl.ds(q * ROWS + row, 8), :]

    collide_edges(load, wall_ref, rate, edge_ref, low_ref, high_ref)


def first_inside_kernel(rate_ref, x_ref, wall_ref, edge_ref, read_ref, inside_ref):
    rate = jnp.full((8, DEPTH), rate_ref[0], jnp.float32)

    def load(q, row):
        return x_ref[pl.ds(q * ROWS + row, 8), :]

    collide_inside(load, wall_ref, rate, inside_ref)
    stream_known(edge_ref, inside_ref, read_ref, ROWS, None)
    read_ref[pl.ds(Q * ROWS, ROWS), :] = wall_ref[...].astype(jnp.float32)


def windows_kernel(seen_ref, front_ref, behind_ref, meta_ref, out_ref, read_ref):
    stream_rest(front_ref, behind_ref, read_ref, ROWS, False)

    def some(g, carry):
        lanes = lanes_of((8, DEPTH))
        for row in range(0, HALF, 8):
            mixed = []
            for j in range(4):
                at = pl.multiple_of((4 * g + j) * ROWS + row, 8)
                top = read_ref[pl.ds(at, 8), :]
                bottom = turn(read_ref[pl.ds(at + HALF, 8), :], HALF, 1)
                mixed.append(
                    [
                        jnp.where(((lanes + GHOST - OWN * k) & (DEPTH - 1)) < HALF, top, bottom)
                        for k in range(LEVELS)
                    ]
                )
            for target in range(LEVELS):
                shift = GHOST - OWN * target
                main = [turn(mixed[j][target], shift, 1) for j in range(3)]
                extra = [turn(mixed[3][target], shift + by, 1) for by in (16, 48, 96)]
                for j, value in enumerate(fold_turned(*main, *extra)):
                    at = pl.multiple_of(target * WINDOW + (3 * g + j) * HALF + row, 8)
                    out_ref[pl.ds(at, 8), :] = value
        return carry

    lax.fori_loop(0, GROUPS, some, 0)
    for target in range(LEVELS):
        at = (target + 1) * WINDOW - META
        out_ref[pl.ds(at, META), :] = meta_ref[...]
        out_ref[pl.ds(at + 2, 1), :] = jnp.full((1, DEPTH), target, jnp.float32)


def unpack_pair(in_ref, state_ref, wall_ref, first, second):
    def some(g, carry):
        left = in_half((8, DEPTH), 0)
        for row in range(0, HALF, 8):
            parts = []
            for level in (first, second):
                at = pl.multiple_of(level * WINDOW + 3 * g * HALF + row, 8)
                three = [in_ref[pl.ds(at + j * HALF, 8), :] for j in range(3)]
                parts.append(three + [unfold(*three)])
            for j in range(4):
                one, two = parts[0][j], parts[1][j]
                crossed = turn(jnp.where(left, two, one), HALF, 1)
                at = pl.multiple_of((4 * g + j) * PITCH + row, 8)
                state_ref[pl.ds(at, 8), :] = jnp.where(left, one, crossed)
                state_ref[pl.ds(at + HALF, 8), :] = jnp.where(left, crossed, two)
        return carry

    lax.fori_loop(0, GROUPS, some, 0)
    wall_ref[...] = state_ref[pl.ds(Q * PITCH, ROWS), :]


def unpack_kernel(tables_ref, rates_ref, in_ref, s_ref, wall_ref, rows_ref):
    unpack_pair(in_ref, s_ref, wall_ref, 3, 2)
    pick_rows(s_ref, 1, tables_ref, table_at(2, DOWN_SEND), rows_ref, UNIT, 0)


def unpack_other_kernel(tables_ref, rates_ref, in_ref, low_ref, t_ref, wall_ref, taken_ref):
    unpack_pair(in_ref, t_ref, wall_ref, 1, 0)
    taken_ref[...] = jnp.zeros((PITCH, DEPTH), jnp.float32)

    def mark(j, carry):
        row = tables_ref[table_at(3, DOWN_RECV) + j]
        spot = pl.ds(jnp.where(row < 0, ROWS, row), 1)
        taken_ref[spot, :] = jnp.where(in_half((1, DEPTH), 0), 1.0, 0.0)
        return carry

    lax.fori_loop(0, 2 * PEERS, mark, 0, unroll=8)


def apply(state_ref, couplings, tables_ref, buffers):
    for half, at, index, unit, offset, narrow in couplings:
        place_rows(state_ref, half, tables_ref, at, buffers[index], unit, offset, narrow)


def edges_kernel(levels, couplings, buffers, carried, halved, tables_ref, rates_ref, *refs):
    refs = list(refs)[1:]
    wall_ref = refs.pop(0)
    in_refs = [refs.pop(0) for _ in range(buffers)]
    other_refs = [refs.pop(0) for _ in range(2)] if carried else []
    work_ref, edge_ref, low_ref, high_ref = refs
    apply(work_ref, couplings, tables_ref, in_refs)

    def load(q, row):
        return work_ref[pl.ds(q * PITCH + row, 8), :]

    rate = pair_rate(rates_ref, *levels)
    collide_edges(load, wall_ref, rate, edge_ref, low_ref, high_ref, halved)
    for source, target in zip(other_refs, (low_ref, high_ref)):
        target[pl.ds(4 * BLOCKS, 4 * BLOCKS), :] = source[...]


def inside_kernel(levels, keep, extra, couplings, buffers, tables_ref, rates_ref, *refs):
    refs = list(refs)
    work_ref, wall_ref, edge_ref = refs.pop(0), refs.pop(0), refs.pop(0)
    old_ref = work_ref if keep else None
    other_ref = refs.pop(0) if extra and not extra[0] else None
    in_refs = [refs.pop(0) for _ in range(buffers)]
    inside_ref = refs.pop()
    read_ref = refs.pop(0)
    next_ref = refs.pop(0) if couplings else None

    def load(q, row):
        return work_ref[pl.ds(q * PITCH + row, 8), :]

    collide_inside(load, wall_ref, pair_rate(rates_ref, *levels), inside_ref)
    stream_known(edge_ref, inside_ref, read_ref, PITCH, old_ref, next_ref)
    apply(next_ref, couplings, tables_ref, in_refs)
    if extra:
        own, half, at = extra
        source = old_ref if own else other_ref
        pick_rows(source, half, tables_ref, at, refs.pop(0), 2 * UNIT, UNIT)


def joined_kernel(first, second, ins, outs, *refs):
    refs = list(refs)
    scalars = [[refs.pop(0), refs.pop(0)] for _ in range(2)]
    inputs = [[refs.pop(0) for _ in range(count)] for count in ins]
    outputs = [[refs.pop(0) for _ in range(count)] for count in outs]
    for i, kernel in enumerate((first, second)):
        kernel(*scalars[i], *inputs[i], *outputs[i], refs[i])


def rest_kernel(keep, picks, unit, carried, ahead, inputs, tables_ref, front_ref, behind_ref, *refs):
    taken_ref = refs[0] if ahead else None
    refs = list(refs)[inputs:]
    seen_ref, rows_ref = refs.pop(0), refs.pop(0)
    next_ref = refs.pop(0) if ahead else None
    other_ref = refs.pop(0) if carried else None
    stream_rest(
        front_ref, behind_ref, seen_ref, PITCH, keep, 0, next_ref, taken_ref, halved=keep
    )
    if carried:
        stream_rest(front_ref, behind_ref, other_ref, PITCH, True, 4 * BLOCKS, halved=True)
    for other, half, at, offset, narrow in picks:
        source = other_ref if other else seen_ref
        pick_rows(source, half, tables_ref, at, rows_ref, unit, offset, narrow)


def pack_level(work_ref, half, out_ref):
    def one(q, carry):
        chunk = lanes_of((8, DEPTH)) // OWN
        for row in range(0, WIDTH, 8):
            packed = None
            for plane in range(PLANES):
                at = pl.multiple_of(q * PITCH + plane * WIDTH + row, 8)
                value = turn(work_ref[pl.ds(at, 8), :], OWN * plane - HALF * half - GHOST, 1)
                packed = value if packed is None else jnp.where(chunk == plane, value, packed)
            out_ref[pl.ds(pl.multiple_of(q * WIDTH + row, 8), 8), :] = packed
        return carry

    lax.fori_loop(0, Q, one, 0, unroll=9)


def pack_levels(tables_ref, work_ref, levels, out_refs):
    for me in range(LEVELS):

        @pl.when(tables_ref[ME] == me)
        def _():
            for half, level in levels:
                pack_level(work_ref, half, out_refs[(level - me) % LEVELS])


def other_early_kernel(couplings, tables_ref, rates_ref, state_ref, b2, b5, out_ref, work_ref):
    copy_state(state_ref, out_ref)
    apply(out_ref, couplings, tables_ref, (b2, b5))


def other_last_kernel(couplings, tables_ref, rates_ref, state_ref, b6, *refs):
    out_refs, work_ref = refs[:-1], refs[-1]
    copy_state(state_ref, work_ref)
    apply(work_ref, couplings, tables_ref, (b6,))
    pack_levels(tables_ref, work_ref, ((1, 0), (0, 1)), out_refs)


def last_kernel(couplings, tables_ref, rates_ref, state_ref, b7, *refs):
    out_refs, work_ref = refs[LEVELS:-1], refs[-1]
    copy_state(state_ref, work_ref)
    apply(work_ref, couplings, tables_ref, (b7,))
    pack_levels(tables_ref, work_ref, ((1, 2), (0, 3)), out_refs)


def output_kernel(tables_ref, *refs):
    in_refs, out_ref = refs[:-1], refs[-1]
    chunk = lanes_of((WIDTH, DEPTH)) // OWN
    for me in range(LEVELS):

        @pl.when(tables_ref[ME] == me)
        def _():
            def one(q, carry):
                parts = [
                    in_refs[(me - c) % LEVELS][pl.ds(pl.multiple_of(q * WIDTH, 8), WIDTH), :]
                    for c in range(LEVELS)
                ]
                for plane in range(PLANES):
                    whole = None
                    for c in range(LEVELS):
                        value = turn(parts[c], OWN * (c - plane), 1)
                        whole = value if whole is None else jnp.where(chunk == c, value, whole)
                    out_ref[pl.ds(pl.multiple_of(q * ROWS + plane * WIDTH, 8), WIDTH), :] = whole
                return carry

            lax.fori_loop(0, Q, one, 0, unroll=3)


def trade_planes(low, high):
    count = lax.axis_size("gx")
    forward = [(i, (i + 1) % count) for i in range(count)]
    backward = [(target, source) for source, target in forward]
    return lax.ppermute(low, "gx", backward), lax.ppermute(high, "gx", forward)


def trade_rows(rows):
    blocks = rows.reshape(PEERS, -1, DEPTH)
    return lax.all_to_all(blocks, "gx", split_axis=0, concat_axis=0, tiled=True).reshape(
        rows.shape
    )


def on_device(populations, solid_mask, relax_rates, down_send, down_recv, up_send, up_recv):
    meta = jnp.concatenate(
        [value.reshape(-1) for value in (down_send, down_recv, up_send, up_recv)]
    ).astype(jnp.float32)
    meta = jnp.concatenate([meta, jnp.broadcast_to(relax_rates, (META * DEPTH - meta.size,))])
    meta = meta.reshape(META, DEPTH)
    x = jnp.transpose(populations.reshape(ROWS, Q, DEPTH), (1, 0, 2)).reshape(Q * ROWS, DEPTH)
    wall = solid_mask.reshape(ROWS, DEPTH)
    flow = [(Q * ROWS, DEPTH), (9 * WIDTH, DEPTH), (9 * WIDTH, DEPTH)]
    state = (STATE, DEPTH)

    edge, low, high = call(
        first_edges_kernel, [(Q * HALF, DEPTH), *flow[1:]], (relax_rates, x, wall), smem=1
    )
    front, behind = trade_planes(low, high)
    (seen,) = call(
        first_inside_kernel,
        [((Q + 1) * ROWS, DEPTH)],
        (relax_rates, x, wall, edge),
        smem=1,
        scratch=[(Q * HALF, DEPTH)],
    )
    windows, _ = call(
        windows_kernel,
        [(LEVELS * WINDOW, DEPTH), ((Q + 1) * ROWS, DEPTH)],
        (seen, front, behind, meta),
        aliases={0: 1},
    )
    windows = lax.all_to_all(
        windows.reshape(LEVELS, WINDOW, DEPTH), "lvl", 0, 0, tiled=True
    )
    tables = windows[:, WINDOW - META : WINDOW - META + 3, :].astype(jnp.int32).reshape(-1)
    rates = windows[:, WINDOW - 1, 0]
    windows = windows.reshape(-1, DEPTH)
    s, wall_s, rows = call(
        unpack_kernel,
        [state, (ROWS, DEPTH), (PEERS * UNIT, DEPTH)],
        (tables, rates, windows),
        smem=2,
    )
    got = {0: trade_rows(rows)}

    def taken(step, offset, half, level, which, narrow=False):
        buffer = got[step]
        return buffer, half, table_at(level, which), buffer.shape[0] // PEERS, offset, narrow

    def gather_takes(takes):
        buffers, couplings = [], []
        for buffer, half, at, unit, offset, narrow in takes:
            index = next((i for i, b in enumerate(buffers) if b is buffer), len(buffers))
            if index == len(buffers):
                buffers.append(buffer)
            couplings.append((half, at, index, unit, offset, narrow))
        return buffers, couplings

    def edges(value, walls, levels, takes, halved, carried=()):
        buffers, couplings = gather_takes(takes)
        planes = (8 * BLOCKS // (1 if carried or not halved else 2), DEPTH)
        return call(
            functools.partial(
                edges_kernel, levels, couplings, len(buffers), bool(carried), halved
            ),
            [state, (Q * HALF, DEPTH), planes, planes],
            (tables, rates, value, walls, *buffers, *carried),
            smem=2,
            aliases={2: 0},
        )

    def inside(work, walls, edge, levels, keep, extra=None, other=None, takes=(), join=None):
        buffers, couplings = gather_takes(takes)
        ins = [work, walls, edge]
        ins += [other] if extra and not extra[0] else []
        ins += buffers
        kernel = functools.partial(
            inside_kernel, levels, keep, extra, couplings, len(buffers)
        )
        outs = [state] * (2 if takes else 1) + ([(PEERS * 2 * UNIT, DEPTH)] if extra else [])
        scratch = [(Q * HALF, DEPTH)]
        if join is None:
            return call(kernel, outs, (tables, rates, *ins), smem=2, scratch=scratch)
        second, more_ins, more_outs = join
        return call(
            functools.partial(
                joined_kernel, kernel, second, (len(ins), len(more_ins)), (len(outs), len(more_outs))
            ),
            outs + more_outs,
            (tables, rates, tables, rates, *ins, *more_ins),
            smem=4,
            scratch=scratch + [state],
        )

    down_23 = (False, 1, table_at(2, DOWN_SEND), 0, False)
    up_32 = (False, 0, table_at(3, UP_SEND), 0, False)
    extras = {
        1: (False, 0, table_at(1, DOWN_SEND)),
        2: (False, 1, table_at(0, DOWN_SEND)),
        3: (True, 1, table_at(2, UP_SEND)),
    }
    picks = {
        1: [up_32],
        2: [down_23],
        3: [up_32],
        4: [down_23],
        5: [
            up_32,
            (True, 0, table_at(1, DOWN_SEND), UNIT, False),
            (True, 0, table_at(1, UP_SEND), 2 * UNIT, True),
        ],
        6: [down_23, (False, 1, table_at(2, UP_SEND), UNIT, True)],
        7: [(False, 0, table_at(3, UP_SEND), 0, True)],
    }
    units = {1: 48, 2: 48, 3: 48, 4: 24, 5: 64, 6: 40, 7: 16}
    for step in range(1, 8):
        odd = step % 2 == 1
        if odd:
            takes = [taken(step - 1, 0, 0, 3, DOWN_RECV)]
        else:
            takes = [taken(step - 1, 0, 1, 2, UP_RECV)]
            if step == 6:
                takes.append(taken(5, UNIT, 1, 2, DOWN_RECV))
            elif step == 2:
                takes.append(taken(1, UNIT, 1, 2, DOWN_RECV))
        carried = step == 5
        work, edge, low, high = edges(
            s, wall_s, (3, 2), takes, odd, (t_low, t_high) if carried else ()
        )
        front, behind = trade_planes(low, high)
        if step == 1:
            t, wall_t, coupled = call(
                unpack_other_kernel,
                [state, (ROWS, DEPTH), (PITCH, DEPTH)],
                (tables, rates, windows, low),
                smem=2,
            )
        extra = extras.get(step)
        ahead = []
        if odd:
            ahead.append(taken(step - 1, 0, 0, 3, DOWN_RECV))
            if step in (3, 7):
                ahead.append(taken(1 if step == 3 else 5, UNIT, 1, 2, DOWN_RECV))
        join = None
        if step == 6:
            couplings = [
                (0, table_at(1, DOWN_RECV), 0, units[2], UNIT, False),
                (1, table_at(0, UP_RECV), 1, units[5], 2 * UNIT, True),
            ]
            early = functools.partial(other_early_kernel, couplings)
            join = (early, (t, got[2], got[5]), [state])
        if step == 7:
            couplings = [(0, table_at(1, UP_RECV), 0, units[6], UNIT, True)]
            late = functools.partial(other_last_kernel, couplings)
            join = (late, (t, got[6]), [(Q * WIDTH, DEPTH)] * LEVELS)
        seen, *rows = inside(work, wall_s, edge, (3, 2), odd, extra, t, ahead, join)
        following = [rows.pop(0)] if ahead else []
        if step == 6:
            t = rows.pop()
        if step == 7:
            packed, rows = rows, []
        if step == 4:
            takes = [taken(2, UNIT, 0, 1, DOWN_RECV), taken(3, UNIT, 0, 1, UP_RECV)]
            t_work, t_edge, t_low, t_high = edges(t, wall_t, (1, 0), takes, True)
            seen, t_work, t_edge, t_low, t_high = lax.optimization_barrier(
                (seen, t_work, t_edge, t_low, t_high)
            )
        if step == 5:
            (t,) = inside(t_work, wall_t, t_edge, (1, 0), True)
        unit = units[step]
        ins = [tables, front, behind] + ([coupled] if ahead else [])
        outs, aliases = [], {}
        for value in (seen, *rows, *following, *([t] if carried else [])):
            if value is seen or rows:
                slot = len(outs)
            else:
                slot = len(outs) + 1 if len(outs) == 1 else len(outs)
            if slot == 2 and len(outs) == 1:
                outs.append((PEERS * unit, DEPTH))
            aliases[len(ins)] = slot
            outs.append(value.shape)
            ins.append(value)
        if len(outs) == 1:
            outs.append((PEERS * unit, DEPTH))
        s, got[step], *others = call(
            functools.partial(
                rest_kernel, odd, picks[step], unit, carried, bool(ahead), len(ins) - 3
            ),
            outs,
            ins,
            smem=1,
            aliases=aliases,
        )
        if ahead:
            s = others.pop(0)
        if carried:
            (t,) = others
        got[step] = trade_rows(got[step])

    couplings = [(1, table_at(2, UP_RECV), 0, units[7], 0, True)]
    packed = call(
        functools.partial(last_kernel, couplings),
        [(Q * WIDTH, DEPTH)] * LEVELS,
        (tables, rates, s, got[7], *packed),
        smem=2,
        scratch=[state],
        aliases={4 + i: i for i in range(LEVELS)},
    )
    parts = [packed[0]] + [
        lax.ppermute(packed[by], "lvl", [(i, (i + by) % LEVELS) for i in range(LEVELS)])
        for by in range(1, LEVELS)
    ]
    (final,) = call(output_kernel, [(Q * ROWS, DEPTH)], (tables, *parts), smem=1)
    final = jnp.transpose(final.reshape(Q, ROWS, DEPTH), (1, 0, 2))
    return final.reshape(1, PLANES, WIDTH, Q, DEPTH)


def solution(mesh):
    return jax.shard_map(
        on_device,
        mesh=mesh,
        in_specs=(
            P("lvl", "gx", None, None, None),
            P("lvl", "gx", None, None),
            P("lvl"),
            P("lvl", "gx", None, None),
            P("lvl", "gx", None, None),
            P("lvl", "gx", None, None),
            P("lvl", "gx", None, None),
        ),
        out_specs=P("lvl", "gx", None, None, None),
        check_vma=False,
    )
```

```python
import functools

import jax
import jax.numpy as jnp
from jax import lax
from jax.experimental import pallas as pl
from jax.experimental.pallas import tpu as pltpu
from jax.sharding import PartitionSpec as P

Q = 27
PLANES = 4
WIDTH = 32
ROWS = PLANES * WIDTH
DEPTH = 128
PEERS = 32
LEVELS = 4
HALF = 64
OWN = 32
GHOST = 16
PITCH = 136
QPAD = 32
STATE = QPAD * PITCH
UNIT = 24
NARROW = 16
BLOCKS = 9 * WIDTH // 8
GROUPS = 7
META = 8
WINDOW = 3 * GROUPS * HALF + META

VMEM = pl.BlockSpec(memory_space=pltpu.VMEM)
SMEM = pl.BlockSpec(memory_space=pltpu.SMEM)

DOWN_SEND, DOWN_RECV, UP_SEND, UP_RECV = range(4)
ME = 4 * 2 * PEERS
LEVEL_TABLES = ME + DEPTH


def table_at(level, which):
    return level * LEVEL_TABLES + which * 2 * PEERS


def call(kernel, outs, ins, smem=0, scratch=(), aliases=None):
    moved = sum(value.size for value in ins) + sum(rows * depth for rows, depth in outs)
    return pl.pallas_call(
        kernel,
        out_shape=[jax.ShapeDtypeStruct(shape, jnp.float32) for shape in outs],
        in_specs=[SMEM] * smem + [VMEM] * (len(ins) - smem),
        out_specs=[VMEM] * len(outs),
        scratch_shapes=[pltpu.VMEM(shape, jnp.float32) for shape in scratch],
        input_output_aliases=aliases or {},
        cost_estimate=pl.CostEstimate(
            flops=10 * moved, bytes_accessed=4 * moved, transcendentals=0
        ),
        compiler_params=pltpu.CompilerParams(vmem_limit_bytes=14 * 1024 * 1024),
    )(*ins)


def lanes_of(shape):
    return lax.broadcasted_iota(jnp.int32, shape, 1)


def in_half(shape, half):
    lanes = lanes_of(shape)
    return lanes < HALF if half == 0 else lanes >= HALF


def turn(value, shift, axis):
    size = value.shape[axis]
    shift = shift % size
    return value if shift == 0 else pltpu.roll(value, shift, axis)


def gaps(shape):
    lanes = lanes_of(shape)
    return (lanes >= 56) & (lanes < 72), (lanes < 8) | (lanes >= 120)


def fold(t0, t1, t2, extra):
    return fold_turned(t0, t1, t2, *(turn(extra, shift, 1) for shift in (16, 48, 96)))


def fold_turned(t0, t1, t2, e16, e48, e96):
    inner, outer = gaps(t0.shape)
    return (
        jnp.where(inner, e48, jnp.where(outer, e96, t0)),
        jnp.where(inner, e16, jnp.where(outer, e48, t1)),
        jnp.where(inner, e96, jnp.where(outer, e16, t2)),
    )


def unfold(t0, t1, t2):
    inner, _ = gaps(t0.shape)
    e48 = turn(jnp.where(inner, t0, t1), -48, 1)
    e96 = turn(jnp.where(inner, t2, t0), -96, 1)
    e16 = turn(jnp.where(inner, t1, t2), -16, 1)
    spot = lanes_of(t0.shape) & (HALF - 1)
    return jnp.where(spot < 24, e48, jnp.where(spot < 40, e96, e16))


def fold_own(m0, m1, m2, m3):
    quarter = lanes_of(m0.shape) // OWN

    def join(a, b):
        return jnp.where(
            quarter < 2,
            jnp.where(quarter == 0, turn(a, -16, 1), turn(a, -48, 1)),
            jnp.where(quarter == 2, turn(b, 48, 1), turn(b, 16, 1)),
        )

    return join(m0, m1), join(m2, m3)


def unfold_own(t0, t1):
    left = in_half(t0.shape, 0)
    out = []
    for value in (t0, t1):
        out.append(jnp.where(left, turn(value, 16, 1), turn(value, 48, 1)))
        out.append(jnp.where(left, turn(value, -48, 1), turn(value, -16, 1)))
    return out


def collide(f, wall, rate):
    t, d = [], []
    for pair in range(9):
        low, mid, high = f[3 * pair : 3 * pair + 3]
        t.append(low + high + 4.0 * mid)
        d.append(high - low)
    total, along_y, along_z = [], [], []
    for a in range(3):
        total.append(t[3 * a] + t[3 * a + 2] + 4.0 * t[3 * a + 1])
        along_y.append(t[3 * a + 2] - t[3 * a])
        along_z.append(d[3 * a] + d[3 * a + 2] + 4.0 * d[3 * a + 1])
    mass = total[0] + total[2] + 4.0 * total[1]
    inverse = 3.0 / mass
    ux = (total[2] - total[0]) * inverse
    uy = (along_y[0] + along_y[2] + 4.0 * along_y[1]) * inverse
    uz = (along_z[0] + along_z[2] + 4.0 * along_z[1]) * inverse
    scaled = rate * mass * (1.0 / 216.0)
    half = 0.5 * scaled
    base = scaled - scaled * ((ux * ux + uy * uy + uz * uz) * (1.0 / 6.0))
    keep = 1.0 - rate
    sums = {
        (0, 0, 1): uz,
        (0, 1, 0): uy,
        (1, 0, 0): ux,
        (0, 1, -1): uy - uz,
        (0, 1, 1): uy + uz,
        (1, 0, -1): ux - uz,
        (1, 0, 1): ux + uz,
        (1, -1, 0): ux - uy,
        (1, 1, 0): ux + uy,
    }
    for b in (-1, 1):
        for e in (-1, 1):
            sums[(1, b, e)] = sums[(1, b, 0)] + uz if e == 1 else sums[(1, b, 0)] - uz
    out = [None] * Q
    out[13] = jnp.where(wall, f[13], keep * f[13] + base)
    for (a, b, e), along in sums.items():
        i = 9 * (a + 1) + 3 * (b + 1) + (e + 1)
        j = 26 - i
        part = half * along
        odd = part + part
        even = base + part * along
        out[i] = jnp.where(wall, f[j], keep * f[i] + (even + odd))
        out[j] = jnp.where(wall, f[i], keep * f[j] + (even - odd))
    return out


def collide_rows(load, wall_ref, rate, store, tiles):
    def tile(i, carry):
        row = pl.multiple_of(tiles(i) * 8, 8)
        wall = wall_ref[pl.ds(row, 8), :] > 0.5
        out = collide([load(q, row) for q in range(Q)], wall, rate)
        for q in range(Q):
            store(q, row, turn(out[q], q % 3 - 1, 1))
        return carry

    lax.fori_loop(0, ROWS // 16, tile, 0, unroll=4)


def edge_tiles(i):
    return jnp.where(i < 4, i, i + 8)


def inner_tiles(i):
    return i + 4


def collide_edges(load, wall_ref, rate, edge_ref, low_ref, high_ref, halved=False):
    def store(q, row, value):
        at = jnp.where(row < WIDTH, row, row - 2 * WIDTH)
        edge_ref[pl.ds(pl.multiple_of(q * HALF + at, 8), 8), :] = value

    collide_rows(load, wall_ref, rate, store, edge_tiles)

    def block(first, i):
        return edge_ref[pl.ds(first + i // 4 * HALF + i % 4 * 8, 8), :]

    for ref, first in ((low_ref, 0), (high_ref, 18 * HALF + WIDTH)):
        if halved:
            for i in range(BLOCKS // 2):
                ref[pl.ds(8 * i, 8), :] = jnp.where(
                    in_half((8, DEPTH), 0),
                    block(first, i),
                    turn(block(first, i + BLOCKS // 2), HALF, 1),
                )
        else:
            for i in range(BLOCKS):
                ref[pl.ds(8 * i, 8), :] = block(first, i)


def collide_inside(load, wall_ref, rate, inside_ref):
    def store(q, row, value):
        inside_ref[pl.ds(pl.multiple_of(q * HALF + row - WIDTH, 8), 8), :] = value

    collide_rows(load, wall_ref, rate, store, inner_tiles)


def stream_known(edge_ref, inside_ref, read_ref, pitch, old_ref, next_ref=None):
    for q in range(Q):
        for plane in range(PLANES):
            source = plane - (q // 9 - 1)
            spot = pl.ds(q * pitch + plane * WIDTH, WIDTH)
            if 0 <= source < PLANES:
                if source in (0, PLANES - 1):
                    value = edge_ref[pl.ds(q * HALF + (WIDTH if source else 0), WIDTH), :]
                else:
                    value = inside_ref[pl.ds(q * HALF + (source - 1) * WIDTH, WIDTH), :]
                value = turn(value, q // 3 % 3 - 1, 0)
                if old_ref is not None:
                    value = jnp.where(in_half((WIDTH, DEPTH), 0), value, old_ref[spot, :])
            elif old_ref is not None:
                value = old_ref[spot, :]
            else:
                continue
            read_ref[spot, :] = value
            if next_ref is not None:
                next_ref[spot, :] = value


def stream_rest(
    front_ref, behind_ref, read_ref, pitch, keep, start=0, next_ref=None, taken_ref=None, halved=False
):
    def block(ref, i):
        if halved and i >= BLOCKS // 2:
            return turn(ref[pl.ds(start + 8 * i - 4 * BLOCKS, 8), :], HALF, 1)
        return ref[pl.ds(start + 8 * i, 8), :]

    for q in range(9):
        for velocity, plane, ref in ((q, PLANES - 1, front_ref), (q + 18, 0, behind_ref)):
            spot = pl.ds(velocity * pitch + plane * WIDTH, WIDTH)
            value = jnp.concatenate([block(ref, 4 * q + i) for i in range(4)], axis=0)
            value = turn(value, q // 3 - 1, 0)
            if keep:
                value = jnp.where(in_half((WIDTH, DEPTH), 0), value, read_ref[spot, :])
            read_ref[spot, :] = value
            if next_ref is not None:
                placed = taken_ref[pl.ds(plane * WIDTH, WIDTH), :] > 0.5
                free = in_half((WIDTH, DEPTH), 0) & jnp.logical_not(placed)
                next_ref[spot, :] = jnp.where(free, value, next_ref[spot, :])


def pick_rows(state_ref, half, tables_ref, at, out_ref, unit, offset, narrow=False):
    group = 16

    def some(g, carry):
        for j in range(group):
            peer = g * group + j
            first = jnp.maximum(tables_ref[at + 2 * peer], 0)
            second = jnp.maximum(tables_ref[at + 2 * peer + 1], 0)
            merged = []
            for c in range(QPAD // 8):
                one = state_ref[pl.ds(first + c * 8 * PITCH, 8, stride=PITCH), :]
                two = state_ref[pl.ds(second + c * 8 * PITCH, 8, stride=PITCH), :]
                if half == 0:
                    two = turn(two, HALF, 1)
                else:
                    one = turn(one, HALF, 1)
                merged.append(jnp.where(in_half((8, DEPTH), 0), one, two))
            for c, value in enumerate((fold_own if narrow else fold)(*merged)):
                spot = pl.multiple_of(peer * unit + offset + 8 * c, 8)
                out_ref[pl.ds(spot, 8), :] = value
        return carry

    lax.fori_loop(0, PEERS // group, some, 0)


def place_rows(state_ref, half, tables_ref, at, in_ref, unit, offset, narrow=False):
    group = 16

    def some(g, carry):
        stores = []
        for j in range(group):
            peer = g * group + j
            parts = [
                in_ref[pl.ds(pl.multiple_of(peer * unit + offset + 8 * c, 8), 8), :]
                for c in range(2 if narrow else 3)
            ]
            parts = unfold_own(*parts) if narrow else parts + [unfold(*parts)]
            for k in range(2):
                row = tables_ref[at + 2 * peer + k]
                row = jnp.where(row < 0, ROWS, row)
                for c, value in enumerate(parts):
                    if k != half:
                        value = turn(value, HALF, 1)
                    where = pl.ds(row + c * 8 * PITCH, 8, stride=PITCH)
                    stores.append(
                        (where, jnp.where(in_half((8, DEPTH), half), value, state_ref[where, :]))
                    )
        for where, value in stores:
            state_ref[where, :] = value
        return carry

    lax.fori_loop(0, PEERS // group, some, 0)


def copy_state(source_ref, target_ref):
    def one(q, carry):
        at = pl.multiple_of(q * PITCH, 8)
        target_ref[pl.ds(at, ROWS), :] = source_ref[pl.ds(at, ROWS), :]
        return carry

    lax.fori_loop(0, Q, one, 0)


def pair_rate(rates_ref, first, second):
    return jnp.where(in_half((8, DEPTH), 0), rates_ref[first], rates_ref[second])


def first_edges_kernel(rate_ref, x_ref, wall_ref, edge_ref, low_ref, high_ref):
    rate = jnp.full((8, DEPTH), rate_ref[0], jnp.float32)

    def load(q, row):
        return x_ref[pl.ds(q * ROWS + row, 8), :]

    collide_edges(load, wall_ref, rate, edge_ref, low_ref, high_ref)


def first_inside_kernel(rate_ref, x_ref, wall_ref, edge_ref, read_ref, inside_ref):
    rate = jnp.full((8, DEPTH), rate_ref[0], jnp.float32)

    def load(q, row):
        return x_ref[pl.ds(q * ROWS + row, 8), :]

    collide_inside(load, wall_ref, rate, inside_ref)
    stream_known(edge_ref, inside_ref, read_ref, ROWS, None)
    read_ref[pl.ds(Q * ROWS, ROWS), :] = wall_ref[...].astype(jnp.float32)


def windows_kernel(seen_ref, front_ref, behind_ref, meta_ref, out_ref, read_ref):
    stream_rest(front_ref, behind_ref, read_ref, ROWS, False)

    def some(g, carry):
        lanes = lanes_of((8, DEPTH))
        for row in range(0, HALF, 8):
            mixed = []
            for j in range(4):
                at = pl.multiple_of((4 * g + j) * ROWS + row, 8)
                top = read_ref[pl.ds(at, 8), :]
                bottom = turn(read_ref[pl.ds(at + HALF, 8), :], HALF, 1)
                mixed.append(
                    [
                        jnp.where(((lanes + GHOST - OWN * k) & (DEPTH - 1)) < HALF, top, bottom)
                        for k in range(LEVELS)
                    ]
                )
            for target in range(LEVELS):
                shift = GHOST - OWN * target
                main = [turn(mixed[j][target], shift, 1) for j in range(3)]
                extra = [turn(mixed[3][target], shift + by, 1) for by in (16, 48, 96)]
                for j, value in enumerate(fold_turned(*main, *extra)):
                    at = pl.multiple_of(target * WINDOW + (3 * g + j) * HALF + row, 8)
                    out_ref[pl.ds(at, 8), :] = value
        return carry

    lax.fori_loop(0, GROUPS, some, 0)
    for target in range(LEVELS):
        at = (target + 1) * WINDOW - META
        out_ref[pl.ds(at, META), :] = meta_ref[...]
        out_ref[pl.ds(at + 2, 1), :] = jnp.full((1, DEPTH), target, jnp.float32)


def unpack_pair(in_ref, state_ref, wall_ref, first, second):
    def some(g, carry):
        left = in_half((8, DEPTH), 0)
        for row in range(0, HALF, 8):
            parts = []
            for level in (first, second):
                at = pl.multiple_of(level * WINDOW + 3 * g * HALF + row, 8)
                three = [in_ref[pl.ds(at + j * HALF, 8), :] for j in range(3)]
                parts.append(three + [unfold(*three)])
            for j in range(4):
                one, two = parts[0][j], parts[1][j]
                crossed = turn(jnp.where(left, two, one), HALF, 1)
                at = pl.multiple_of((4 * g + j) * PITCH + row, 8)
                state_ref[pl.ds(at, 8), :] = jnp.where(left, one, crossed)
                state_ref[pl.ds(at + HALF, 8), :] = jnp.where(left, crossed, two)
        return carry

    lax.fori_loop(0, GROUPS, some, 0)
    wall_ref[...] = state_ref[pl.ds(Q * PITCH, ROWS), :]


def unpack_kernel(tables_ref, rates_ref, in_ref, s_ref, wall_ref, rows_ref):
    unpack_pair(in_ref, s_ref, wall_ref, 3, 2)
    pick_rows(s_ref, 1, tables_ref, table_at(2, DOWN_SEND), rows_ref, UNIT, 0)


def unpack_other_kernel(tables_ref, rates_ref, in_ref, low_ref, t_ref, wall_ref, taken_ref):
    unpack_pair(in_ref, t_ref, wall_ref, 1, 0)
    taken_ref[...] = jnp.zeros((PITCH, DEPTH), jnp.float32)

    def mark(j, carry):
        row = tables_ref[table_at(3, DOWN_RECV) + j]
        spot = pl.ds(jnp.where(row < 0, ROWS, row), 1)
        taken_ref[spot, :] = jnp.where(in_half((1, DEPTH), 0), 1.0, 0.0)
        return carry

    lax.fori_loop(0, 2 * PEERS, mark, 0, unroll=8)


def apply(state_ref, couplings, tables_ref, buffers):
    for half, at, index, unit, offset, narrow in couplings:
        place_rows(state_ref, half, tables_ref, at, buffers[index], unit, offset, narrow)


def edges_kernel(levels, couplings, buffers, carried, halved, tables_ref, rates_ref, *refs):
    refs = list(refs)[1:]
    wall_ref = refs.pop(0)
    in_refs = [refs.pop(0) for _ in range(buffers)]
    other_refs = [refs.pop(0) for _ in range(2)] if carried else []
    work_ref, edge_ref, low_ref, high_ref = refs
    apply(work_ref, couplings, tables_ref, in_refs)

    def load(q, row):
        return work_ref[pl.ds(q * PITCH + row, 8), :]

    rate = pair_rate(rates_ref, *levels)
    collide_edges(load, wall_ref, rate, edge_ref, low_ref, high_ref, halved)
    for source, target in zip(other_refs, (low_ref, high_ref)):
        target[pl.ds(4 * BLOCKS, 4 * BLOCKS), :] = source[...]


def inside_kernel(levels, keep, extra, couplings, buffers, tables_ref, rates_ref, *refs):
    refs = list(refs)
    work_ref, wall_ref, edge_ref = refs.pop(0), refs.pop(0), refs.pop(0)
    old_ref = work_ref if keep else None
    other_ref = refs.pop(0) if extra and not extra[0] else None
    in_refs = [refs.pop(0) for _ in range(buffers)]
    inside_ref = refs.pop()
    read_ref = refs.pop(0)
    next_ref = refs.pop(0) if couplings else None

    def load(q, row):
        return work_ref[pl.ds(q * PITCH + row, 8), :]

    collide_inside(load, wall_ref, pair_rate(rates_ref, *levels), inside_ref)
    stream_known(edge_ref, inside_ref, read_ref, PITCH, old_ref, next_ref)
    apply(next_ref, couplings, tables_ref, in_refs)
    if extra:
        own, half, at = extra
        source = old_ref if own else other_ref
        pick_rows(source, half, tables_ref, at, refs.pop(0), 2 * UNIT, UNIT)


def joined_kernel(first, second, ins, outs, *refs):
    refs = list(refs)
    scalars = [[refs.pop(0), refs.pop(0)] for _ in range(2)]
    inputs = [[refs.pop(0) for _ in range(count)] for count in ins]
    outputs = [[refs.pop(0) for _ in range(count)] for count in outs]
    for i, kernel in enumerate((first, second)):
        kernel(*scalars[i], *inputs[i], *outputs[i], refs[i])


def rest_kernel(keep, picks, unit, carried, ahead, inputs, tables_ref, front_ref, behind_ref, *refs):
    taken_ref = refs[0] if ahead else None
    refs = list(refs)[inputs:]
    seen_ref, rows_ref = refs.pop(0), refs.pop(0)
    next_ref = refs.pop(0) if ahead else None
    other_ref = refs.pop(0) if carried else None
    stream_rest(
        front_ref, behind_ref, seen_ref, PITCH, keep, 0, next_ref, taken_ref, halved=keep
    )
    if carried:
        stream_rest(front_ref, behind_ref, other_ref, PITCH, True, 4 * BLOCKS, halved=True)
    for other, half, at, offset, narrow in picks:
        source = other_ref if other else seen_ref
        pick_rows(source, half, tables_ref, at, rows_ref, unit, offset, narrow)


def pack_level(work_ref, half, out_ref):
    def one(q, carry):
        chunk = lanes_of((8, DEPTH)) // OWN
        for row in range(0, WIDTH, 8):
            packed = None
            for plane in range(PLANES):
                at = pl.multiple_of(q * PITCH + plane * WIDTH + row, 8)
                value = turn(work_ref[pl.ds(at, 8), :], OWN * plane - HALF * half - GHOST, 1)
                packed = value if packed is None else jnp.where(chunk == plane, value, packed)
            out_ref[pl.ds(pl.multiple_of(q * WIDTH + row, 8), 8), :] = packed
        return carry

    lax.fori_loop(0, Q, one, 0, unroll=9)


def pack_levels(tables_ref, work_ref, levels, out_refs):
    for me in range(LEVELS):

        @pl.when(tables_ref[ME] == me)
        def _():
            for half, level in levels:
                pack_level(work_ref, half, out_refs[(level - me) % LEVELS])


def other_early_kernel(couplings, tables_ref, rates_ref, state_ref, b2, b5, out_ref, work_ref):
    copy_state(state_ref, out_ref)
    apply(out_ref, couplings, tables_ref, (b2, b5))


def other_last_kernel(couplings, tables_ref, rates_ref, state_ref, b6, *refs):
    out_refs, work_ref = refs[:-1], refs[-1]
    copy_state(state_ref, work_ref)
    apply(work_ref, couplings, tables_ref, (b6,))
    pack_levels(tables_ref, work_ref, ((1, 0), (0, 1)), out_refs)


def last_kernel(couplings, tables_ref, rates_ref, state_ref, b7, *refs):
    out_refs, work_ref = refs[LEVELS:-1], refs[-1]
    apply(work_ref, couplings, tables_ref, (b7,))
    pack_levels(tables_ref, work_ref, ((1, 2), (0, 3)), out_refs)


def output_kernel(tables_ref, *refs):
    in_refs, out_ref = refs[:-1], refs[-1]
    chunk = lanes_of((WIDTH, DEPTH)) // OWN
    for me in range(LEVELS):

        @pl.when(tables_ref[ME] == me)
        def _():
            def one(q, carry):
                parts = [
                    in_refs[(me - c) % LEVELS][pl.ds(pl.multiple_of(q * WIDTH, 8), WIDTH), :]
                    for c in range(LEVELS)
                ]
                for plane in range(PLANES):
                    whole = None
                    for c in range(LEVELS):
                        value = turn(parts[c], OWN * (c - plane), 1)
                        whole = value if whole is None else jnp.where(chunk == c, value, whole)
                    out_ref[pl.ds(pl.multiple_of(q * ROWS + plane * WIDTH, 8), WIDTH), :] = whole
                return carry

            lax.fori_loop(0, Q, one, 0, unroll=3)


def trade_planes(low, high):
    count = lax.axis_size("gx")
    forward = [(i, (i + 1) % count) for i in range(count)]
    backward = [(target, source) for source, target in forward]
    behind = lax.ppermute(high, "gx", forward)
    return lax.ppermute(low, "gx", backward), behind


def trade_rows(rows):
    blocks = rows.reshape(PEERS, -1, DEPTH)
    return lax.all_to_all(blocks, "gx", split_axis=0, concat_axis=0, tiled=True).reshape(
        rows.shape
    )


def on_device(populations, solid_mask, relax_rates, down_send, down_recv, up_send, up_recv):
    meta = jnp.concatenate(
        [value.reshape(-1) for value in (down_send, down_recv, up_send, up_recv)]
    ).astype(jnp.float32)
    meta = jnp.concatenate([meta, jnp.broadcast_to(relax_rates, (META * DEPTH - meta.size,))])
    meta = meta.reshape(META, DEPTH)
    x = jnp.transpose(populations.reshape(ROWS, Q, DEPTH), (1, 0, 2)).reshape(Q * ROWS, DEPTH)
    wall = solid_mask.reshape(ROWS, DEPTH)
    flow = [(Q * ROWS, DEPTH), (9 * WIDTH, DEPTH), (9 * WIDTH, DEPTH)]
    state = (STATE, DEPTH)

    edge, low, high = call(
        first_edges_kernel, [(Q * HALF, DEPTH), *flow[1:]], (relax_rates, x, wall), smem=1
    )
    front, behind = trade_planes(low, high)
    (seen,) = call(
        first_inside_kernel,
        [((Q + 1) * ROWS, DEPTH)],
        (relax_rates, x, wall, edge),
        smem=1,
        scratch=[(Q * HALF, DEPTH)],
    )
    windows, _ = call(
        windows_kernel,
        [(LEVELS * WINDOW, DEPTH), ((Q + 1) * ROWS, DEPTH)],
        (seen, front, behind, meta),
        aliases={0: 1},
    )
    windows = lax.all_to_all(
        windows.reshape(LEVELS, WINDOW, DEPTH), "lvl", 0, 0, tiled=True
    )
    tables = windows[:, WINDOW - META : WINDOW - META + 3, :].astype(jnp.int32).reshape(-1)
    rates = windows[:, WINDOW - 1, 0]
    windows = windows.reshape(-1, DEPTH)
    s, wall_s, rows = call(
        unpack_kernel,
        [state, (ROWS, DEPTH), (PEERS * UNIT, DEPTH)],
        (tables, rates, windows),
        smem=2,
    )
    got = {0: trade_rows(rows)}

    def taken(step, offset, half, level, which, narrow=False):
        buffer = got[step]
        return buffer, half, table_at(level, which), buffer.shape[0] // PEERS, offset, narrow

    def gather_takes(takes):
        buffers, couplings = [], []
        for buffer, half, at, unit, offset, narrow in takes:
            index = next((i for i, b in enumerate(buffers) if b is buffer), len(buffers))
            if index == len(buffers):
                buffers.append(buffer)
            couplings.append((half, at, index, unit, offset, narrow))
        return buffers, couplings

    def edges(value, walls, levels, takes, halved, carried=()):
        buffers, couplings = gather_takes(takes)
        planes = (8 * BLOCKS // (1 if carried or not halved else 2), DEPTH)
        return call(
            functools.partial(
                edges_kernel, levels, couplings, len(buffers), bool(carried), halved
            ),
            [state, (Q * HALF, DEPTH), planes, planes],
            (tables, rates, value, walls, *buffers, *carried),
            smem=2,
            aliases={2: 0},
        )

    def inside(work, walls, edge, levels, keep, extra=None, other=None, takes=(), join=None):
        buffers, couplings = gather_takes(takes)
        ins = [work, walls, edge]
        ins += [other] if extra and not extra[0] else []
        ins += buffers
        kernel = functools.partial(
            inside_kernel, levels, keep, extra, couplings, len(buffers)
        )
        outs = [state] * (2 if takes else 1) + ([(PEERS * 2 * UNIT, DEPTH)] if extra else [])
        scratch = [(Q * HALF, DEPTH)]
        if join is None:
            return call(kernel, outs, (tables, rates, *ins), smem=2, scratch=scratch)
        second, more_ins, more_outs = join
        return call(
            functools.partial(
                joined_kernel, kernel, second, (len(ins), len(more_ins)), (len(outs), len(more_outs))
            ),
            outs + more_outs,
            (tables, rates, tables, rates, *ins, *more_ins),
            smem=4,
            scratch=scratch + [state],
        )

    down_23 = (False, 1, table_at(2, DOWN_SEND), 0, False)
    up_32 = (False, 0, table_at(3, UP_SEND), 0, False)
    extras = {
        1: (False, 0, table_at(1, DOWN_SEND)),
        2: (False, 1, table_at(0, DOWN_SEND)),
        3: (True, 1, table_at(2, UP_SEND)),
    }
    picks = {
        1: [up_32],
        2: [down_23],
        3: [up_32],
        4: [down_23],
        5: [
            up_32,
            (True, 0, table_at(1, DOWN_SEND), UNIT, False),
            (True, 0, table_at(1, UP_SEND), 2 * UNIT, True),
        ],
        6: [down_23, (False, 1, table_at(2, UP_SEND), UNIT, True)],
        7: [(False, 0, table_at(3, UP_SEND), 0, True)],
    }
    units = {1: 48, 2: 48, 3: 48, 4: 24, 5: 64, 6: 40, 7: 16}
    for step in range(1, 8):
        odd = step % 2 == 1
        if odd:
            takes = [taken(step - 1, 0, 0, 3, DOWN_RECV)]
        else:
            takes = [taken(step - 1, 0, 1, 2, UP_RECV)]
            if step == 6:
                takes.append(taken(5, UNIT, 1, 2, DOWN_RECV))
            elif step == 2:
                takes.append(taken(1, UNIT, 1, 2, DOWN_RECV))
        carried = step == 5
        work, edge, low, high = edges(
            s, wall_s, (3, 2), takes, odd, (t_low, t_high) if carried else ()
        )
        front, behind = trade_planes(low, high)
        if step == 1:
            t, wall_t, coupled = call(
                unpack_other_kernel,
                [state, (ROWS, DEPTH), (PITCH, DEPTH)],
                (tables, rates, windows, low),
                smem=2,
            )
        extra = extras.get(step)
        ahead = []
        if odd:
            ahead.append(taken(step - 1, 0, 0, 3, DOWN_RECV))
            if step in (3, 7):
                ahead.append(taken(1 if step == 3 else 5, UNIT, 1, 2, DOWN_RECV))
        join = None
        if step == 6:
            couplings = [
                (0, table_at(1, DOWN_RECV), 0, units[2], UNIT, False),
                (1, table_at(0, UP_RECV), 1, units[5], 2 * UNIT, True),
            ]
            early = functools.partial(other_early_kernel, couplings)
            join = (early, (t, got[2], got[5]), [state])
        if step == 7:
            couplings = [(0, table_at(1, UP_RECV), 0, units[6], UNIT, True)]
            late = functools.partial(other_last_kernel, couplings)
            join = (late, (t, got[6]), [(Q * WIDTH, DEPTH)] * LEVELS)
        seen, *rows = inside(work, wall_s, edge, (3, 2), odd, extra, t, ahead, join)
        following = [rows.pop(0)] if ahead else []
        if step == 6:
            t = rows.pop()
        if step == 7:
            packed, rows = rows, []
        if step == 4:
            takes = [taken(2, UNIT, 0, 1, DOWN_RECV), taken(3, UNIT, 0, 1, UP_RECV)]
            t_work, t_edge, t_low, t_high = edges(t, wall_t, (1, 0), takes, True)
            seen, t_work, t_edge, t_low, t_high = lax.optimization_barrier(
                (seen, t_work, t_edge, t_low, t_high)
            )
        if step == 5:
            (t,) = inside(t_work, wall_t, t_edge, (1, 0), True)
        unit = units[step]
        ins = [tables, front, behind] + ([coupled] if ahead else [])
        outs, aliases = [], {}
        for value in (seen, *rows, *following, *([t] if carried else [])):
            if value is seen or rows:
                slot = len(outs)
            else:
                slot = len(outs) + 1 if len(outs) == 1 else len(outs)
            if slot == 2 and len(outs) == 1:
                outs.append((PEERS * unit, DEPTH))
            aliases[len(ins)] = slot
            outs.append(value.shape)
            ins.append(value)
        if len(outs) == 1:
            outs.append((PEERS * unit, DEPTH))
        s, got[step], *others = call(
            functools.partial(
                rest_kernel, odd, picks[step], unit, carried, bool(ahead), len(ins) - 3
            ),
            outs,
            ins,
            smem=1,
            aliases=aliases,
        )
        if ahead:
            s = others.pop(0)
        if carried:
            (t,) = others
        got[step] = trade_rows(got[step])

    couplings = [(1, table_at(2, UP_RECV), 0, units[7], 0, True)]
    packed = call(
        functools.partial(last_kernel, couplings),
        [(Q * WIDTH, DEPTH)] * LEVELS + [state],
        (tables, rates, s, got[7], *packed),
        smem=2,
        aliases={2: LEVELS, **{4 + i: i for i in range(LEVELS)}},
    )
    parts = [packed[0]] + [
        lax.ppermute(packed[by], "lvl", [(i, (i + by) % LEVELS) for i in range(LEVELS)])
        for by in range(1, LEVELS)
    ]
    (final,) = call(output_kernel, [(Q * ROWS, DEPTH)], (tables, *parts), smem=1)
    final = jnp.transpose(final.reshape(Q, ROWS, DEPTH), (1, 0, 2))
    return final.reshape(1, PLANES, WIDTH, Q, DEPTH)


def solution(mesh):
    return jax.shard_map(
        on_device,
        mesh=mesh,
        in_specs=(
            P("lvl", "gx", None, None, None),
            P("lvl", "gx", None, None),
            P("lvl"),
            P("lvl", "gx", None, None),
            P("lvl", "gx", None, None),
            P("lvl", "gx", None, None),
            P("lvl", "gx", None, None),
        ),
        out_specs=P("lvl", "gx", None, None, None),
        check_vma=False,
    )
```
